32 devices in a mesh: group: 2 (over x), date: 16 (over z, y, core).
Axes of the slice: x: 2, y: 2, z: 4, core: 2. Of those that a mesh axis runs over, the one named last changes fastest.
Arguments:
- slc_stack: bfloat16 [16, 2, 32, 16384], P('date', None, 'group'), parts along dimension 2, may hold values from -30 to 30
- band_taps: bfloat16 [2, 2, 32], replicated, may hold values from -1 to 1
- pair_flags: int32 [16, 4], P('date'), may hold values from 0 to 1, as said below
Outputs:
- iono_phase: float32 [16, 8, 1024], P('date', 'group'), parts along dimension 1
- weight_sum: float32 [16, 8, 1024], P('date', 'group'), parts along dimension 1
The draws below stay inside these ranges and needn't reach their ends.
There are 2 independent parts, one for each index of `group`. The reference program is written for one: setup_inputs(seed, part) draws one part's arguments, and reference() takes and returns one part's arrays. A program takes and returns all parts, laid end to end along the dimension named above; an argument that names none is the same for every part. Nothing has to cross between parts.
Inputs may be any that keep to these rules, and one draw needn't show every extreme that they name: pair_flags[d,0] is 1 for every date but the last; pair_flags[d,k] is 0 where d + k + 1 >= 16.
All inputs are finite; a program needn't handle non-finite values.
Results may differ from the reference program's by a relative error of at most 0.002.
Values may be sent and summed in bfloat16 or wider, within the bound.
No kernel may reach another device: no remote copies, remote signals or barrier semaphores. Data moves between devices by JAX's collectives and lax.ppermute only.
A program may use at most 128 MiB of HBM per device.

```python
import jax
import jax.numpy as jnp
from jax import lax

ROWS = 16
RANGE = 16384
TAPS = 32
ML_AZ = 4
ML_RG = 16
SPAN = 4
RADIUS = 8
ITERS = 4
DATES = 16
AZ_L = 4
RG_L = 1024


def draw_slc_stack(key, part):
    keys = jax.random.split(jax.random.fold_in(key, 17), 5)
    scenery = jax.random.normal(keys[0], (2, ROWS, RANGE), jnp.float32)
    slopes = jax.random.uniform(keys[1], (DATES, 1, 1), jnp.float32, -3.0, 3.0)
    columns = jnp.arange(RANGE, dtype=jnp.float32)[None, None, :] * (25.0 / RANGE)
    rough = 0.4 * jax.random.normal(keys[2], (DATES, ROWS, RANGE), jnp.float32)
    angles = slopes * columns + rough
    real_part = scenery[0][None] * jnp.cos(angles) - scenery[1][None] * jnp.sin(angles)
    imag_part = scenery[0][None] * jnp.sin(angles) + scenery[1][None] * jnp.cos(angles)
    noise = 0.5 * jax.random.normal(keys[4], (DATES, 2, ROWS, RANGE), jnp.float32)
    result = jnp.stack([real_part, imag_part], axis=1) + noise
    return jnp.clip(result, -30.0, 30.0).astype(jnp.bfloat16)


def draw_pair_flags(key, part):
    flags = jax.random.randint(jax.random.fold_in(key, 29), (DATES, SPAN), 0, 2, jnp.int32)
    column = lax.broadcasted_iota(jnp.int32, (DATES, SPAN), 1)
    date_ids = lax.broadcasted_iota(jnp.int32, (DATES, SPAN), 0)
    flags = jnp.where(column == 0, 1, flags)
    present = (date_ids + column + 1 < DATES).astype(jnp.int32)
    return (flags * present).astype(jnp.int32)


def scatter_about(key, shape, scale, bound, held_as=jnp.bfloat16):
    drawn = scale * jax.random.normal(key, shape, jnp.float32)
    return jnp.clip(drawn, min=-bound, max=bound).astype(held_as)


def setup_inputs(seed: int = 0, part: int = 0) -> dict:
    seeds = jax.random.split(jax.random.key(seed), 4)
    part_splits = jax.random.split(jax.random.fold_in(seeds[3], part), 4)
    return {
        "slc_stack": draw_slc_stack(jax.random.fold_in(jax.random.fold_in(seeds[3], part), 71), part),
        "band_taps": scatter_about(seeds[1], (2, 2, TAPS), TAPS ** -0.5, 1.0),
        "pair_flags": draw_pair_flags(jax.random.fold_in(seeds[3], 71), part),
    }


eps_power = 1e-06
floor_weight = 0.1
ridge_weight = 0.05
split_coef = 2.0

def band_split(one_scene, band_taps):
    signal = one_scene.astype(jnp.float32)
    left_pad = TAPS // 2
    padded = jnp.pad(signal, ((0, 0), (0, 0), (left_pad, TAPS - 1 - left_pad)))
    coeffs = band_taps.astype(jnp.float32)
    result = jnp.zeros((2, 2, ROWS, RANGE), jnp.float32)
    for offset in range(TAPS):
        window = padded[:, :, offset:offset + RANGE]
        real_tap = coeffs[:, 0, offset][:, None, None]
        imag_tap = coeffs[:, 1, offset][:, None, None]
        real_part = real_tap * window[0] - imag_tap * window[1]
        imag_part = imag_tap * window[0] + real_tap * window[1]
        result = result + jnp.stack([real_part, imag_part], axis=1)
    return result.astype(jnp.bfloat16)

def multilook(values):
    shaped = values.reshape(values.shape[:-2] + (AZ_L, ML_AZ, RG_L, ML_RG))
    return shaped.sum(axis=(-3, -1))

def later_of(values, offset):
    return jnp.concatenate([values[offset:], jnp.zeros_like(values[:offset])], axis=0)

def earlier_of(values, offset):
    return jnp.concatenate([jnp.zeros_like(values[:offset]), values[:-offset]], axis=0)

def reference(slc_stack, band_taps, pair_flags):
    bands = lax.map(lambda one_scene: band_split(one_scene, band_taps), slc_stack)

    def power_of(piece):
        values = piece.astype(jnp.float32)
        return multilook(values[:, 0] * values[:, 0] + values[:, 1] * values[:, 1])
    powers = lax.map(power_of, bands)
    date_ids = jnp.arange(DATES, dtype=jnp.int32)

    def pair_of(date_index):
        own_bands = lax.dynamic_index_in_dim(bands, date_index, 0, keepdims=False).astype(jnp.float32)
        real_list = []
        imag_list = []
        for offset in range(1, SPAN + 1):
            other_index = jnp.minimum(date_index + offset, DATES - 1).astype(jnp.int32)
            present = (date_index + offset < DATES).astype(jnp.float32)
            partner = lax.dynamic_index_in_dim(bands, other_index, 0, keepdims=False).astype(jnp.float32) * present
            real_part = own_bands[:, 0] * partner[:, 0] + own_bands[:, 1] * partner[:, 1]
            imag_part = own_bands[:, 1] * partner[:, 0] - own_bands[:, 0] * partner[:, 1]
            real_list.append(multilook(real_part))
            imag_list.append(multilook(imag_part))
        return (jnp.stack(real_list, axis=0), jnp.stack(imag_list, axis=0))
    cross_real, cross_imag = lax.map(pair_of, date_ids)
    partner_power = jnp.stack([later_of(powers, offset) for offset in range(1, SPAN + 1)], axis=1)
    own_power = powers[:, None]
    coherence = (cross_real ** 2 + cross_imag ** 2) / (own_power * partner_power + eps_power)
    flags = pair_flags.astype(jnp.float32)[:, :, None, None]
    weight = flags * 0.5 * (coherence[:, :, 0] + coherence[:, :, 1])
    normalizer = jnp.sqrt((own_power[:, :, 0] * partner_power[:, :, 0] + eps_power) * (own_power[:, :, 1] * partner_power[:, :, 1] + eps_power))
    cross_term = cross_imag[:, :, 0] * cross_real[:, :, 1] - cross_real[:, :, 0] * cross_imag[:, :, 1]
    raw_phase = split_coef * cross_term / normalizer
    row_ids = lax.broadcasted_iota(jnp.int32, (RG_L, RG_L), 0)
    col_ids = lax.broadcasted_iota(jnp.int32, (RG_L, RG_L), 1)
    box_matrix = (jnp.abs(row_ids - col_ids) <= RADIUS).astype(jnp.float32)
    numerator = jnp.matmul(weight * raw_phase, box_matrix, precision=lax.Precision.HIGHEST)
    denominator = jnp.matmul(weight, box_matrix, precision=lax.Precision.HIGHEST)
    pair_phase = numerator / (denominator + floor_weight)
    smooth_weight = denominator / (2 * RADIUS + 1)
    first_pair = pair_phase[:, 0]
    chain_start = jnp.cumsum(jnp.concatenate([jnp.zeros_like(first_pair[:1]), first_pair[:-1]], axis=0), axis=0)
    low_weight = [earlier_of(smooth_weight[:, offset - 1], offset) for offset in range(1, SPAN + 1)]
    low_phase = [earlier_of(pair_phase[:, offset - 1], offset) for offset in range(1, SPAN + 1)]
    weight_sum = jnp.zeros_like(chain_start)
    for offset in range(1, SPAN + 1):
        weight_sum = weight_sum + smooth_weight[:, offset - 1] + low_weight[offset - 1]
    diagonal = weight_sum + ridge_weight
    iono_phase = chain_start
    for sweep_index in range(ITERS):
        accumulated = ridge_weight * chain_start
        for offset in range(1, SPAN + 1):
            accumulated = accumulated + smooth_weight[:, offset - 1] * (later_of(iono_phase, offset) - pair_phase[:, offset - 1])
            accumulated = accumulated + low_weight[offset - 1] * (earlier_of(iono_phase, offset) + low_phase[offset - 1])
        iono_phase = accumulated / diagonal
    return (iono_phase, weight_sum)
```

```python
import jax
import jax.numpy as jnp
from jax import lax
from jax.experimental import pallas as pl
from jax.experimental.pallas import tpu as pltpu
from jax.sharding import PartitionSpec as P

TAPS = 32
ML_AZ = 4
ML_RG = 16
SPAN = 4
RADIUS = 8
ITERS = 4
LANES = 128
CELLS = LANES // ML_RG

eps_power = 1e-06
floor_weight = 0.1
ridge_weight = 0.05
split_coef = 2.0


def iota(shape, axis):
    return lax.broadcasted_iota(jnp.int32, shape, axis)


def back(x, steps):
    return pltpu.roll(x, LANES - steps, 1)


def group_sums(x0, x1, x2, x3):
    lane = iota((8, LANES), 1)
    even = lane % 2 == 0
    low = lane % 4 < 2
    u = jnp.where(even, x0 + back(x0, 1), x1 + pltpu.roll(x1, 1, 1))
    v = jnp.where(even, x2 + back(x2, 1), x3 + pltpu.roll(x3, 1, 1))
    return jnp.where(low, u + back(u, 2), v + pltpu.roll(v, 2, 1))


def pick4(x0, x1, x2, x3):
    lane = iota((8, LANES), 1) % 4
    return jnp.where(lane < 2, jnp.where(lane == 0, x0, x1), jnp.where(lane == 2, x2, x3))


def fill_filter(taps_ref, m_ref):
    width = 2 * LANES
    sub = iota((CELLS, width), 0)

    def placed(row):
        taps = jnp.broadcast_to(taps_ref[row : row + 1, :], (CELLS, width))
        result = jnp.zeros((CELLS, width), jnp.float32)
        for c in range(CELLS):
            result = jnp.where(sub == c, pltpu.roll(taps, (ML_RG * c - TAPS // 2) % width, 1), result)
        return result

    def along(base, j):
        both = [base if jj == 0 else pltpu.roll(base, jj, 1) for jj in (j, j + 1)]
        return jnp.concatenate(both, axis=0)

    for band in range(2):
        real, imag = placed(2 * band), placed(2 * band + 1)
        for j in range(0, ML_RG, 2):
            tr, ti = along(real, j), along(imag, j)
            real_row = ((band * 2 + 0) * ML_RG + j) * CELLS
            imag_row = ((band * 2 + 1) * ML_RG + j) * CELLS
            m_ref[real_row : real_row + 16, :width] = tr.astype(jnp.bfloat16)
            m_ref[real_row : real_row + 16, width:] = (-ti).astype(jnp.bfloat16)
            m_ref[imag_row : imag_row + 16, :width] = ti.astype(jnp.bfloat16)
            m_ref[imag_row : imag_row + 16, width:] = tr.astype(jnp.bfloat16)


def row_of(band, part, j):
    start = ((band * 2 + part) * ML_RG + j) * CELLS
    return slice(start, start + CELLS)


def apply_filter(matrix, windows):
    bands = lax.dot_general(
        matrix, windows, (((1,), (1,)), ((), ())), preferred_element_type=jnp.float32
    )
    return bands.astype(jnp.bfloat16).astype(jnp.float32)


def power_of(b_ref, d, band):
    total = jnp.zeros((CELLS, LANES), jnp.float32)
    for j in range(ML_RG):
        r = b_ref[d, row_of(band, 0, j)]
        i = b_ref[d, row_of(band, 1, j)]
        total = total + (r * r + i * i)
    return group_sums(total, total, total, total)


def weigh(cross, own, partner, flags):
    (re0, im0), (re1, im1) = cross
    pow0 = own[0] * partner[0] + eps_power
    pow1 = own[1] * partner[1] + eps_power
    coherence = (re0 * re0 + im0 * im0) / pow0 + (re1 * re1 + im1 * im1) / pow1
    weight = flags * 0.5 * coherence
    raw = split_coef * (im0 * re1 - re0 * im1) / jnp.sqrt(pow0 * pow1)
    return weight, weight * raw


def cell_sums(x):
    sub = iota((CELLS, LANES), 0)
    upto = x
    for step in (1, 2, 4):
        upto = upto + jnp.where(sub >= step, pltpu.roll(upto, step, 0), 0.0)
    total = jnp.broadcast_to(upto[CELLS - 1 : CELLS], (CELLS, LANES))
    return upto, total - upto + x, total


def solve_kernel(
    taps_ref, y_ref, out_ref, m_ref, b_ref, wh_ref, hb_ref, pw_ref, fl_ref, fh_ref, q_ref, s_ref, bt_ref, x_ref
):
    n, _, rows, _ = y_ref.shape
    lanes = rows - 4 * ML_AZ
    halos = hb_ref.shape[0]
    lane = iota((8, LANES), 1)
    sub = iota((8, LANES), 0)
    zero = jnp.zeros((8, LANES), jnp.float32)
    fill_filter(taps_ref, m_ref)

    def filtered(d, carry):
        windows, edges = [], []
        for part in range(2):
            v = y_ref[d, part].astype(jnp.float32).reshape(rows // 8, 8, LANES)
            subs = iota((rows // 8 - 1, 8, LANES), 1)
            merged = pltpu.roll(jnp.where(subs < 4, v[1:], v[:-1]), 4, 1)
            wide = iota((rows // 8 - 2, 8, LANES), 2)
            edge = jnp.where(wide < LANES // 2, merged[1:], merged[:-1])
            windows.append(v[1:-1].reshape(lanes, LANES))
            windows.append(edge.reshape(lanes, LANES))
            first, second, before, final = v[0], v[1], v[rows // 8 - 2], v[rows // 8 - 1]
            later = pltpu.roll(jnp.where(sub < 4, second, final), 4, 0)
            sooner = pltpu.roll(jnp.where(sub < 4, first, before), 4, 0)
            edges.append(jnp.where(sub < 4, final, first))
            edges.append(jnp.where(lane < LANES // 2, later, sooner))
            if part == 0:
                main = final[4:5]
                main = jnp.where(lane[:1] < LANES // 2, pltpu.roll(main, LANES // 2, 1), main)
                fl_ref[d] = jnp.broadcast_to(main, (8, LANES))
                side = first[0:1]
                side = jnp.where(lane[:1] < LANES // 2, side, pltpu.roll(side, LANES // 2, 1))
                fh_ref[d // 16] = jnp.where(lane // 8 == d % 16, jnp.broadcast_to(side, (8, LANES)), fh_ref[d // 16])
        windows = jnp.concatenate(windows, axis=1)
        if lanes < LANES:
            windows = jnp.concatenate([windows, jnp.zeros((LANES - lanes, 4 * LANES), jnp.float32)], axis=0)
        wh_ref[d] = jnp.concatenate(edges, axis=1)
        b_ref[d] = apply_filter(m_ref[...], windows.astype(jnp.bfloat16))
        for band in range(2):
            pw_ref[d, band] = power_of(b_ref, d, band)
        return carry

    lax.fori_loop(0, n, filtered, 0)

    for h in range(halos):
        hb_ref[h] = apply_filter(m_ref[...], wh_ref[16 * h : 16 * h + 16].reshape(LANES, 4 * LANES).astype(jnp.bfloat16))

    def pairs(d, carry):
        later = [jnp.minimum(d + k, n - 1) for k in range(1, SPAN + 1)]
        cross, partner = [], []
        for band in range(2):
            real = [zero] * SPAN
            imag = [zero] * SPAN
            for j in range(ML_RG):
                r = b_ref[d, row_of(band, 0, j)]
                i = b_ref[d, row_of(band, 1, j)]
                for k in range(SPAN):
                    pr = b_ref[later[k], row_of(band, 0, j)]
                    pi = b_ref[later[k], row_of(band, 1, j)]
                    real[k] = real[k] + (r * pr + i * pi)
                    imag[k] = imag[k] + (i * pr - r * pi)
            cross.append((group_sums(*real), group_sums(*imag)))
            partner.append(pick4(*[pw_ref[e, band] for e in later]))
        own = [pw_ref[d, band] for band in range(2)]
        weight, weighted = weigh(cross, own, partner, fl_ref[d])
        q_ref[0, d] = weight
        q_ref[1, d] = weighted
        return carry

    lax.fori_loop(0, n, pairs, 0)

    edge_sums = []
    hpow = [[power_of(hb_ref, h, band) for band in range(2)] for h in range(halos)]
    for h in range(halos):
        after = min(h + 1, halos - 1)

        def shifted(value, value_after, k):
            moved = back(value, 8 * k)
            if after == h:
                return moved
            return jnp.where(lane < LANES - 8 * k, moved, back(value_after, 8 * k))

        cross, partner = [], []
        for band in range(2):
            real = [zero] * SPAN
            imag = [zero] * SPAN
            for j in range(ML_RG):
                r = hb_ref[h, row_of(band, 0, j)]
                i = hb_ref[h, row_of(band, 1, j)]
                ra = hb_ref[after, row_of(band, 0, j)]
                ia = hb_ref[after, row_of(band, 1, j)]
                for k in range(SPAN):
                    pr = shifted(r, ra, k + 1)
                    pi = shifted(i, ia, k + 1)
                    real[k] = real[k] + (r * pr + i * pi)
                    imag[k] = imag[k] + (i * pr - r * pi)
            cross.append((group_sums(*real), group_sums(*imag)))
            partner.append(pick4(*[shifted(hpow[h][band], hpow[after][band], k) for k in range(1, SPAN + 1)]))
        weight, weighted = weigh(cross, hpow[h], partner, fh_ref[h])
        for which, value in enumerate((weight, weighted)):
            upto, onward, _ = cell_sums(value)
            wh_ref[h, :, which * 256 : which * 256 + 128] = upto
            wh_ref[h, :, which * 256 + 128 : which * 256 + 256] = onward

    for d in range(SPAN):
        x_ref[0, d] = zero
        x_ref[1, d] = zero
        x_ref[0, n + SPAN + d] = zero
        x_ref[1, n + SPAN + d] = zero
        for k in range(SPAN):
            s_ref[0, d, k] = zero
            s_ref[1, d, k] = zero

    def smooth(d, chain):
        h, place = d // 16, 8 * (d % 16)
        boxes = []
        for which in range(2):
            upto, onward, total = cell_sums(q_ref[which, d])
            far_upto = pltpu.roll(wh_ref[h, :, which * 256 : which * 256 + 128], (lanes - 4 - place) % LANES, 1)
            far_onward = pltpu.roll(wh_ref[h, :, which * 256 + 128 : which * 256 + 256], (LANES - 4 - place) % LANES, 1)
            sooner = jnp.where(lane < 4, far_onward, pltpu.roll(onward, 4, 1))
            later = jnp.where(lane >= lanes - 4, far_upto, back(upto, 4))
            boxes.append(total + sooner + later)
        phase = boxes[1] / (boxes[0] + floor_weight)
        weight = boxes[0] * (1.0 / (2 * RADIUS + 1))
        product = weight * phase
        total_weight = zero
        pull = ridge_weight * chain
        for k in range(SPAN):
            s = weight if k == 0 else back(weight, k)
            g = product if k == 0 else back(product, k)
            s_ref[0, d + SPAN, k] = s
            s_ref[1, d + SPAN, k] = g
            total_weight = total_weight + s + s_ref[0, d + SPAN - 1 - k, k]
            pull = pull - g + s_ref[1, d + SPAN - 1 - k, k]
        x_ref[0, d + SPAN] = chain
        bt_ref[0, d] = pull
        bt_ref[1, d] = 1.0 / (total_weight + ridge_weight)
        out_ref[d] = pltpu.roll(total_weight, 1, 1)
        return chain + phase

    lax.fori_loop(0, n, smooth, zero)

    for sweep in range(ITERS):
        old, new = sweep % 2, (sweep + 1) % 2

        def relax(d, carry):
            total = bt_ref[0, d]
            for k in range(SPAN):
                total = total + s_ref[0, d + SPAN, k] * x_ref[old, d + SPAN + 1 + k]
                total = total + s_ref[0, d + SPAN - 1 - k, k] * x_ref[old, d + SPAN - 1 - k]
            value = total * bt_ref[1, d]
            x_ref[new, d + SPAN] = value
            if sweep == ITERS - 1:
                out_ref[d] = jnp.where(lane % 4 == 1, out_ref[d], value)
            return carry

        lax.fori_loop(0, n, relax, 0)


def spread(scene, flags, looks, parts):
    width = scene.shape[2] // parts
    margin = 2 * LANES
    padded = jnp.pad(scene, ((0, 0), (0, 0), (margin, margin)))
    cut = jnp.stack([padded[:, :, width * q : width * (q + 1) + 2 * margin] for q in range(parts)])
    blocks = width // LANES + 4
    cut = cut.reshape(parts, 2, looks, ML_AZ, blocks, LANES).transpose(0, 2, 1, 4, 3, 5)
    shape = cut.shape
    q, block, place = iota(shape, 0), iota(shape, 3), iota(shape, 5)
    pattern = jnp.tile(flags.astype(cut.dtype), LANES // SPAN)
    inside = jnp.where(place // SPAN % 2 == 0, q < parts - 1, q > 0)
    cut = jnp.where((block == blocks - 1) & (place >= LANES // 2), pattern, cut)
    halo_pattern = jnp.where(inside, pattern, jnp.zeros_like(pattern))
    cut = jnp.where((block == 0) & (place < LANES // 2), halo_pattern, cut)
    return cut.reshape(parts * looks, 2, blocks * ML_AZ, LANES)


def local(slc_stack, band_taps, pair_flags):
    n = lax.axis_size("date")
    looks = slc_stack.shape[2] // ML_AZ
    parts = n // looks
    chunks = spread(slc_stack[0], pair_flags[0], looks, parts)
    rows = chunks.shape[2]
    lanes = rows - 4 * ML_AZ
    taps = jnp.pad(band_taps.astype(jnp.float32).reshape(4, TAPS), ((0, 0), (0, 2 * LANES - TAPS)))
    y = lax.all_to_all(chunks, "date", 0, 0, tiled=True)
    halos = n * 8 // LANES
    tile = (8, LANES)
    solved = pl.pallas_call(
        solve_kernel,
        out_shape=jax.ShapeDtypeStruct((n, *tile), jnp.float32),
        in_specs=[pl.BlockSpec(memory_space=pltpu.VMEM)] * 2,
        out_specs=pl.BlockSpec(memory_space=pltpu.VMEM),
        scratch_shapes=[
            pltpu.VMEM((4 * LANES, 4 * LANES), jnp.bfloat16),
            pltpu.VMEM((n, 4 * LANES, LANES), jnp.float32),
            pltpu.VMEM((n, 8, 4 * LANES), jnp.float32),
            pltpu.VMEM((halos, 4 * LANES, LANES), jnp.float32),
            pltpu.VMEM((n, 2, *tile), jnp.float32),
            pltpu.VMEM((n, *tile), jnp.float32),
            pltpu.VMEM((halos, *tile), jnp.float32),
            pltpu.VMEM((2, n, *tile), jnp.float32),
            pltpu.VMEM((2, n + SPAN, SPAN, *tile), jnp.float32),
            pltpu.VMEM((2, n, *tile), jnp.float32),
            pltpu.VMEM((2, n + 2 * SPAN, *tile), jnp.float32),
        ],
        compiler_params=pltpu.CompilerParams(vmem_limit_bytes=60 * 1024 * 1024),
    )(taps, y)
    z = lax.all_to_all(solved, "date", 0, 0, tiled=True)
    z = z[:, :, :lanes].reshape(parts, looks, 8, lanes // 4, 4)[..., :2]
    z = z.transpose(4, 1, 0, 3, 2).reshape(2, 1, looks, parts * lanes * 2)
    return (z[0], z[1])


def solution(mesh):
    in_specs = (P("date", None, "group", None), P(), P("date", None))
    out_specs = (P("date", "group", None), P("date", "group", None))
    return jax.shard_map(local, mesh=mesh, in_specs=in_specs, out_specs=out_specs, check_vma=False)
```

```python
import jax
import jax.numpy as jnp
from jax import lax
from jax.experimental import pallas as pl
from jax.experimental.pallas import tpu as pltpu
from jax.sharding import PartitionSpec as P

TAPS = 32
ML_AZ = 4
ML_RG = 16
SPAN = 4
RADIUS = 8
ITERS = 4
LANES = 128
CELLS = LANES // ML_RG

eps_power = 1e-06
floor_weight = 0.1
ridge_weight = 0.05
split_coef = 2.0


def iota(shape, axis):
    return lax.broadcasted_iota(jnp.int32, shape, axis)


def back(x, steps):
    return pltpu.roll(x, LANES - steps, 1)


def group_sums(x0, x1, x2, x3):
    lane = iota((8, LANES), 1)
    even = lane % 2 == 0
    low = lane % 4 < 2
    u = jnp.where(even, x0 + back(x0, 1), x1 + pltpu.roll(x1, 1, 1))
    v = jnp.where(even, x2 + back(x2, 1), x3 + pltpu.roll(x3, 1, 1))
    return jnp.where(low, u + back(u, 2), v + pltpu.roll(v, 2, 1))


def pick4(x0, x1, x2, x3):
    lane = iota((8, LANES), 1) % 4
    return jnp.where(lane < 2, jnp.where(lane == 0, x0, x1), jnp.where(lane == 2, x2, x3))


def filter_kernel(taps_ref, m_ref):
    width = 2 * LANES
    sub = iota((CELLS, width), 0)

    def placed(row):
        taps = jnp.broadcast_to(taps_ref[row : row + 1, :], (CELLS, width))
        result = jnp.zeros((CELLS, width), jnp.float32)
        for c in range(CELLS):
            result = jnp.where(sub == c, pltpu.roll(taps, (ML_RG * c - TAPS // 2) % width, 1), result)
        return result

    def along(base, j):
        both = [base if jj == 0 else pltpu.roll(base, jj, 1) for jj in (j, j + 1)]
        return jnp.concatenate(both, axis=0)

    for band in range(2):
        real, imag = placed(2 * band), placed(2 * band + 1)
        for j in range(0, ML_RG, 2):
            tr, ti = along(real, j), along(imag, j)
            real_row = ((band * 2 + 0) * ML_RG + j) * CELLS
            imag_row = ((band * 2 + 1) * ML_RG + j) * CELLS
            m_ref[real_row : real_row + 16, :width] = tr.astype(jnp.bfloat16)
            m_ref[real_row : real_row + 16, width:] = (-ti).astype(jnp.bfloat16)
            m_ref[imag_row : imag_row + 16, :width] = ti.astype(jnp.bfloat16)
            m_ref[imag_row : imag_row + 16, width:] = tr.astype(jnp.bfloat16)


def row_of(band, part, j):
    start = ((band * 2 + part) * ML_RG + j) * CELLS
    return slice(start, start + CELLS)


def apply_filter(matrix, windows):
    bands = lax.dot_general(
        matrix, windows, (((1,), (1,)), ((), ())), preferred_element_type=jnp.float32
    )
    return bands.astype(jnp.bfloat16).astype(jnp.float32)


def power_of(b_ref, d, band):
    total = jnp.zeros((CELLS, LANES), jnp.float32)
    for j in range(ML_RG):
        r = b_ref[d, row_of(band, 0, j)]
        i = b_ref[d, row_of(band, 1, j)]
        total = total + (r * r + i * i)
    return group_sums(total, total, total, total)


def weigh(cross, own, partner, flags):
    (re0, im0), (re1, im1) = cross
    pow0 = own[0] * partner[0] + eps_power
    pow1 = own[1] * partner[1] + eps_power
    coherence = (re0 * re0 + im0 * im0) / pow0 + (re1 * re1 + im1 * im1) / pow1
    weight = flags * 0.5 * coherence
    raw = split_coef * (im0 * re1 - re0 * im1) / jnp.sqrt(pow0 * pow1)
    return weight, weight * raw


def cell_sums(x):
    sub = iota((CELLS, LANES), 0)
    upto = x
    for step in (1, 2, 4):
        upto = upto + jnp.where(sub >= step, pltpu.roll(upto, step, 0), 0.0)
    total = jnp.broadcast_to(upto[CELLS - 1 : CELLS], (CELLS, LANES))
    return upto, total - upto + x, total


def solve_kernel(
    m_ref, y_ref, out_ref, b_ref, wh_ref, hb_ref, pw_ref, fl_ref, fh_ref, q_ref, s_ref, bt_ref, x_ref
):
    n, _, rows, _ = y_ref.shape
    lanes = rows - 4 * ML_AZ
    halos = hb_ref.shape[0]
    lane = iota((8, LANES), 1)
    sub = iota((8, LANES), 0)
    zero = jnp.zeros((8, LANES), jnp.float32)

    def each(step, start):
        return lax.fori_loop(0, n, step, start, unroll=n <= 16)

    def filtered(d, carry):
        windows, edges = [], []
        for part in range(2):
            v = y_ref[d, part].astype(jnp.float32).reshape(rows // 8, 8, LANES)
            subs = iota((rows // 8 - 1, 8, LANES), 1)
            merged = pltpu.roll(jnp.where(subs < 4, v[1:], v[:-1]), 4, 1)
            wide = iota((rows // 8 - 2, 8, LANES), 2)
            edge = jnp.where(wide < LANES // 2, merged[1:], merged[:-1])
            windows.append(v[1:-1].reshape(lanes, LANES))
            windows.append(edge.reshape(lanes, LANES))
            first, second, before, final = v[0], v[1], v[rows // 8 - 2], v[rows // 8 - 1]
            later = pltpu.roll(jnp.where(sub < 4, second, final), 4, 0)
            sooner = pltpu.roll(jnp.where(sub < 4, first, before), 4, 0)
            edges.append(jnp.where(sub < 4, final, first))
            edges.append(jnp.where(lane < LANES // 2, later, sooner))
            if part == 0:
                main = final[4:5]
                main = jnp.where(lane[:1] < LANES // 2, pltpu.roll(main, LANES // 2, 1), main)
                fl_ref[d] = jnp.broadcast_to(main, (8, LANES))
                side = first[0:1]
                side = jnp.where(lane[:1] < LANES // 2, side, pltpu.roll(side, LANES // 2, 1))
                fh_ref[d // 16] = jnp.where(lane // 8 == d % 16, jnp.broadcast_to(side, (8, LANES)), fh_ref[d // 16])
        windows = jnp.concatenate(windows, axis=1)
        if lanes < LANES:
            windows = jnp.concatenate([windows, jnp.zeros((LANES - lanes, 4 * LANES), jnp.float32)], axis=0)
        wh_ref[d] = jnp.concatenate(edges, axis=1)
        b_ref[d] = apply_filter(m_ref[...], windows.astype(jnp.bfloat16))
        for band in range(2):
            pw_ref[d, band] = power_of(b_ref, d, band)
        return carry

    each(filtered, 0)

    for h in range(halos):
        hb_ref[h] = apply_filter(m_ref[...], wh_ref[16 * h : 16 * h + 16].reshape(LANES, 4 * LANES).astype(jnp.bfloat16))

    def pairs(d, carry):
        later = [jnp.minimum(d + k, n - 1) for k in range(1, SPAN + 1)]
        cross, partner = [], []
        for band in range(2):
            real = [zero] * SPAN
            imag = [zero] * SPAN
            for j in range(ML_RG):
                r = b_ref[d, row_of(band, 0, j)]
                i = b_ref[d, row_of(band, 1, j)]
                for k in range(SPAN):
                    pr = b_ref[later[k], row_of(band, 0, j)]
                    pi = b_ref[later[k], row_of(band, 1, j)]
                    real[k] = real[k] + (r * pr + i * pi)
                    imag[k] = imag[k] + (i * pr - r * pi)
            cross.append((group_sums(*real), group_sums(*imag)))
            partner.append(pick4(*[pw_ref[e, band] for e in later]))
        own = [pw_ref[d, band] for band in range(2)]
        weight, weighted = weigh(cross, own, partner, fl_ref[d])
        q_ref[0, d] = weight
        q_ref[1, d] = weighted
        return carry

    each(pairs, 0)

    edge_sums = []
    hpow = [[power_of(hb_ref, h, band) for band in range(2)] for h in range(halos)]
    for h in range(halos):
        after = min(h + 1, halos - 1)

        def shifted(value, value_after, k):
            moved = back(value, 8 * k)
            if after == h:
                return moved
            return jnp.where(lane < LANES - 8 * k, moved, back(value_after, 8 * k))

        cross, partner = [], []
        for band in range(2):
            real = [zero] * SPAN
            imag = [zero] * SPAN
            for j in range(ML_RG):
                r = hb_ref[h, row_of(band, 0, j)]
                i = hb_ref[h, row_of(band, 1, j)]
                ra = hb_ref[after, row_of(band, 0, j)]
                ia = hb_ref[after, row_of(band, 1, j)]
                for k in range(SPAN):
                    pr = shifted(r, ra, k + 1)
                    pi = shifted(i, ia, k + 1)
                    real[k] = real[k] + (r * pr + i * pi)
                    imag[k] = imag[k] + (i * pr - r * pi)
            cross.append((group_sums(*real), group_sums(*imag)))
            partner.append(pick4(*[shifted(hpow[h][band], hpow[after][band], k) for k in range(1, SPAN + 1)]))
        weight, weighted = weigh(cross, hpow[h], partner, fh_ref[h])
        for which, value in enumerate((weight, weighted)):
            upto, onward, _ = cell_sums(value)
            wh_ref[h, :, which * 256 : which * 256 + 128] = upto
            wh_ref[h, :, which * 256 + 128 : which * 256 + 256] = onward

    for d in range(SPAN):
        x_ref[0, d] = zero
        x_ref[1, d] = zero
        x_ref[0, n + SPAN + d] = zero
        x_ref[1, n + SPAN + d] = zero
        for k in range(SPAN):
            s_ref[0, d, k] = zero
            s_ref[1, d, k] = zero

    def smooth(d, chain):
        h, place = d // 16, 8 * (d % 16)
        boxes = []
        for which in range(2):
            upto, onward, total = cell_sums(q_ref[which, d])
            far_upto = pltpu.roll(wh_ref[h, :, which * 256 : which * 256 + 128], (lanes - 4 - place) % LANES, 1)
            far_onward = pltpu.roll(wh_ref[h, :, which * 256 + 128 : which * 256 + 256], (LANES - 4 - place) % LANES, 1)
            sooner = jnp.where(lane < 4, far_onward, pltpu.roll(onward, 4, 1))
            later = jnp.where(lane >= lanes - 4, far_upto, back(upto, 4))
            boxes.append(total + sooner + later)
        phase = boxes[1] / (boxes[0] + floor_weight)
        weight = boxes[0] * (1.0 / (2 * RADIUS + 1))
        product = weight * phase
        total_weight = zero
        pull = ridge_weight * chain
        for k in range(SPAN):
            s = weight if k == 0 else back(weight, k)
            g = product if k == 0 else back(product, k)
            s_ref[0, d + SPAN, k] = s
            s_ref[1, d + SPAN, k] = g
            total_weight = total_weight + s + s_ref[0, d + SPAN - 1 - k, k]
            pull = pull - g + s_ref[1, d + SPAN - 1 - k, k]
        x_ref[0, d + SPAN] = chain
        bt_ref[0, d] = pull
        bt_ref[1, d] = 1.0 / (total_weight + ridge_weight)
        out_ref[d] = pltpu.roll(total_weight, 1, 1)
        return chain + phase

    each(smooth, zero)

    for sweep in range(ITERS):
        old, new = sweep % 2, (sweep + 1) % 2

        def relax(d, carry):
            total = bt_ref[0, d]
            for k in range(SPAN):
                total = total + s_ref[0, d + SPAN, k] * x_ref[old, d + SPAN + 1 + k]
                total = total + s_ref[0, d + SPAN - 1 - k, k] * x_ref[old, d + SPAN - 1 - k]
            value = total * bt_ref[1, d]
            x_ref[new, d + SPAN] = value
            if sweep == ITERS - 1:
                out_ref[d] = jnp.where(lane % 4 == 1, out_ref[d], value)
            return carry

        each(relax, 0)


def spread_kernel(x_ref, flags_ref, out_ref, held_ref, made_ref, in_sems, out_sems):
    parts = in_sems.shape[1]
    looks = out_ref.shape[0] // parts
    rows = out_ref.shape[2]
    width = x_ref.shape[3] // parts
    pairs = width // (2 * LANES)
    sub = iota((8, LANES), 0)
    lane = iota((8, LANES), 1)
    flags = [flags_ref[0, k].astype(jnp.float32) for k in range(SPAN)]
    pattern = jnp.where(
        lane % 4 < 2, jnp.where(lane % 4 == 0, flags[0], flags[1]), jnp.where(lane % 4 == 2, flags[2], flags[3])
    )
    zero = jnp.zeros((8, LANES), jnp.float32)

    def fetch(part, q):
        columns = pl.ds(q * width, width)
        return pltpu.make_async_copy(x_ref.at[0, part, :, columns], held_ref.at[part, :, columns], in_sems.at[part, q])

    def send(part, q):
        chunks = pl.ds(q * looks, looks)
        return pltpu.make_async_copy(made_ref.at[chunks, part], out_ref.at[chunks, part], out_sems.at[part, q])

    for part in range(2):
        for q in range(parts):
            fetch(part, q).start()
    for part in range(2):
        made = {}

        def pair_of(index, half):
            if index < 0 or index >= parts * pairs:
                return zero, zero
            if (index, half) not in made:
                start = index * 2 * LANES
                first = held_ref[part, :, start : start + LANES].astype(jnp.float32)[8 * half : 8 * half + 8]
                second = held_ref[part, :, start + LANES : start + 2 * LANES].astype(jnp.float32)[8 * half : 8 * half + 8]
                mixed = pltpu.roll(jnp.where(sub < 4, second, first), 4, 0)
                made[index, half] = (jnp.where(sub < 4, first, mixed), jnp.where(sub < 4, mixed, second))
            return made[index, half]

        for q in range(parts):
            if q == 0:
                fetch(part, 0).wait()
            if q + 1 < parts:
                fetch(part, q + 1).wait()
            for tile in range(rows // 16):
                upper = q * pairs - 1 + 2 * tile
                for half in range(looks // 2):
                    for odd in range(2):
                        top = pair_of(upper, half)[odd]
                        bottom = pair_of(upper + 1, half)[odd]
                        if part == 0 and tile == 0:
                            side = lane // SPAN % 2
                            inside = jnp.where(side == 0, float(q < parts - 1), float(q > 0))
                            top = jnp.where((sub < 4) & (lane < LANES // 2), pattern * inside, top)
                        if part == 0 and tile == rows // 16 - 1:
                            bottom = jnp.where((sub >= 4) & (lane >= LANES // 2), pattern, bottom)
                        both = jnp.concatenate([top, bottom], axis=0).astype(jnp.bfloat16)
                        made_ref[q * looks + 2 * half + odd, part, 16 * tile : 16 * tile + 16, :] = both
            send(part, q).start()
    for part in range(2):
        for q in range(parts):
            send(part, q).wait()


def gather_kernel(z_ref, phase_ref, weight_ref):
    count = z_ref.shape[0]
    looks = phase_ref.shape[1]
    width = 2 * LANES
    source = iota((LANES, 2 * width), 0)
    column = iota((LANES, 2 * width), 1)
    block = column % width // CELLS
    chosen = (source == SPAN * block + column // width).astype(jnp.float32)
    values = z_ref[...].reshape(count * CELLS, LANES)
    moved = jnp.dot(values, chosen, precision=lax.Precision.HIGHEST, preferred_element_type=jnp.float32)
    row = iota((count * CELLS, 2 * width), 0)
    column = iota((count * CELLS, 2 * width), 1)
    moved = jnp.where(row % CELLS == column % CELLS, moved, 0.0)
    adder = (iota((count, count * CELLS), 1) // CELLS == iota((count, count * CELLS), 0)).astype(jnp.float32)
    lines = jnp.dot(adder, moved, precision=lax.Precision.HIGHEST, preferred_element_type=jnp.float32)
    for q in range(count // looks):
        for which, out in enumerate((phase_ref, weight_ref)):
            out[0, :, width * q : width * (q + 1)] = lines[
                looks * q : looks * (q + 1), width * which : width * (which + 1)
            ]


def local(slc_stack, band_taps, pair_flags):
    n = lax.axis_size("date")
    looks = slc_stack.shape[2] // ML_AZ
    parts = n // looks
    lanes = slc_stack.shape[3] // (parts * LANES) * ML_AZ
    rows = lanes + 4 * ML_AZ
    halos = n * 8 // LANES
    tile = (8, LANES)
    in_vmem = pl.BlockSpec(memory_space=pltpu.VMEM)
    anywhere = pl.BlockSpec(memory_space=pl.ANY)
    params = pltpu.CompilerParams(vmem_limit_bytes=60 * 1024 * 1024)
    chunks = pl.pallas_call(
        spread_kernel,
        out_shape=jax.ShapeDtypeStruct((n, 2, rows, LANES), jnp.bfloat16),
        in_specs=[anywhere, pl.BlockSpec(memory_space=pltpu.SMEM)],
        out_specs=anywhere,
        scratch_shapes=[
            pltpu.VMEM(slc_stack.shape[1:], jnp.bfloat16),
            pltpu.VMEM((n, 2, rows, LANES), jnp.bfloat16),
            pltpu.SemaphoreType.DMA((2, parts)),
            pltpu.SemaphoreType.DMA((2, parts)),
        ],
        compiler_params=params,
    )(slc_stack, pair_flags)
    y = pltpu.with_memory_space_constraint(lax.all_to_all(chunks, "date", 0, 0, tiled=True), pltpu.VMEM)
    taps = jnp.pad(band_taps.astype(jnp.float32).reshape(4, TAPS), ((0, 0), (0, 2 * LANES - TAPS)))
    matrix = pl.pallas_call(
        filter_kernel,
        out_shape=jax.ShapeDtypeStruct((4 * LANES, 4 * LANES), jnp.bfloat16),
        in_specs=[in_vmem],
        out_specs=in_vmem,
        compiler_params=params,
    )(taps)
    solved = pl.pallas_call(
        solve_kernel,
        out_shape=jax.ShapeDtypeStruct((n, *tile), jnp.float32),
        in_specs=[in_vmem, in_vmem],
        out_specs=in_vmem,
        scratch_shapes=[
            pltpu.VMEM((n, 4 * LANES, LANES), jnp.float32),
            pltpu.VMEM((n, 8, 4 * LANES), jnp.float32),
            pltpu.VMEM((halos, 4 * LANES, LANES), jnp.float32),
            pltpu.VMEM((n, 2, *tile), jnp.float32),
            pltpu.VMEM((n, *tile), jnp.float32),
            pltpu.VMEM((halos, *tile), jnp.float32),
            pltpu.VMEM((2, n, *tile), jnp.float32),
            pltpu.VMEM((2, n + SPAN, SPAN, *tile), jnp.float32),
            pltpu.VMEM((2, n, *tile), jnp.float32),
            pltpu.VMEM((2, n + 2 * SPAN, *tile), jnp.float32),
        ],
        compiler_params=params,
    )(matrix, y)
    z = lax.all_to_all(solved, "date", 0, 0, tiled=True)
    shape = (1, looks, slc_stack.shape[3] // ML_RG)
    if lanes == LANES:
        return tuple(
            pl.pallas_call(
                gather_kernel,
                out_shape=[jax.ShapeDtypeStruct(shape, jnp.float32)] * 2,
                in_specs=[in_vmem],
                out_specs=[in_vmem] * 2,
                compiler_params=params,
            )(z)
        )
    z = z[:, :, :lanes].reshape(parts, looks, CELLS, lanes // SPAN, SPAN)[..., :2]
    z = z.transpose(4, 1, 0, 3, 2).reshape(2, *shape)
    return (z[0], z[1])


def solution(mesh):
    in_specs = (P("date", None, "group", None), P(), P("date", None))
    out_specs = (P("date", "group", None), P("date", "group", None))
    return jax.shard_map(local, mesh=mesh, in_specs=in_specs, out_specs=out_specs, check_vma=False)
```

```python
import jax
import jax.numpy as jnp
from jax import lax
from jax.experimental import pallas as pl
from jax.experimental.pallas import tpu as pltpu
from jax.sharding import PartitionSpec as P

TAPS = 32
ML_AZ = 4
ML_RG = 16
SPAN = 4
RADIUS = 8
ITERS = 4
LANES = 128
CELLS = LANES // ML_RG

eps_power = 1e-06
floor_weight = 0.1
ridge_weight = 0.05
split_coef = 2.0


def iota(shape, axis):
    return lax.broadcasted_iota(jnp.int32, shape, axis)


def back(x, steps):
    return pltpu.roll(x, LANES - steps, 1)


def group_sums(x0, x1, x2, x3):
    lane = iota((8, LANES), 1)
    even = lane % 2 == 0
    low = lane % 4 < 2
    u = jnp.where(even, x0 + back(x0, 1), x1 + pltpu.roll(x1, 1, 1))
    v = jnp.where(even, x2 + back(x2, 1), x3 + pltpu.roll(x3, 1, 1))
    return jnp.where(low, u + back(u, 2), v + pltpu.roll(v, 2, 1))


def pick4(x0, x1, x2, x3):
    lane = iota((8, LANES), 1) % 4
    return jnp.where(lane < 2, jnp.where(lane == 0, x0, x1), jnp.where(lane == 2, x2, x3))


def filter_kernel(taps_ref, m_ref):
    width = 2 * LANES
    sub = iota((CELLS, width), 0)

    def placed(row):
        taps = jnp.broadcast_to(taps_ref[row : row + 1, :], (CELLS, width))
        result = jnp.zeros((CELLS, width), jnp.float32)
        for c in range(CELLS):
            result = jnp.where(sub == c, pltpu.roll(taps, (ML_RG * c - TAPS // 2) % width, 1), result)
        return result

    def along(base, j):
        both = [base if jj == 0 else pltpu.roll(base, jj, 1) for jj in (j, j + 1)]
        return jnp.concatenate(both, axis=0)

    for band in range(2):
        real, imag = placed(2 * band), placed(2 * band + 1)
        for j in range(0, ML_RG, 2):
            tr, ti = along(real, j), along(imag, j)
            real_row = ((band * 2 + 0) * ML_RG + j) * CELLS
            imag_row = ((band * 2 + 1) * ML_RG + j) * CELLS
            m_ref[real_row : real_row + 16, :width] = tr.astype(jnp.bfloat16)
            m_ref[real_row : real_row + 16, width:] = (-ti).astype(jnp.bfloat16)
            m_ref[imag_row : imag_row + 16, :width] = ti.astype(jnp.bfloat16)
            m_ref[imag_row : imag_row + 16, width:] = tr.astype(jnp.bfloat16)


def row_of(band, part, j):
    start = ((band * 2 + part) * ML_RG + j) * CELLS
    return slice(start, start + CELLS)


def apply_filter(matrix, windows):
    bands = lax.dot_general(
        matrix, windows, (((1,), (1,)), ((), ())), preferred_element_type=jnp.float32
    )
    return bands.astype(jnp.bfloat16).astype(jnp.float32)


def power_of(b_ref, d, band):
    total = jnp.zeros((CELLS, LANES), jnp.float32)
    for j in range(ML_RG):
        r = b_ref[d, row_of(band, 0, j)]
        i = b_ref[d, row_of(band, 1, j)]
        total = total + (r * r + i * i)
    return group_sums(total, total, total, total)


def weigh(cross, own, partner, flags):
    (re0, im0), (re1, im1) = cross
    pow0 = own[0] * partner[0] + eps_power
    pow1 = own[1] * partner[1] + eps_power
    coherence = (re0 * re0 + im0 * im0) / pow0 + (re1 * re1 + im1 * im1) / pow1
    weight = flags * 0.5 * coherence
    raw = split_coef * (im0 * re1 - re0 * im1) / jnp.sqrt(pow0 * pow1)
    return weight, weight * raw


def cell_sums(x):
    sub = iota(x.shape, 1)
    upto = x
    for step in (1, 2, 4):
        upto = upto + jnp.where(sub >= step, pltpu.roll(upto, step, 1), 0.0)
    total = jnp.broadcast_to(upto[:, CELLS - 1 : CELLS], x.shape)
    return upto, total - upto + x, total


def solve_kernel(
    m_ref, y_ref, out_ref, b_ref, wh_ref, hb_ref, pw_ref, fl_ref, fh_ref, c_ref, e_ref, q_ref, s_ref, bt_ref, x_ref
):
    n, _, rows, _ = y_ref.shape
    lanes = rows - 4 * ML_AZ
    halos = hb_ref.shape[0]
    lane = iota((8, LANES), 1)
    sub = iota((8, LANES), 0)
    zero = jnp.zeros((8, LANES), jnp.float32)

    def each(step, start):
        return lax.fori_loop(0, n, step, start, unroll=n <= 16)

    def groups(step, start):
        return lax.fori_loop(0, n // 16, step, start, unroll=n <= 16)

    def windows_of(d):
        windows, edges = [], []
        for part in range(2):
            v = y_ref[d, part].astype(jnp.float32).reshape(rows // 8, 8, LANES)
            subs = iota((rows // 8 - 1, 8, LANES), 1)
            merged = pltpu.roll(jnp.where(subs < 4, v[1:], v[:-1]), 4, 1)
            wide = iota((rows // 8 - 2, 8, LANES), 2)
            edge = jnp.where(wide < LANES // 2, merged[1:], merged[:-1])
            windows.append(v[1:-1].reshape(lanes, LANES))
            windows.append(edge.reshape(lanes, LANES))
            first, second, before, final = v[0], v[1], v[rows // 8 - 2], v[rows // 8 - 1]
            later = pltpu.roll(jnp.where(sub < 4, second, final), 4, 0)
            sooner = pltpu.roll(jnp.where(sub < 4, first, before), 4, 0)
            edges.append(jnp.where(sub < 4, final, first))
            edges.append(jnp.where(lane < LANES // 2, later, sooner))
            if part == 0:
                main = final[4:5]
                main = jnp.where(lane[:1] < LANES // 2, pltpu.roll(main, LANES // 2, 1), main)
                fl_ref[d] = jnp.broadcast_to(main, (8, LANES))
                side = first[0:1]
                side = jnp.where(lane[:1] < LANES // 2, side, pltpu.roll(side, LANES // 2, 1))
                fh_ref[d // 16] = jnp.where(lane // 8 == d % 16, jnp.broadcast_to(side, (8, LANES)), fh_ref[d // 16])
        windows = jnp.concatenate(windows, axis=1)
        if lanes < LANES:
            windows = jnp.concatenate([windows, jnp.zeros((LANES - lanes, 4 * LANES), jnp.float32)], axis=0)
        wh_ref[d] = jnp.concatenate(edges, axis=1)
        return windows.astype(jnp.bfloat16)

    def filtered(pair, carry):
        dates = (2 * pair, 2 * pair + 1)
        bands = apply_filter(m_ref[...], jnp.concatenate([windows_of(d) for d in dates], axis=0))
        for t, d in enumerate(dates):
            b_ref[d] = bands[:, LANES * t : LANES * (t + 1)]
            for band in range(2):
                pw_ref[d, band] = power_of(b_ref, d, band)
        return carry

    lax.fori_loop(0, n // 2, filtered, 0, unroll=n <= 16)

    for h in range(halos):
        hb_ref[h] = apply_filter(m_ref[...], wh_ref[16 * h : 16 * h + 16].reshape(LANES, 4 * LANES).astype(jnp.bfloat16))

    def pairs(d, carry):
        later = [jnp.minimum(d + k, n - 1) for k in range(1, SPAN + 1)]
        for band in range(2):
            real = [zero] * SPAN
            imag = [zero] * SPAN
            for j in range(ML_RG):
                r = b_ref[d, row_of(band, 0, j)]
                i = b_ref[d, row_of(band, 1, j)]
                for k in range(SPAN):
                    pr = b_ref[later[k], row_of(band, 0, j)]
                    pi = b_ref[later[k], row_of(band, 1, j)]
                    real[k] = real[k] + (r * pr + i * pi)
                    imag[k] = imag[k] + (i * pr - r * pi)
            c_ref[2 * band, d] = group_sums(*real)
            c_ref[2 * band + 1, d] = group_sums(*imag)
            c_ref[4 + band, d] = pick4(*[pw_ref[e, band] for e in later])
        return carry

    each(pairs, 0)

    def weights(h, carry):
        dates = pl.ds(16 * h, 16)
        cross = [(c_ref[2 * band, dates], c_ref[2 * band + 1, dates]) for band in range(2)]
        own = [pw_ref[dates, band] for band in range(2)]
        partner = [c_ref[4 + band, dates] for band in range(2)]
        q_ref[0, dates], q_ref[1, dates] = weigh(cross, own, partner, fl_ref[dates])
        return carry

    groups(weights, 0)

    hpow = [[power_of(hb_ref, h, band) for band in range(2)] for h in range(halos)]
    for h in range(halos):
        after = min(h + 1, halos - 1)

        def shifted(value, value_after, k):
            moved = back(value, 8 * k)
            if after == h:
                return moved
            return jnp.where(lane < LANES - 8 * k, moved, back(value_after, 8 * k))

        cross, partner = [], []
        for band in range(2):
            real = [zero] * SPAN
            imag = [zero] * SPAN
            for j in range(ML_RG):
                r = hb_ref[h, row_of(band, 0, j)]
                i = hb_ref[h, row_of(band, 1, j)]
                ra = hb_ref[after, row_of(band, 0, j)]
                ia = hb_ref[after, row_of(band, 1, j)]
                for k in range(SPAN):
                    pr = shifted(r, ra, k + 1)
                    pi = shifted(i, ia, k + 1)
                    real[k] = real[k] + (r * pr + i * pi)
                    imag[k] = imag[k] + (i * pr - r * pi)
            cross.append((group_sums(*real), group_sums(*imag)))
            partner.append(pick4(*[shifted(hpow[h][band], hpow[after][band], k) for k in range(1, SPAN + 1)]))
        weight, weighted = weigh(cross, hpow[h], partner, fh_ref[h])
        for which, value in enumerate((weight, weighted)):
            upto, onward, _ = cell_sums(value[None])
            e_ref[h, which, 0] = upto[0]
            e_ref[h, which, 1] = onward[0]

    for d in range(SPAN):
        x_ref[0, d] = zero
        x_ref[1, d] = zero
        x_ref[0, n + SPAN + d] = zero
        x_ref[1, n + SPAN + d] = zero
        for k in range(SPAN):
            s_ref[0, k, d] = zero
            s_ref[1, k, d] = zero

    def smooth(h, chain):
        dates = pl.ds(16 * h, 16)
        wide = iota((16, 8, LANES), 2)
        boxes = []
        for which in range(2):
            upto, onward, total = cell_sums(q_ref[which, dates])
            far_upto = [pltpu.roll(e_ref[h, which, 0], (lanes - 4 - 8 * t) % LANES, 1) for t in range(16)]
            far_onward = [pltpu.roll(e_ref[h, which, 1], (LANES - 4 - 8 * t) % LANES, 1) for t in range(16)]
            sooner = jnp.where(wide < 4, jnp.stack(far_onward), pltpu.roll(onward, 4, 2))
            later = jnp.where(wide >= lanes - 4, jnp.stack(far_upto), pltpu.roll(upto, LANES - 4, 2))
            boxes.append(total + sooner + later)
        phase = boxes[1] / (boxes[0] + floor_weight)
        weight = boxes[0] * (1.0 / (2 * RADIUS + 1))
        product = weight * phase
        own = pl.ds(16 * h + SPAN, 16)
        for k in range(SPAN):
            s_ref[0, k, own] = weight if k == 0 else pltpu.roll(weight, LANES - k, 2)
            s_ref[1, k, own] = product if k == 0 else pltpu.roll(product, LANES - k, 2)
        for t in range(16):
            x_ref[0, 16 * h + t + SPAN] = chain
            chain = chain + phase[t]
        total_weight = jnp.zeros((16, 8, LANES), jnp.float32)
        pull = ridge_weight * x_ref[0, own]
        for k in range(SPAN):
            low = pl.ds(16 * h + SPAN - 1 - k, 16)
            total_weight = total_weight + s_ref[0, k, own] + s_ref[0, k, low]
            pull = pull - s_ref[1, k, own] + s_ref[1, k, low]
        bt_ref[0, dates] = pull
        bt_ref[1, dates] = 1.0 / (total_weight + ridge_weight)
        out_ref[dates] = pltpu.roll(total_weight, 1, 2)
        return chain

    groups(smooth, zero)

    for sweep in range(ITERS):
        old, new = sweep % 2, (sweep + 1) % 2

        def relax(h, carry):
            total = bt_ref[0, pl.ds(16 * h, 16)]
            for k in range(SPAN):
                total = total + s_ref[0, k, pl.ds(16 * h + SPAN, 16)] * x_ref[old, pl.ds(16 * h + SPAN + 1 + k, 16)]
                below = pl.ds(16 * h + SPAN - 1 - k, 16)
                total = total + s_ref[0, k, below] * x_ref[old, below]
            value = total * bt_ref[1, pl.ds(16 * h, 16)]
            x_ref[new, pl.ds(16 * h + SPAN, 16)] = value
            if sweep == ITERS - 1:
                dates = pl.ds(16 * h, 16)
                out_ref[dates] = jnp.where(iota((16, 8, LANES), 2) % 4 == 1, out_ref[dates], value)
            return carry

        groups(relax, 0)


def spread_kernel(x_ref, flags_ref, out_ref, held_ref, in_sems):
    parts = in_sems.shape[1]
    looks = out_ref.shape[0] // parts
    rows = out_ref.shape[2]
    width = x_ref.shape[3] // parts
    pairs = width // (2 * LANES)
    sub = iota((8, LANES), 0)
    lane = iota((8, LANES), 1)
    flags = [flags_ref[0, k].astype(jnp.float32) for k in range(SPAN)]
    pattern = jnp.where(
        lane % 4 < 2, jnp.where(lane % 4 == 0, flags[0], flags[1]), jnp.where(lane % 4 == 2, flags[2], flags[3])
    )
    zero = jnp.zeros((8, LANES), jnp.float32)

    def fetch(part, q):
        columns = pl.ds(q * width, width)
        return pltpu.make_async_copy(x_ref.at[0, part, :, columns], held_ref.at[part, :, columns], in_sems.at[part, q])

    for part in range(2):
        for q in range(parts):
            fetch(part, q).start()
    for part in range(2):
        made = {}

        def pair_of(index, half):
            if index < 0 or index >= parts * pairs:
                return zero, zero
            if (index, half) not in made:
                start = index * 2 * LANES
                first = held_ref[part, :, start : start + LANES].astype(jnp.float32)[8 * half : 8 * half + 8]
                second = held_ref[part, :, start + LANES : start + 2 * LANES].astype(jnp.float32)[8 * half : 8 * half + 8]
                mixed = pltpu.roll(jnp.where(sub < 4, second, first), 4, 0)
                made[index, half] = (jnp.where(sub < 4, first, mixed), jnp.where(sub < 4, mixed, second))
            return made[index, half]

        for q in range(parts):
            if q == 0:
                fetch(part, 0).wait()
            if q + 1 < parts:
                fetch(part, q + 1).wait()
            for tile in range(rows // 16):
                upper = q * pairs - 1 + 2 * tile
                for half in range(looks // 2):
                    for odd in range(2):
                        top = pair_of(upper, half)[odd]
                        bottom = pair_of(upper + 1, half)[odd]
                        if part == 0 and tile == 0:
                            side = lane // SPAN % 2
                            inside = jnp.where(side == 0, float(q < parts - 1), float(q > 0))
                            top = jnp.where((sub < 4) & (lane < LANES // 2), pattern * inside, top)
                        if part == 0 and tile == rows // 16 - 1:
                            bottom = jnp.where((sub >= 4) & (lane >= LANES // 2), pattern, bottom)
                        both = jnp.concatenate([top, bottom], axis=0).astype(jnp.bfloat16)
                        out_ref[q * looks + 2 * half + odd, part, 16 * tile : 16 * tile + 16, :] = both


def gather_kernel(z_ref, phase_ref, weight_ref):
    count = z_ref.shape[0]
    looks = phase_ref.shape[1]
    width = 2 * LANES
    source = iota((LANES, 2 * width), 0)
    column = iota((LANES, 2 * width), 1)
    block = column % width // CELLS
    chosen = (source == SPAN * block + column // width).astype(jnp.float32)
    values = z_ref[...].reshape(count * CELLS, LANES)
    moved = jnp.dot(values, chosen, precision=lax.Precision.HIGHEST, preferred_element_type=jnp.float32)
    row = iota((count * CELLS, 2 * width), 0)
    column = iota((count * CELLS, 2 * width), 1)
    moved = jnp.where(row % CELLS == column % CELLS, moved, 0.0)
    adder = (iota((count, count * CELLS), 1) // CELLS == iota((count, count * CELLS), 0)).astype(jnp.float32)
    lines = jnp.dot(adder, moved, precision=lax.Precision.HIGHEST, preferred_element_type=jnp.float32)
    for q in range(count // looks):
        for which, out in enumerate((phase_ref, weight_ref)):
            out[0, :, width * q : width * (q + 1)] = lines[
                looks * q : looks * (q + 1), width * which : width * (which + 1)
            ]


def local(slc_stack, band_taps, pair_flags):
    n = lax.axis_size("date")
    looks = slc_stack.shape[2] // ML_AZ
    parts = n // looks
    lanes = slc_stack.shape[3] // (parts * LANES) * ML_AZ
    rows = lanes + 4 * ML_AZ
    halos = n * 8 // LANES
    tile = (8, LANES)
    in_vmem = pl.BlockSpec(memory_space=pltpu.VMEM)
    anywhere = pl.BlockSpec(memory_space=pl.ANY)
    params = pltpu.CompilerParams(vmem_limit_bytes=60 * 1024 * 1024)
    chunks = pl.pallas_call(
        spread_kernel,
        out_shape=pltpu.VMEM((n, 2, rows, LANES), jnp.bfloat16),
        in_specs=[anywhere, pl.BlockSpec(memory_space=pltpu.SMEM)],
        out_specs=in_vmem,
        scratch_shapes=[
            pltpu.VMEM(slc_stack.shape[1:], jnp.bfloat16),
            pltpu.SemaphoreType.DMA((2, parts)),
        ],
        compiler_params=params,
    )(slc_stack, pair_flags)
    y = pltpu.with_memory_space_constraint(lax.all_to_all(chunks, "date", 0, 0, tiled=True), pltpu.VMEM)
    taps = jnp.pad(band_taps.astype(jnp.float32).reshape(4, TAPS), ((0, 0), (0, 2 * LANES - TAPS)))
    matrix = pl.pallas_call(
        filter_kernel,
        out_shape=pltpu.VMEM((4 * LANES, 4 * LANES), jnp.bfloat16),
        in_specs=[in_vmem],
        out_specs=in_vmem,
        compiler_params=params,
    )(taps)
    matrix = pltpu.with_memory_space_constraint(matrix, pltpu.VMEM)
    solved = pl.pallas_call(
        solve_kernel,
        out_shape=pltpu.VMEM((n, *tile), jnp.float32),
        in_specs=[in_vmem, in_vmem],
        out_specs=in_vmem,
        scratch_shapes=[
            pltpu.VMEM((n, 4 * LANES, LANES), jnp.float32),
            pltpu.VMEM((n, 8, 4 * LANES), jnp.float32),
            pltpu.VMEM((halos, 4 * LANES, LANES), jnp.float32),
            pltpu.VMEM((n, 2, *tile), jnp.float32),
            pltpu.VMEM((n, *tile), jnp.float32),
            pltpu.VMEM((halos, *tile), jnp.float32),
            pltpu.VMEM((6, n, *tile), jnp.float32),
            pltpu.VMEM((halos, 2, 2, *tile), jnp.float32),
            pltpu.VMEM((2, n, *tile), jnp.float32),
            pltpu.VMEM((2, SPAN, n + SPAN, *tile), jnp.float32),
            pltpu.VMEM((2, n, *tile), jnp.float32),
            pltpu.VMEM((2, n + 2 * SPAN, *tile), jnp.float32),
        ],
        compiler_params=params,
    )(matrix, y)
    z = lax.all_to_all(solved, "date", 0, 0, tiled=True)
    shape = (1, looks, slc_stack.shape[3] // ML_RG)
    if lanes == LANES:
        return tuple(
            pl.pallas_call(
                gather_kernel,
                out_shape=[jax.ShapeDtypeStruct(shape, jnp.float32)] * 2,
                in_specs=[in_vmem],
                out_specs=[in_vmem] * 2,
                compiler_params=params,
            )(pltpu.with_memory_space_constraint(z, pltpu.VMEM))
        )
    z = z[:, :, :lanes].reshape(parts, looks, CELLS, lanes // SPAN, SPAN)[..., :2]
    z = z.transpose(4, 1, 0, 3, 2).reshape(2, *shape)
    return (z[0], z[1])


def solution(mesh):
    in_specs = (P("date", None, "group", None), P(), P("date", None))
    out_specs = (P("date", "group", None), P("date", "group", None))
    return jax.shard_map(local, mesh=mesh, in_specs=in_specs, out_specs=out_specs, check_vma=False)
```

```python
import jax
import jax.numpy as jnp
from jax import lax
from jax.experimental import pallas as pl
from jax.experimental.pallas import tpu as pltpu
from jax.sharding import PartitionSpec as P

TAPS = 32
ML_AZ = 4
ML_RG = 16
SPAN = 4
RADIUS = 8
ITERS = 4
LANES = 128
CELLS = LANES // ML_RG

eps_power = 1e-06
floor_weight = 0.1
ridge_weight = 0.05
split_coef = 2.0


def iota(shape, axis):
    return lax.broadcasted_iota(jnp.int32, shape, axis)


def back(x, steps):
    return pltpu.roll(x, LANES - steps, 1)


def group_sums(x0, x1, x2, x3):
    lane = iota((8, LANES), 1)
    even = lane % 2 == 0
    low = lane % 4 < 2
    u = jnp.where(even, x0 + back(x0, 1), x1 + pltpu.roll(x1, 1, 1))
    v = jnp.where(even, x2 + back(x2, 1), x3 + pltpu.roll(x3, 1, 1))
    return jnp.where(low, u + back(u, 2), v + pltpu.roll(v, 2, 1))


def pick4(x0, x1, x2, x3):
    lane = iota((8, LANES), 1) % 4
    return jnp.where(lane < 2, jnp.where(lane == 0, x0, x1), jnp.where(lane == 2, x2, x3))


def fill_filter(taps_ref, m_ref):
    width = 2 * LANES
    sub = iota((CELLS, width), 0)

    def placed(row):
        taps = jnp.broadcast_to(taps_ref[row], (CELLS, width))
        result = jnp.zeros((CELLS, width), jnp.float32)
        for c in range(CELLS):
            result = jnp.where(sub == c, pltpu.roll(taps, (ML_RG * c - TAPS // 2) % width, 1), result)
        return result

    def along(base, j):
        both = [base if jj == 0 else pltpu.roll(base, jj, 1) for jj in (j, j + 1)]
        return jnp.concatenate(both, axis=0)

    for band in range(2):
        real, imag = placed(2 * band), placed(2 * band + 1)
        for j in range(0, ML_RG, 2):
            tr, ti = along(real, j), along(imag, j)
            real_row = ((band * 2 + 0) * ML_RG + j) * CELLS
            imag_row = ((band * 2 + 1) * ML_RG + j) * CELLS
            m_ref[real_row : real_row + 16, :width] = tr.astype(jnp.bfloat16)
            m_ref[real_row : real_row + 16, width:] = (-ti).astype(jnp.bfloat16)
            m_ref[imag_row : imag_row + 16, :width] = ti.astype(jnp.bfloat16)
            m_ref[imag_row : imag_row + 16, width:] = tr.astype(jnp.bfloat16)


def row_of(band, part, j):
    start = ((band * 2 + part) * ML_RG + j) * CELLS
    return slice(start, start + CELLS)


def apply_filter(matrix, windows):
    bands = lax.dot_general(
        matrix, windows, (((1,), (1,)), ((), ())), preferred_element_type=jnp.float32
    )
    return bands.astype(jnp.bfloat16).astype(jnp.float32)


def power_of(b_ref, d, band):
    total = jnp.zeros((CELLS, LANES), jnp.float32)
    for j in range(ML_RG):
        r = b_ref[d, row_of(band, 0, j)]
        i = b_ref[d, row_of(band, 1, j)]
        total = total + (r * r + i * i)
    return group_sums(total, total, total, total)


def weigh(cross, own, partner, flags):
    (re0, im0), (re1, im1) = cross
    pow0 = own[0] * partner[0] + eps_power
    pow1 = own[1] * partner[1] + eps_power
    coherence = (re0 * re0 + im0 * im0) / pow0 + (re1 * re1 + im1 * im1) / pow1
    weight = flags * 0.5 * coherence
    raw = split_coef * (im0 * re1 - re0 * im1) / jnp.sqrt(pow0 * pow1)
    return weight, weight * raw


def cell_sums(x):
    sub = iota(x.shape, 1)
    upto = x
    for step in (1, 2, 4):
        upto = upto + jnp.where(sub >= step, pltpu.roll(upto, step, 1), 0.0)
    total = jnp.broadcast_to(upto[:, CELLS - 1 : CELLS], x.shape)
    return upto, total - upto + x, total


def solve_kernel(
    m_ref, y_ref, out_ref, b_ref, wh_ref, hb_ref, pw_ref, fl_ref, fh_ref, c_ref, e_ref, q_ref, s_ref, bt_ref, x_ref
):
    n, _, rows, _ = y_ref.shape
    lanes = rows - 4 * ML_AZ
    halos = hb_ref.shape[0]
    lane = iota((8, LANES), 1)
    sub = iota((8, LANES), 0)
    zero = jnp.zeros((8, LANES), jnp.float32)

    def each(step, start):
        return lax.fori_loop(0, n, step, start, unroll=n <= 16)

    def groups(step, start):
        return lax.fori_loop(0, n // 16, step, start, unroll=n <= 16)

    def windows_of(d):
        windows, edges = [], []
        for part in range(2):
            v = y_ref[d, part].astype(jnp.float32).reshape(rows // 8, 8, LANES)
            subs = iota((rows // 8 - 1, 8, LANES), 1)
            merged = pltpu.roll(jnp.where(subs < 4, v[1:], v[:-1]), 4, 1)
            wide = iota((rows // 8 - 2, 8, LANES), 2)
            edge = jnp.where(wide < LANES // 2, merged[1:], merged[:-1])
            windows.append(v[1:-1].reshape(lanes, LANES))
            windows.append(edge.reshape(lanes, LANES))
            first, second, before, final = v[0], v[1], v[rows // 8 - 2], v[rows // 8 - 1]
            later = pltpu.roll(jnp.where(sub < 4, second, final), 4, 0)
            sooner = pltpu.roll(jnp.where(sub < 4, first, before), 4, 0)
            edges.append(jnp.where(sub < 4, final, first))
            edges.append(jnp.where(lane < LANES // 2, later, sooner))
            if part == 0:
                main = final[4:5]
                main = jnp.where(lane[:1] < LANES // 2, pltpu.roll(main, LANES // 2, 1), main)
                fl_ref[d] = jnp.broadcast_to(main, (8, LANES))
                side = first[0:1]
                side = jnp.where(lane[:1] < LANES // 2, side, pltpu.roll(side, LANES // 2, 1))
                fh_ref[d // 16] = jnp.where(lane // 8 == d % 16, jnp.broadcast_to(side, (8, LANES)), fh_ref[d // 16])
        windows = jnp.concatenate(windows, axis=1)
        if lanes < LANES:
            windows = jnp.concatenate([windows, jnp.zeros((LANES - lanes, 4 * LANES), jnp.float32)], axis=0)
        wh_ref[d] = jnp.concatenate(edges, axis=1)
        return windows.astype(jnp.bfloat16)

    def filtered(pair, carry):
        dates = (2 * pair, 2 * pair + 1)
        bands = apply_filter(m_ref[...], jnp.concatenate([windows_of(d) for d in dates], axis=0))
        for t, d in enumerate(dates):
            b_ref[d] = bands[:, LANES * t : LANES * (t + 1)]
            for band in range(2):
                pw_ref[d, band] = power_of(b_ref, d, band)
        return carry

    lax.fori_loop(0, n // 2, filtered, 0, unroll=n <= 16)

    for h in range(halos):
        hb_ref[h] = apply_filter(m_ref[...], wh_ref[16 * h : 16 * h + 16].reshape(LANES, 4 * LANES).astype(jnp.bfloat16))

    def pairs(d, carry):
        later = [jnp.minimum(d + k, n - 1) for k in range(1, SPAN + 1)]
        for band in range(2):
            real = [zero] * SPAN
            imag = [zero] * SPAN
            for j in range(ML_RG):
                r = b_ref[d, row_of(band, 0, j)]
                i = b_ref[d, row_of(band, 1, j)]
                for k in range(SPAN):
                    pr = b_ref[later[k], row_of(band, 0, j)]
                    pi = b_ref[later[k], row_of(band, 1, j)]
                    real[k] = real[k] + (r * pr + i * pi)
                    imag[k] = imag[k] + (i * pr - r * pi)
            c_ref[2 * band, d] = group_sums(*real)
            c_ref[2 * band + 1, d] = group_sums(*imag)
            c_ref[4 + band, d] = pick4(*[pw_ref[e, band] for e in later])
        return carry

    each(pairs, 0)

    def weights(h, carry):
        dates = pl.ds(16 * h, 16)
        cross = [(c_ref[2 * band, dates], c_ref[2 * band + 1, dates]) for band in range(2)]
        own = [pw_ref[dates, band] for band in range(2)]
        partner = [c_ref[4 + band, dates] for band in range(2)]
        q_ref[0, dates], q_ref[1, dates] = weigh(cross, own, partner, fl_ref[dates])
        return carry

    groups(weights, 0)

    hpow = [[power_of(hb_ref, h, band) for band in range(2)] for h in range(halos)]
    for h in range(halos):
        after = min(h + 1, halos - 1)

        def shifted(value, value_after, k):
            moved = back(value, 8 * k)
            if after == h:
                return moved
            return jnp.where(lane < LANES - 8 * k, moved, back(value_after, 8 * k))

        cross, partner = [], []
        for band in range(2):
            real = [zero] * SPAN
            imag = [zero] * SPAN
            for j in range(ML_RG):
                r = hb_ref[h, row_of(band, 0, j)]
                i = hb_ref[h, row_of(band, 1, j)]
                ra = hb_ref[after, row_of(band, 0, j)]
                ia = hb_ref[after, row_of(band, 1, j)]
                for k in range(SPAN):
                    pr = shifted(r, ra, k + 1)
                    pi = shifted(i, ia, k + 1)
                    real[k] = real[k] + (r * pr + i * pi)
                    imag[k] = imag[k] + (i * pr - r * pi)
            cross.append((group_sums(*real), group_sums(*imag)))
            partner.append(pick4(*[shifted(hpow[h][band], hpow[after][band], k) for k in range(1, SPAN + 1)]))
        weight, weighted = weigh(cross, hpow[h], partner, fh_ref[h])
        for which, value in enumerate((weight, weighted)):
            upto, onward, _ = cell_sums(value[None])
            e_ref[h, which, 0] = upto[0]
            e_ref[h, which, 1] = onward[0]

    for d in range(SPAN):
        x_ref[0, d] = zero
        x_ref[1, d] = zero
        x_ref[0, n + SPAN + d] = zero
        x_ref[1, n + SPAN + d] = zero
        for k in range(SPAN):
            s_ref[0, k, d] = zero
            s_ref[1, k, d] = zero

    def smooth(h, chain):
        dates = pl.ds(16 * h, 16)
        wide = iota((16, 8, LANES), 2)
        boxes = []
        for which in range(2):
            upto, onward, total = cell_sums(q_ref[which, dates])
            far_upto = [pltpu.roll(e_ref[h, which, 0], (lanes - 4 - 8 * t) % LANES, 1) for t in range(16)]
            far_onward = [pltpu.roll(e_ref[h, which, 1], (LANES - 4 - 8 * t) % LANES, 1) for t in range(16)]
            sooner = jnp.where(wide < 4, jnp.stack(far_onward), pltpu.roll(onward, 4, 2))
            later = jnp.where(wide >= lanes - 4, jnp.stack(far_upto), pltpu.roll(upto, LANES - 4, 2))
            boxes.append(total + sooner + later)
        phase = boxes[1] / (boxes[0] + floor_weight)
        weight = boxes[0] * (1.0 / (2 * RADIUS + 1))
        product = weight * phase
        own = pl.ds(16 * h + SPAN, 16)
        for k in range(SPAN):
            s_ref[0, k, own] = weight if k == 0 else pltpu.roll(weight, LANES - k, 2)
            s_ref[1, k, own] = product if k == 0 else pltpu.roll(product, LANES - k, 2)
        for t in range(16):
            x_ref[0, 16 * h + t + SPAN] = chain
            chain = chain + phase[t]
        total_weight = jnp.zeros((16, 8, LANES), jnp.float32)
        pull = ridge_weight * x_ref[0, own]
        for k in range(SPAN):
            low = pl.ds(16 * h + SPAN - 1 - k, 16)
            total_weight = total_weight + s_ref[0, k, own] + s_ref[0, k, low]
            pull = pull - s_ref[1, k, own] + s_ref[1, k, low]
        bt_ref[0, dates] = pull
        bt_ref[1, dates] = 1.0 / (total_weight + ridge_weight)
        out_ref[dates] = pltpu.roll(total_weight, 1, 2)
        return chain

    groups(smooth, zero)

    for sweep in range(ITERS):
        old, new = sweep % 2, (sweep + 1) % 2

        def relax(h, carry):
            total = bt_ref[0, pl.ds(16 * h, 16)]
            for k in range(SPAN):
                total = total + s_ref[0, k, pl.ds(16 * h + SPAN, 16)] * x_ref[old, pl.ds(16 * h + SPAN + 1 + k, 16)]
                below = pl.ds(16 * h + SPAN - 1 - k, 16)
                total = total + s_ref[0, k, below] * x_ref[old, below]
            value = total * bt_ref[1, pl.ds(16 * h, 16)]
            x_ref[new, pl.ds(16 * h + SPAN, 16)] = value
            if sweep == ITERS - 1:
                dates = pl.ds(16 * h, 16)
                out_ref[dates] = jnp.where(iota((16, 8, LANES), 2) % 4 == 1, out_ref[dates], value)
            return carry

        groups(relax, 0)


def spread_kernel(x_ref, far_flags_ref, far_taps_ref, out_ref, m_ref, held_ref, flags_ref, taps_ref, wide_ref, in_sems, side_sems):
    parts = in_sems.shape[1]
    looks = out_ref.shape[0] // parts
    rows = out_ref.shape[2]
    width = x_ref.shape[3] // parts
    pairs = width // (2 * LANES)
    sub = iota((8, LANES), 0)
    lane = iota((8, LANES), 1)
    zero = jnp.zeros((8, LANES), jnp.float32)

    def fetch(part, q):
        columns = pl.ds(q * width, width)
        return pltpu.make_async_copy(x_ref.at[0, part, :, columns], held_ref.at[part, :, columns], in_sems.at[part, q])

    get_flags = pltpu.make_async_copy(far_flags_ref, flags_ref, side_sems.at[0])
    get_taps = pltpu.make_async_copy(far_taps_ref, taps_ref, side_sems.at[1])
    get_taps.start()
    get_flags.start()
    for part in range(2):
        for q in range(parts):
            fetch(part, q).start()
    wide_ref[...] = jnp.zeros_like(wide_ref)
    get_taps.wait()
    for band in range(2):
        for part in range(2):
            wide_ref[2 * band + part, :, :TAPS] = taps_ref[band, part : part + 1, :].astype(jnp.float32)
    fill_filter(wide_ref, m_ref)
    get_flags.wait()
    flags = [flags_ref[0, k].astype(jnp.float32) for k in range(SPAN)]
    pattern = jnp.where(
        lane % 4 < 2, jnp.where(lane % 4 == 0, flags[0], flags[1]), jnp.where(lane % 4 == 2, flags[2], flags[3])
    )
    for part in range(2):
        made = {}

        def pair_of(index, half):
            if index < 0 or index >= parts * pairs:
                return zero, zero
            if (index, half) not in made:
                start = index * 2 * LANES
                first = held_ref[part, :, start : start + LANES].astype(jnp.float32)[8 * half : 8 * half + 8]
                second = held_ref[part, :, start + LANES : start + 2 * LANES].astype(jnp.float32)[8 * half : 8 * half + 8]
                mixed = pltpu.roll(jnp.where(sub < 4, second, first), 4, 0)
                made[index, half] = (jnp.where(sub < 4, first, mixed), jnp.where(sub < 4, mixed, second))
            return made[index, half]

        for q in range(parts):
            if q == 0:
                fetch(part, 0).wait()
            if q + 1 < parts:
                fetch(part, q + 1).wait()
            for tile in range(rows // 16):
                upper = q * pairs - 1 + 2 * tile
                for half in range(looks // 2):
                    for odd in range(2):
                        top = pair_of(upper, half)[odd]
                        bottom = pair_of(upper + 1, half)[odd]
                        if part == 0 and tile == 0:
                            side = lane // SPAN % 2
                            inside = jnp.where(side == 0, float(q < parts - 1), float(q > 0))
                            top = jnp.where((sub < 4) & (lane < LANES // 2), pattern * inside, top)
                        if part == 0 and tile == rows // 16 - 1:
                            bottom = jnp.where((sub >= 4) & (lane >= LANES // 2), pattern, bottom)
                        both = jnp.concatenate([top, bottom], axis=0).astype(jnp.bfloat16)
                        out_ref[q * looks + 2 * half + odd, part, 16 * tile : 16 * tile + 16, :] = both


def gather_kernel(z_ref, phase_ref, weight_ref):
    count = z_ref.shape[0]
    looks = phase_ref.shape[1]
    width = 2 * LANES
    source = iota((LANES, 2 * width), 0)
    column = iota((LANES, 2 * width), 1)
    block = column % width // CELLS
    chosen = (source == SPAN * block + column // width).astype(jnp.float32)
    values = z_ref[...].reshape(count * CELLS, LANES)
    moved = jnp.dot(values, chosen, precision=lax.Precision.HIGHEST, preferred_element_type=jnp.float32)
    row = iota((count * CELLS, 2 * width), 0)
    column = iota((count * CELLS, 2 * width), 1)
    moved = jnp.where(row % CELLS == column % CELLS, moved, 0.0)
    adder = (iota((count, count * CELLS), 1) // CELLS == iota((count, count * CELLS), 0)).astype(jnp.float32)
    lines = jnp.dot(adder, moved, precision=lax.Precision.HIGHEST, preferred_element_type=jnp.float32)
    for q in range(count // looks):
        for which, out in enumerate((phase_ref, weight_ref)):
            out[0, :, width * q : width * (q + 1)] = lines[
                looks * q : looks * (q + 1), width * which : width * (which + 1)
            ]


def local(slc_stack, band_taps, pair_flags):
    n = lax.axis_size("date")
    looks = slc_stack.shape[2] // ML_AZ
    parts = n // looks
    lanes = slc_stack.shape[3] // (parts * LANES) * ML_AZ
    rows = lanes + 4 * ML_AZ
    halos = n * 8 // LANES
    tile = (8, LANES)
    in_vmem = pl.BlockSpec(memory_space=pltpu.VMEM)
    anywhere = pl.BlockSpec(memory_space=pl.ANY)
    params = pltpu.CompilerParams(vmem_limit_bytes=60 * 1024 * 1024)
    chunks, matrix = pl.pallas_call(
        spread_kernel,
        out_shape=[
            pltpu.VMEM((n, 2, rows, LANES), jnp.bfloat16),
            pltpu.VMEM((4 * LANES, 4 * LANES), jnp.bfloat16),
        ],
        in_specs=[anywhere] * 3,
        out_specs=[in_vmem] * 2,
        scratch_shapes=[
            pltpu.VMEM(slc_stack.shape[1:], jnp.bfloat16),
            pltpu.SMEM(pair_flags.shape, jnp.int32),
            pltpu.VMEM(band_taps.shape, jnp.bfloat16),
            pltpu.VMEM((4, 1, 2 * LANES), jnp.float32),
            pltpu.SemaphoreType.DMA((2, parts)),
            pltpu.SemaphoreType.DMA((2,)),
        ],
        compiler_params=params,
    )(slc_stack, pair_flags, band_taps)
    y = pltpu.with_memory_space_constraint(lax.all_to_all(chunks, "date", 0, 0, tiled=True), pltpu.VMEM)
    matrix = pltpu.with_memory_space_constraint(matrix, pltpu.VMEM)
    solved = pl.pallas_call(
        solve_kernel,
        out_shape=pltpu.VMEM((n, *tile), jnp.float32),
        in_specs=[in_vmem, in_vmem],
        out_specs=in_vmem,
        scratch_shapes=[
            pltpu.VMEM((n, 4 * LANES, LANES), jnp.float32),
            pltpu.VMEM((n, 8, 4 * LANES), jnp.float32),
            pltpu.VMEM((halos, 4 * LANES, LANES), jnp.float32),
            pltpu.VMEM((n, 2, *tile), jnp.float32),
            pltpu.VMEM((n, *tile), jnp.float32),
            pltpu.VMEM((halos, *tile), jnp.float32),
            pltpu.VMEM((6, n, *tile), jnp.float32),
            pltpu.VMEM((halos, 2, 2, *tile), jnp.float32),
            pltpu.VMEM((2, n, *tile), jnp.float32),
            pltpu.VMEM((2, SPAN, n + SPAN, *tile), jnp.float32),
            pltpu.VMEM((2, n, *tile), jnp.float32),
            pltpu.VMEM((2, n + 2 * SPAN, *tile), jnp.float32),
        ],
        compiler_params=params,
    )(matrix, y)
    z = lax.all_to_all(solved, "date", 0, 0, tiled=True)
    shape = (1, looks, slc_stack.shape[3] // ML_RG)
    if lanes == LANES:
        return tuple(
            pl.pallas_call(
                gather_kernel,
                out_shape=[jax.ShapeDtypeStruct(shape, jnp.float32)] * 2,
                in_specs=[in_vmem],
                out_specs=[in_vmem] * 2,
                compiler_params=params,
            )(pltpu.with_memory_space_constraint(z, pltpu.VMEM))
        )
    z = z[:, :, :lanes].reshape(parts, looks, CELLS, lanes // SPAN, SPAN)[..., :2]
    z = z.transpose(4, 1, 0, 3, 2).reshape(2, *shape)
    return (z[0], z[1])


def solution(mesh):
    in_specs = (P("date", None, "group", None), P(), P("date", None))
    out_specs = (P("date", "group", None), P("date", "group", None))
    return jax.shard_map(local, mesh=mesh, in_specs=in_specs, out_specs=out_specs, check_vma=False)
```

```python
import jax
import jax.numpy as jnp
from jax import lax
from jax.experimental import pallas as pl
from jax.experimental.pallas import tpu as pltpu
from jax.sharding import PartitionSpec as P

TAPS = 32
ML_AZ = 4
ML_RG = 16
SPAN = 4
RADIUS = 8
ITERS = 4
LANES = 128
CELLS = LANES // ML_RG

eps_power = 1e-06
floor_weight = 0.1
ridge_weight = 0.05
split_coef = 2.0


def iota(shape, axis):
    return lax.broadcasted_iota(jnp.int32, shape, axis)


def back(x, steps):
    return pltpu.roll(x, LANES - steps, 1)


def group_sums(x0, x1, x2, x3):
    lane = iota((8, LANES), 1)
    even = lane % 2 == 0
    low = lane % 4 < 2
    u = jnp.where(even, x0 + back(x0, 1), x1 + pltpu.roll(x1, 1, 1))
    v = jnp.where(even, x2 + back(x2, 1), x3 + pltpu.roll(x3, 1, 1))
    return jnp.where(low, u + back(u, 2), v + pltpu.roll(v, 2, 1))


def pick4(x0, x1, x2, x3):
    lane = iota((8, LANES), 1) % 4
    return jnp.where(lane < 2, jnp.where(lane == 0, x0, x1), jnp.where(lane == 2, x2, x3))


def fill_filter(taps_ref, m_ref):
    width = 2 * LANES
    sub = iota((CELLS, width), 0)

    def placed(row):
        taps = jnp.broadcast_to(taps_ref[row], (CELLS, width))
        result = jnp.zeros((CELLS, width), jnp.float32)
        for c in range(CELLS):
            result = jnp.where(sub == c, pltpu.roll(taps, (ML_RG * c - TAPS // 2) % width, 1), result)
        return result

    def along(base, j):
        both = [base if jj == 0 else pltpu.roll(base, jj, 1) for jj in (j, j + 1)]
        return jnp.concatenate(both, axis=0)

    for band in range(2):
        real, imag = placed(2 * band), placed(2 * band + 1)
        for j in range(0, ML_RG, 2):
            tr, ti = along(real, j), along(imag, j)
            real_row = ((band * 2 + 0) * ML_RG + j) * CELLS
            imag_row = ((band * 2 + 1) * ML_RG + j) * CELLS
            m_ref[real_row : real_row + 16, :width] = tr.astype(jnp.bfloat16)
            m_ref[real_row : real_row + 16, width:] = (-ti).astype(jnp.bfloat16)
            m_ref[imag_row : imag_row + 16, :width] = ti.astype(jnp.bfloat16)
            m_ref[imag_row : imag_row + 16, width:] = tr.astype(jnp.bfloat16)


def row_of(band, part, j):
    start = ((band * 2 + part) * ML_RG + j) * CELLS
    return slice(start, start + CELLS)


def apply_filter(matrix, windows):
    bands = lax.dot_general(
        matrix, windows, (((1,), (1,)), ((), ())), preferred_element_type=jnp.float32
    )
    return bands.astype(jnp.bfloat16).astype(jnp.float32)


def power_of(b_ref, d, band):
    total = jnp.zeros((CELLS, LANES), jnp.float32)
    for j in range(ML_RG):
        r = b_ref[d, row_of(band, 0, j)]
        i = b_ref[d, row_of(band, 1, j)]
        total = total + (r * r + i * i)
    return group_sums(total, total, total, total)


def weigh(cross, own, partner, flags):
    (re0, im0), (re1, im1) = cross
    pow0 = own[0] * partner[0] + eps_power
    pow1 = own[1] * partner[1] + eps_power
    coherence = (re0 * re0 + im0 * im0) / pow0 + (re1 * re1 + im1 * im1) / pow1
    weight = flags * 0.5 * coherence
    raw = split_coef * (im0 * re1 - re0 * im1) / jnp.sqrt(pow0 * pow1)
    return weight, weight * raw


def cell_sums(x):
    sub = iota(x.shape, 1)
    upto = x
    for step in (1, 2, 4):
        upto = upto + jnp.where(sub >= step, pltpu.roll(upto, step, 1), 0.0)
    total = jnp.broadcast_to(upto[:, CELLS - 1 : CELLS], x.shape)
    return upto, total - upto + x, total


def solve_kernel(
    m_ref, y_ref, out_ref, b_ref, wh_ref, hb_ref, pw_ref, fl_ref, fh_ref, c_ref, e_ref, q_ref, s_ref, bt_ref, x_ref
):
    n, rows, _ = y_ref.shape
    tiles = rows // 16
    lanes = 8 * (tiles - 1)
    halos = hb_ref.shape[0]
    lane = iota((8, LANES), 1)
    sub = iota((8, LANES), 0)
    zero = jnp.zeros((8, LANES), jnp.float32)

    def each(step, start):
        return lax.fori_loop(0, n, step, start, unroll=n <= 16)

    def groups(step, start):
        return lax.fori_loop(0, n // 16, step, start, unroll=n <= 16)

    def windows_of(d):
        windows, edges = [], []
        held = y_ref[d].astype(jnp.float32).reshape(rows // 8, 8, LANES)
        beyond = held[rows // 8 - 1]
        main = beyond[0:1]
        main = jnp.where(lane[:1] < LANES // 2, pltpu.roll(main, LANES // 2, 1), main)
        fl_ref[d] = jnp.broadcast_to(main, (8, LANES))
        side = beyond[4:5]
        middle = (lane[:1] >= LANES // 4) & (lane[:1] < 3 * LANES // 4)
        side = jnp.where(middle, side, pltpu.roll(side, LANES // 2, 1))
        fh_ref[d // 16] = jnp.where(lane // 8 == d % 16, jnp.broadcast_to(side, (8, LANES)), fh_ref[d // 16])
        for part in range(2):
            v = held[part * tiles : (part + 1) * tiles]
            subs = iota((tiles - 1, 8, LANES), 1)
            wide = iota((tiles - 1, 8, LANES), 2)
            main = pltpu.roll(jnp.where(subs < 4, v[1:], v[:-1]), 4, 1)
            edge = jnp.where(wide < LANES // 2, v[1:], v[:-1])
            windows.append(main.reshape(lanes, LANES))
            windows.append(edge.reshape(lanes, LANES))
            first, last = v[0], v[tiles - 1]
            far = beyond if part == 0 else pltpu.roll(beyond, LANES - TAPS // 2, 1)
            edges.append(pltpu.roll(jnp.where(sub < 4, first, last), 4, 0))
            later = jnp.where(sub < 4, far, first)
            sooner = jnp.where(sub < 4, last, far)
            edges.append(jnp.where(lane < LANES // 2, later, sooner))
        windows = jnp.concatenate(windows, axis=1)
        if lanes < LANES:
            windows = jnp.concatenate([windows, jnp.zeros((LANES - lanes, 4 * LANES), jnp.float32)], axis=0)
        wh_ref[d] = jnp.concatenate(edges, axis=1)
        return windows.astype(jnp.bfloat16)

    def filtered(pair, carry):
        dates = (2 * pair, 2 * pair + 1)
        bands = apply_filter(m_ref[...], jnp.concatenate([windows_of(d) for d in dates], axis=0))
        for t, d in enumerate(dates):
            b_ref[d] = bands[:, LANES * t : LANES * (t + 1)]
            for band in range(2):
                pw_ref[d, band] = power_of(b_ref, d, band)
        return carry

    lax.fori_loop(0, n // 2, filtered, 0, unroll=n <= 16)

    for h in range(halos):
        hb_ref[h] = apply_filter(m_ref[...], wh_ref[16 * h : 16 * h + 16].reshape(LANES, 4 * LANES).astype(jnp.bfloat16))

    def pairs(d, carry):
        later = [jnp.minimum(d + k, n - 1) for k in range(1, SPAN + 1)]
        for band in range(2):
            real = [zero] * SPAN
            imag = [zero] * SPAN
            for j in range(ML_RG):
                r = b_ref[d, row_of(band, 0, j)]
                i = b_ref[d, row_of(band, 1, j)]
                for k in range(SPAN):
                    pr = b_ref[later[k], row_of(band, 0, j)]
                    pi = b_ref[later[k], row_of(band, 1, j)]
                    real[k] = real[k] + (r * pr + i * pi)
                    imag[k] = imag[k] + (i * pr - r * pi)
            c_ref[2 * band, d] = group_sums(*real)
            c_ref[2 * band + 1, d] = group_sums(*imag)
            c_ref[4 + band, d] = pick4(*[pw_ref[e, band] for e in later])
        return carry

    each(pairs, 0)

    def weights(h, carry):
        dates = pl.ds(16 * h, 16)
        cross = [(c_ref[2 * band, dates], c_ref[2 * band + 1, dates]) for band in range(2)]
        own = [pw_ref[dates, band] for band in range(2)]
        partner = [c_ref[4 + band, dates] for band in range(2)]
        q_ref[0, dates], q_ref[1, dates] = weigh(cross, own, partner, fl_ref[dates])
        return carry

    groups(weights, 0)

    hpow = [[power_of(hb_ref, h, band) for band in range(2)] for h in range(halos)]
    for h in range(halos):
        after = min(h + 1, halos - 1)

        def shifted(value, value_after, k):
            moved = back(value, 8 * k)
            if after == h:
                return moved
            return jnp.where(lane < LANES - 8 * k, moved, back(value_after, 8 * k))

        cross, partner = [], []
        for band in range(2):
            real = [zero] * SPAN
            imag = [zero] * SPAN
            for j in range(ML_RG):
                r = hb_ref[h, row_of(band, 0, j)]
                i = hb_ref[h, row_of(band, 1, j)]
                ra = hb_ref[after, row_of(band, 0, j)]
                ia = hb_ref[after, row_of(band, 1, j)]
                for k in range(SPAN):
                    pr = shifted(r, ra, k + 1)
                    pi = shifted(i, ia, k + 1)
                    real[k] = real[k] + (r * pr + i * pi)
                    imag[k] = imag[k] + (i * pr - r * pi)
            cross.append((group_sums(*real), group_sums(*imag)))
            partner.append(pick4(*[shifted(hpow[h][band], hpow[after][band], k) for k in range(1, SPAN + 1)]))
        weight, weighted = weigh(cross, hpow[h], partner, fh_ref[h])
        for which, value in enumerate((weight, weighted)):
            upto, onward, _ = cell_sums(value[None])
            e_ref[h, which, 0] = upto[0]
            e_ref[h, which, 1] = onward[0]

    for d in range(SPAN):
        x_ref[0, d] = zero
        x_ref[1, d] = zero
        x_ref[0, n + SPAN + d] = zero
        x_ref[1, n + SPAN + d] = zero
        for k in range(SPAN):
            s_ref[0, k, d] = zero
            s_ref[1, k, d] = zero

    def smooth(h, chain):
        dates = pl.ds(16 * h, 16)
        wide = iota((16, 8, LANES), 2)
        boxes = []
        for which in range(2):
            upto, onward, total = cell_sums(q_ref[which, dates])
            far_upto = [pltpu.roll(e_ref[h, which, 0], (lanes - 4 - 8 * t) % LANES, 1) for t in range(16)]
            far_onward = [pltpu.roll(e_ref[h, which, 1], (LANES - 4 - 8 * t) % LANES, 1) for t in range(16)]
            sooner = jnp.where(wide < 4, jnp.stack(far_onward), pltpu.roll(onward, 4, 2))
            later = jnp.where(wide >= lanes - 4, jnp.stack(far_upto), pltpu.roll(upto, LANES - 4, 2))
            boxes.append(total + sooner + later)
        phase = boxes[1] / (boxes[0] + floor_weight)
        weight = boxes[0] * (1.0 / (2 * RADIUS + 1))
        product = weight * phase
        own = pl.ds(16 * h + SPAN, 16)
        for k in range(SPAN):
            s_ref[0, k, own] = weight if k == 0 else pltpu.roll(weight, LANES - k, 2)
            s_ref[1, k, own] = product if k == 0 else pltpu.roll(product, LANES - k, 2)
        for t in range(16):
            x_ref[0, 16 * h + t + SPAN] = chain
            chain = chain + phase[t]
        total_weight = jnp.zeros((16, 8, LANES), jnp.float32)
        pull = ridge_weight * x_ref[0, own]
        for k in range(SPAN):
            low = pl.ds(16 * h + SPAN - 1 - k, 16)
            total_weight = total_weight + s_ref[0, k, own] + s_ref[0, k, low]
            pull = pull - s_ref[1, k, own] + s_ref[1, k, low]
        bt_ref[0, dates] = pull
        bt_ref[1, dates] = 1.0 / (total_weight + ridge_weight)
        out_ref[dates] = pltpu.roll(total_weight, 1, 2)
        return chain

    groups(smooth, zero)

    for sweep in range(ITERS):
        old, new = sweep % 2, (sweep + 1) % 2

        def relax(h, carry):
            total = bt_ref[0, pl.ds(16 * h, 16)]
            for k in range(SPAN):
                total = total + s_ref[0, k, pl.ds(16 * h + SPAN, 16)] * x_ref[old, pl.ds(16 * h + SPAN + 1 + k, 16)]
                below = pl.ds(16 * h + SPAN - 1 - k, 16)
                total = total + s_ref[0, k, below] * x_ref[old, below]
            value = total * bt_ref[1, pl.ds(16 * h, 16)]
            x_ref[new, pl.ds(16 * h + SPAN, 16)] = value
            if sweep == ITERS - 1:
                dates = pl.ds(16 * h, 16)
                out_ref[dates] = jnp.where(iota((16, 8, LANES), 2) % 4 == 1, out_ref[dates], value)
            return carry

        groups(relax, 0)


def spread_kernel(x_ref, far_flags_ref, far_taps_ref, out_ref, m_ref, held_ref, flags_ref, taps_ref, wide_ref, in_sems, side_sems):
    parts = in_sems.shape[1]
    looks = out_ref.shape[0] // parts
    width = x_ref.shape[3] // parts
    blocks = width // LANES
    pairs = blocks // 2
    reach = TAPS // 2
    sub = iota((8, LANES), 0)
    lane = iota((8, LANES), 1)
    zero = jnp.zeros((8, LANES), jnp.float32)

    def fetch(part, q):
        columns = pl.ds(q * width, width)
        return pltpu.make_async_copy(x_ref.at[0, part, :, columns], held_ref.at[part, :, columns], in_sems.at[part, q])

    get_flags = pltpu.make_async_copy(far_flags_ref, flags_ref, side_sems.at[0])
    get_taps = pltpu.make_async_copy(far_taps_ref, taps_ref, side_sems.at[1])
    get_taps.start()
    get_flags.start()
    for q in range(parts):
        for part in range(2):
            fetch(part, q).start()
    wide_ref[...] = jnp.zeros_like(wide_ref)
    get_taps.wait()
    for band in range(2):
        for part in range(2):
            wide_ref[2 * band + part, :, :TAPS] = taps_ref[band, part : part + 1, :].astype(jnp.float32)
    fill_filter(wide_ref, m_ref)
    get_flags.wait()
    flags = [flags_ref[0, k].astype(jnp.float32) for k in range(SPAN)]
    pattern = jnp.where(
        lane % 4 < 2, jnp.where(lane % 4 == 0, flags[0], flags[1]), jnp.where(lane % 4 == 2, flags[2], flags[3])
    )
    made = {}

    def half_of(part, block, half):
        if block < 0 or block >= parts * blocks:
            return zero
        start = block * LANES
        return held_ref[part, :, start : start + LANES].astype(jnp.float32)[8 * half : 8 * half + 8]

    def pair_of(part, index, half):
        if (part, index, half) not in made:
            first = half_of(part, 2 * index - 1, half)
            second = half_of(part, 2 * index, half)
            mixed = pltpu.roll(jnp.where(sub < 4, second, first), 4, 0)
            made[part, index, half] = (jnp.where(sub < 4, first, mixed), jnp.where(sub < 4, mixed, second))
        return made[part, index, half]

    def beyond(q, half, odd):
        after, before = [], []
        for part in range(2):
            value = half_of(part, blocks * (q + 1) + 1, half)
            after.append(pltpu.roll(value, 4, 0) if odd else value)
            value = half_of(part, blocks * q - 2, half)
            before.append(value if odd else pltpu.roll(value, 4, 0))
        side = lane // SPAN % 2
        inside = jnp.where(side == 0, float(q < parts - 1), float(q > 0))
        top = jnp.where(lane < reach, after[0], jnp.where(lane < 2 * reach, pltpu.roll(after[1], reach, 1), pattern))
        bottom = jnp.where(lane >= LANES - reach, before[0], pattern * inside)
        bottom = jnp.where(lane < reach, pltpu.roll(before[1], reach, 1), bottom)
        return jnp.where(sub < 4, top, bottom)

    for q in range(parts):
        for part in range(2):
            if q == 0:
                fetch(part, 0).wait()
            if q + 1 < parts:
                fetch(part, q + 1).wait()
        for half in range(looks // 2):
            for odd in range(2):
                chunk = q * looks + 2 * half + odd
                rows = [pair_of(part, q * pairs + i, half)[odd] for part in range(2) for i in range(pairs + 1)]
                for i in range(0, len(rows), 2):
                    both = jnp.concatenate(rows[i : i + 2], axis=0)
                    out_ref[chunk, 8 * i : 8 * i + 16, :] = both.astype(jnp.bfloat16)
                out_ref[chunk, 8 * len(rows) : 8 * len(rows) + 8, :] = beyond(q, half, odd).astype(jnp.bfloat16)


def gather_kernel(z_ref, phase_ref, weight_ref):
    count = z_ref.shape[0]
    looks = phase_ref.shape[1]
    width = 2 * LANES
    source = iota((3 * LANES, 2 * width), 0) % LANES
    column = iota((3 * LANES, 2 * width), 1)
    block = column % width // CELLS
    chosen = jnp.where(source == SPAN * block + column // width, 1.0, 0.0).astype(jnp.bfloat16)
    rest = z_ref[...].reshape(count * CELLS, LANES)
    pieces = []
    for _ in range(3):
        pieces.append(rest.astype(jnp.bfloat16))
        rest = rest - pieces[-1].astype(jnp.float32)
    moved = jnp.dot(jnp.concatenate(pieces, axis=1), chosen, preferred_element_type=jnp.float32)
    moved = moved.reshape(count, CELLS, 2 * width)
    lines = jnp.where(iota(moved.shape, 1) == iota(moved.shape, 2) % CELLS, moved, 0.0).sum(axis=1)
    for q in range(count // looks):
        for which, out in enumerate((phase_ref, weight_ref)):
            out[0, :, width * q : width * (q + 1)] = lines[
                looks * q : looks * (q + 1), width * which : width * (which + 1)
            ]


def local(slc_stack, band_taps, pair_flags):
    n = lax.axis_size("date")
    looks = slc_stack.shape[2] // ML_AZ
    parts = n // looks
    lanes = slc_stack.shape[3] // (parts * LANES) * ML_AZ
    rows = 2 * (lanes + 2 * ML_AZ) + 8
    halos = n * 8 // LANES
    tile = (8, LANES)
    in_vmem = pl.BlockSpec(memory_space=pltpu.VMEM)
    anywhere = pl.BlockSpec(memory_space=pl.ANY)
    params = pltpu.CompilerParams(vmem_limit_bytes=60 * 1024 * 1024)
    chunks, matrix = pl.pallas_call(
        spread_kernel,
        out_shape=[
            pltpu.VMEM((n, rows, LANES), jnp.bfloat16),
            pltpu.VMEM((4 * LANES, 4 * LANES), jnp.bfloat16),
        ],
        in_specs=[anywhere] * 3,
        out_specs=[in_vmem] * 2,
        scratch_shapes=[
            pltpu.VMEM(slc_stack.shape[1:], jnp.bfloat16),
            pltpu.SMEM(pair_flags.shape, jnp.int32),
            pltpu.VMEM(band_taps.shape, jnp.bfloat16),
            pltpu.VMEM((4, 1, 2 * LANES), jnp.float32),
            pltpu.SemaphoreType.DMA((2, parts)),
            pltpu.SemaphoreType.DMA((2,)),
        ],
        compiler_params=params,
    )(slc_stack, pair_flags, band_taps)
    y = pltpu.with_memory_space_constraint(lax.all_to_all(chunks, "date", 0, 0, tiled=True), pltpu.VMEM)
    matrix = pltpu.with_memory_space_constraint(matrix, pltpu.VMEM)
    solved = pl.pallas_call(
        solve_kernel,
        out_shape=pltpu.VMEM((n, *tile), jnp.float32),
        in_specs=[in_vmem, in_vmem],
        out_specs=in_vmem,
        scratch_shapes=[
            pltpu.VMEM((n, 4 * LANES, LANES), jnp.float32),
            pltpu.VMEM((n, 8, 4 * LANES), jnp.float32),
            pltpu.VMEM((halos, 4 * LANES, LANES), jnp.float32),
            pltpu.VMEM((n, 2, *tile), jnp.float32),
            pltpu.VMEM((n, *tile), jnp.float32),
            pltpu.VMEM((halos, *tile), jnp.float32),
            pltpu.VMEM((6, n, *tile), jnp.float32),
            pltpu.VMEM((halos, 2, 2, *tile), jnp.float32),
            pltpu.VMEM((2, n, *tile), jnp.float32),
            pltpu.VMEM((2, SPAN, n + SPAN, *tile), jnp.float32),
            pltpu.VMEM((2, n, *tile), jnp.float32),
            pltpu.VMEM((2, n + 2 * SPAN, *tile), jnp.float32),
        ],
        compiler_params=params,
    )(matrix, y)
    z = lax.all_to_all(solved, "date", 0, 0, tiled=True)
    shape = (1, looks, slc_stack.shape[3] // ML_RG)
    if lanes == LANES:
        return tuple(
            pl.pallas_call(
                gather_kernel,
                out_shape=[jax.ShapeDtypeStruct(shape, jnp.float32)] * 2,
                in_specs=[in_vmem],
                out_specs=[in_vmem] * 2,
                compiler_params=params,
            )(pltpu.with_memory_space_constraint(z, pltpu.VMEM))
        )
    z = z[:, :, :lanes].reshape(parts, looks, CELLS, lanes // SPAN, SPAN)[..., :2]
    z = z.transpose(4, 1, 0, 3, 2).reshape(2, *shape)
    return (z[0], z[1])


def solution(mesh):
    in_specs = (P("date", None, "group", None), P(), P("date", None))
    out_specs = (P("date", "group", None), P("date", "group", None))
    return jax.shard_map(local, mesh=mesh, in_specs=in_specs, out_specs=out_specs, check_vma=False)
```

```python
import jax
import jax.numpy as jnp
from jax import lax
from jax.experimental import pallas as pl
from jax.experimental.pallas import tpu as pltpu
from jax.sharding import PartitionSpec as P

TAPS = 32
ML_AZ = 4
ML_RG = 16
SPAN = 4
RADIUS = 8
ITERS = 4
LANES = 128
CELLS = LANES // ML_RG

eps_power = 1e-06
floor_weight = 0.1
ridge_weight = 0.05
split_coef = 2.0


def iota(shape, axis):
    return lax.broadcasted_iota(jnp.int32, shape, axis)


def back(x, steps):
    return pltpu.roll(x, LANES - steps, 1)


def group_sums(x0, x1, x2, x3):
    lane = iota((8, LANES), 1)
    even = lane % 2 == 0
    low = lane % 4 < 2
    u = jnp.where(even, x0 + back(x0, 1), x1 + pltpu.roll(x1, 1, 1))
    v = jnp.where(even, x2 + back(x2, 1), x3 + pltpu.roll(x3, 1, 1))
    return jnp.where(low, u + back(u, 2), v + pltpu.roll(v, 2, 1))


def pick4(x0, x1, x2, x3):
    lane = iota((8, LANES), 1) % 4
    return jnp.where(lane < 2, jnp.where(lane == 0, x0, x1), jnp.where(lane == 2, x2, x3))


def fill_filter(taps_ref, m_ref):
    width = 2 * LANES
    sub = iota((CELLS, width), 0)

    def placed(row):
        taps = jnp.broadcast_to(taps_ref[row], (CELLS, width))
        result = jnp.zeros((CELLS, width), jnp.float32)
        for c in range(CELLS):
            result = jnp.where(sub == c, pltpu.roll(taps, (ML_RG * c - TAPS // 2) % width, 1), result)
        return result

    def along(base, j):
        both = [base if jj == 0 else pltpu.roll(base, jj, 1) for jj in (j, j + 1)]
        return jnp.concatenate(both, axis=0)

    for band in range(2):
        real, imag = placed(2 * band), placed(2 * band + 1)
        for j in range(0, ML_RG, 2):
            tr, ti = along(real, j), along(imag, j)
            real_row = ((band * 2 + 0) * ML_RG + j) * CELLS
            imag_row = ((band * 2 + 1) * ML_RG + j) * CELLS
            m_ref[real_row : real_row + 16, :width] = tr.astype(jnp.bfloat16)
            m_ref[real_row : real_row + 16, width:] = (-ti).astype(jnp.bfloat16)
            m_ref[imag_row : imag_row + 16, :width] = ti.astype(jnp.bfloat16)
            m_ref[imag_row : imag_row + 16, width:] = tr.astype(jnp.bfloat16)


def row_of(band, part, j):
    start = ((band * 2 + part) * ML_RG + j) * CELLS
    return slice(start, start + CELLS)


def apply_filter(matrix, windows):
    bands = lax.dot_general(
        matrix, windows, (((1,), (1,)), ((), ())), preferred_element_type=jnp.float32
    )
    return bands.astype(jnp.bfloat16).astype(jnp.float32)


def power_of(b_ref, d, band):
    total = jnp.zeros((CELLS, LANES), jnp.float32)
    for j in range(ML_RG):
        r = b_ref[d, row_of(band, 0, j)]
        i = b_ref[d, row_of(band, 1, j)]
        total = total + (r * r + i * i)
    return group_sums(total, total, total, total)


def weigh(cross, own, partner, flags):
    (re0, im0), (re1, im1) = cross
    pow0 = own[0] * partner[0] + eps_power
    pow1 = own[1] * partner[1] + eps_power
    coherence = (re0 * re0 + im0 * im0) / pow0 + (re1 * re1 + im1 * im1) / pow1
    weight = flags * 0.5 * coherence
    raw = split_coef * (im0 * re1 - re0 * im1) / jnp.sqrt(pow0 * pow1)
    return weight, weight * raw


def cell_sums(x):
    sub = iota(x.shape, 1)
    upto = x
    for step in (1, 2, 4):
        upto = upto + jnp.where(sub >= step, pltpu.roll(upto, step, 1), 0.0)
    total = jnp.broadcast_to(upto[:, CELLS - 1 : CELLS], x.shape)
    return upto, total - upto + x, total


def solve_kernel(
    m_ref, y_ref, out_ref, b_ref, u_ref, wh_ref, hb_ref, pw_ref, fl_ref, fh_ref, c_ref, e_ref, q_ref, s_ref, bt_ref, x_ref
):
    n, rows, _ = y_ref.shape
    tiles = rows // 16
    lanes = 8 * (tiles - 1)
    halos = hb_ref.shape[0]
    kept = u_ref.shape[0] == n
    lane = iota((8, LANES), 1)
    sub = iota((8, LANES), 0)
    zero = jnp.zeros((8, LANES), jnp.float32)

    def each(step, start):
        return lax.fori_loop(0, n, step, start, unroll=n <= 16)

    def groups(step, start):
        return lax.fori_loop(0, n // 16, step, start, unroll=n <= 16)

    def windows_of(d):
        windows, edges = [], []
        held = y_ref[d].astype(jnp.float32).reshape(rows // 8, 8, LANES)
        beyond = held[rows // 8 - 1]
        main = beyond[0:1]
        main = jnp.where(lane[:1] < LANES // 2, pltpu.roll(main, LANES // 2, 1), main)
        fl_ref[d] = jnp.broadcast_to(main, (8, LANES))
        side = beyond[4:5]
        middle = (lane[:1] >= LANES // 4) & (lane[:1] < 3 * LANES // 4)
        side = jnp.where(middle, side, pltpu.roll(side, LANES // 2, 1))
        fh_ref[d // 16] = jnp.where(lane // 8 == d % 16, jnp.broadcast_to(side, (8, LANES)), fh_ref[d // 16])
        for part in range(2):
            v = held[part * tiles : (part + 1) * tiles]
            subs = iota((tiles - 1, 8, LANES), 1)
            wide = iota((tiles - 1, 8, LANES), 2)
            main = pltpu.roll(jnp.where(subs < 4, v[1:], v[:-1]), 4, 1)
            edge = jnp.where(wide < LANES // 2, v[1:], v[:-1])
            windows.append(main.reshape(lanes, LANES))
            windows.append(edge.reshape(lanes, LANES))
            first, last = v[0], v[tiles - 1]
            far = beyond if part == 0 else pltpu.roll(beyond, LANES - TAPS // 2, 1)
            edges.append(pltpu.roll(jnp.where(sub < 4, first, last), 4, 0))
            later = jnp.where(sub < 4, far, first)
            sooner = jnp.where(sub < 4, last, far)
            edges.append(jnp.where(lane < LANES // 2, later, sooner))
        windows = jnp.concatenate(windows, axis=1)
        if lanes < LANES:
            windows = jnp.concatenate([windows, jnp.zeros((LANES - lanes, 4 * LANES), jnp.float32)], axis=0)
        wh_ref[d] = jnp.concatenate(edges, axis=1)
        return windows.astype(jnp.bfloat16)

    def filtered(pair, carry):
        dates = (2 * pair, 2 * pair + 1)
        bands = apply_filter(m_ref[...], jnp.concatenate([windows_of(d) for d in dates], axis=0))
        for t, d in enumerate(dates):
            own = bands[:, LANES * t : LANES * (t + 1)]
            b_ref[d] = own
            for band in range(2 if kept else 0):
                real = own[2 * band * LANES : (2 * band + 1) * LANES]
                imag = own[(2 * band + 1) * LANES : (2 * band + 2) * LANES]
                u_ref[d, 2 * band * LANES : (2 * band + 1) * LANES] = real + imag
                u_ref[d, (2 * band + 1) * LANES : (2 * band + 2) * LANES] = real - imag
            for band in range(2):
                pw_ref[d, band] = power_of(b_ref, d, band)
        return carry

    lax.fori_loop(0, n // 2, filtered, 0, unroll=n <= 16)

    for h in range(halos):
        hb_ref[h] = apply_filter(m_ref[...], wh_ref[16 * h : 16 * h + 16].reshape(LANES, 4 * LANES).astype(jnp.bfloat16))

    def mixed(d, band, j, which):
        if kept:
            return u_ref[d, row_of(band, which, j)]
        real, imag = b_ref[d, row_of(band, 0, j)], b_ref[d, row_of(band, 1, j)]
        return real - imag if which else real + imag

    def pairs(d, carry):
        later = [jnp.minimum(d + k, n - 1) for k in range(1, SPAN + 1)]
        for band in range(2):
            shared = [zero] * SPAN
            plus = [zero] * SPAN
            minus = [zero] * SPAN
            for j in range(ML_RG):
                r = b_ref[d, row_of(band, 0, j)]
                i = b_ref[d, row_of(band, 1, j)]
                both = mixed(d, band, j, 0)
                for k in range(SPAN):
                    shared[k] = shared[k] + both * b_ref[later[k], row_of(band, 0, j)]
                    plus[k] = plus[k] + r * mixed(later[k], band, j, 0)
                    minus[k] = minus[k] + i * mixed(later[k], band, j, 1)
            c_ref[2 * band, d] = group_sums(*[a - b for a, b in zip(shared, minus)])
            c_ref[2 * band + 1, d] = group_sums(*[a - b for a, b in zip(shared, plus)])
            c_ref[4 + band, d] = pick4(*[pw_ref[e, band] for e in later])
        return carry

    each(pairs, 0)

    def weights(h, carry):
        dates = pl.ds(16 * h, 16)
        cross = [(c_ref[2 * band, dates], c_ref[2 * band + 1, dates]) for band in range(2)]
        own = [pw_ref[dates, band] for band in range(2)]
        partner = [c_ref[4 + band, dates] for band in range(2)]
        q_ref[0, dates], q_ref[1, dates] = weigh(cross, own, partner, fl_ref[dates])
        return carry

    groups(weights, 0)

    hpow = [[power_of(hb_ref, h, band) for band in range(2)] for h in range(halos)]
    for h in range(halos):
        after = min(h + 1, halos - 1)

        def shifted(value, value_after, k):
            moved = back(value, 8 * k)
            if after == h:
                return moved
            return jnp.where(lane < LANES - 8 * k, moved, back(value_after, 8 * k))

        cross, partner = [], []
        for band in range(2):
            real = [zero] * SPAN
            imag = [zero] * SPAN
            for j in range(ML_RG):
                r = hb_ref[h, row_of(band, 0, j)]
                i = hb_ref[h, row_of(band, 1, j)]
                ra = hb_ref[after, row_of(band, 0, j)]
                ia = hb_ref[after, row_of(band, 1, j)]
                for k in range(SPAN):
                    pr = shifted(r, ra, k + 1)
                    pi = shifted(i, ia, k + 1)
                    real[k] = real[k] + (r * pr + i * pi)
                    imag[k] = imag[k] + (i * pr - r * pi)
            cross.append((group_sums(*real), group_sums(*imag)))
            partner.append(pick4(*[shifted(hpow[h][band], hpow[after][band], k) for k in range(1, SPAN + 1)]))
        weight, weighted = weigh(cross, hpow[h], partner, fh_ref[h])
        for which, value in enumerate((weight, weighted)):
            upto, onward, _ = cell_sums(value[None])
            e_ref[h, which, 0] = upto[0]
            e_ref[h, which, 1] = onward[0]

    for d in range(SPAN):
        x_ref[0, d] = zero
        x_ref[1, d] = zero
        x_ref[0, n + SPAN + d] = zero
        x_ref[1, n + SPAN + d] = zero
        for k in range(SPAN):
            s_ref[0, k, d] = zero
            s_ref[1, k, d] = zero

    def smooth(h, chain):
        dates = pl.ds(16 * h, 16)
        wide = iota((16, 8, LANES), 2)
        boxes = []
        for which in range(2):
            upto, onward, total = cell_sums(q_ref[which, dates])
            far_upto = [pltpu.roll(e_ref[h, which, 0], (lanes - 4 - 8 * t) % LANES, 1) for t in range(16)]
            far_onward = [pltpu.roll(e_ref[h, which, 1], (LANES - 4 - 8 * t) % LANES, 1) for t in range(16)]
            sooner = jnp.where(wide < 4, jnp.stack(far_onward), pltpu.roll(onward, 4, 2))
            later = jnp.where(wide >= lanes - 4, jnp.stack(far_upto), pltpu.roll(upto, LANES - 4, 2))
            boxes.append(total + sooner + later)
        phase = boxes[1] / (boxes[0] + floor_weight)
        weight = boxes[0] * (1.0 / (2 * RADIUS + 1))
        product = weight * phase
        own = pl.ds(16 * h + SPAN, 16)
        for k in range(SPAN):
            s_ref[0, k, own] = weight if k == 0 else pltpu.roll(weight, LANES - k, 2)
            s_ref[1, k, own] = product if k == 0 else pltpu.roll(product, LANES - k, 2)
        for t in range(16):
            x_ref[0, 16 * h + t + SPAN] = chain
            chain = chain + phase[t]
        total_weight = jnp.zeros((16, 8, LANES), jnp.float32)
        pull = ridge_weight * x_ref[0, own]
        for k in range(SPAN):
            low = pl.ds(16 * h + SPAN - 1 - k, 16)
            total_weight = total_weight + s_ref[0, k, own] + s_ref[0, k, low]
            pull = pull - s_ref[1, k, own] + s_ref[1, k, low]
        bt_ref[0, dates] = pull
        bt_ref[1, dates] = 1.0 / (total_weight + ridge_weight)
        out_ref[dates] = pltpu.roll(total_weight, 1, 2)
        return chain

    groups(smooth, zero)

    for sweep in range(ITERS):
        old, new = sweep % 2, (sweep + 1) % 2

        def relax(h, carry):
            total = bt_ref[0, pl.ds(16 * h, 16)]
            for k in range(SPAN):
                total = total + s_ref[0, k, pl.ds(16 * h + SPAN, 16)] * x_ref[old, pl.ds(16 * h + SPAN + 1 + k, 16)]
                below = pl.ds(16 * h + SPAN - 1 - k, 16)
                total = total + s_ref[0, k, below] * x_ref[old, below]
            value = total * bt_ref[1, pl.ds(16 * h, 16)]
            x_ref[new, pl.ds(16 * h + SPAN, 16)] = value
            if sweep == ITERS - 1:
                dates = pl.ds(16 * h, 16)
                out_ref[dates] = jnp.where(iota((16, 8, LANES), 2) % 4 == 1, out_ref[dates], value)
            return carry

        groups(relax, 0)


def spread_kernel(x_ref, far_flags_ref, far_taps_ref, out_ref, m_ref, held_ref, flags_ref, taps_ref, wide_ref, in_sems, side_sems):
    parts = in_sems.shape[1]
    looks = out_ref.shape[0] // parts
    width = x_ref.shape[3] // parts
    blocks = width // LANES
    pairs = blocks // 2
    reach = TAPS // 2
    sub = iota((8, LANES), 0)
    lane = iota((8, LANES), 1)
    zero = jnp.zeros((8, LANES), jnp.float32)

    def fetch(part, q):
        columns = pl.ds(q * width, width)
        return pltpu.make_async_copy(x_ref.at[0, part, :, columns], held_ref.at[part, :, columns], in_sems.at[part, q])

    get_flags = pltpu.make_async_copy(far_flags_ref, flags_ref, side_sems.at[0])
    get_taps = pltpu.make_async_copy(far_taps_ref, taps_ref, side_sems.at[1])
    get_taps.start()
    get_flags.start()
    for q in range(parts):
        for part in range(2):
            fetch(part, q).start()
    wide_ref[...] = jnp.zeros_like(wide_ref)
    get_taps.wait()
    for band in range(2):
        for part in range(2):
            wide_ref[2 * band + part, :, :TAPS] = taps_ref[band, part : part + 1, :].astype(jnp.float32)
    fill_filter(wide_ref, m_ref)
    get_flags.wait()
    flags = [flags_ref[0, k].astype(jnp.float32) for k in range(SPAN)]
    pattern = jnp.where(
        lane % 4 < 2, jnp.where(lane % 4 == 0, flags[0], flags[1]), jnp.where(lane % 4 == 2, flags[2], flags[3])
    )
    made = {}

    def half_of(part, block, half):
        if block < 0 or block >= parts * blocks:
            return zero
        start = block * LANES
        return held_ref[part, :, start : start + LANES].astype(jnp.float32)[8 * half : 8 * half + 8]

    def pair_of(part, index, half):
        if (part, index, half) not in made:
            first = half_of(part, 2 * index - 1, half)
            second = half_of(part, 2 * index, half)
            mixed = pltpu.roll(jnp.where(sub < 4, second, first), 4, 0)
            made[part, index, half] = (jnp.where(sub < 4, first, mixed), jnp.where(sub < 4, mixed, second))
        return made[part, index, half]

    def beyond(q, half, odd):
        after, before = [], []
        for part in range(2):
            value = half_of(part, blocks * (q + 1) + 1, half)
            after.append(pltpu.roll(value, 4, 0) if odd else value)
            value = half_of(part, blocks * q - 2, half)
            before.append(value if odd else pltpu.roll(value, 4, 0))
        side = lane // SPAN % 2
        inside = jnp.where(side == 0, float(q < parts - 1), float(q > 0))
        top = jnp.where(lane < reach, after[0], jnp.where(lane < 2 * reach, pltpu.roll(after[1], reach, 1), pattern))
        bottom = jnp.where(lane >= LANES - reach, before[0], pattern * inside)
        bottom = jnp.where(lane < reach, pltpu.roll(before[1], reach, 1), bottom)
        return jnp.where(sub < 4, top, bottom)

    for q in range(parts):
        for part in range(2):
            if q == 0:
                fetch(part, 0).wait()
            if q + 1 < parts:
                fetch(part, q + 1).wait()
        for half in range(looks // 2):
            for odd in range(2):
                chunk = q * looks + 2 * half + odd
                rows = [pair_of(part, q * pairs + i, half)[odd] for part in range(2) for i in range(pairs + 1)]
                for i in range(0, len(rows), 2):
                    both = jnp.concatenate(rows[i : i + 2], axis=0)
                    out_ref[chunk, 8 * i : 8 * i + 16, :] = both.astype(jnp.bfloat16)
                out_ref[chunk, 8 * len(rows) : 8 * len(rows) + 8, :] = beyond(q, half, odd).astype(jnp.bfloat16)


def gather_kernel(z_ref, phase_ref, weight_ref):
    count = z_ref.shape[0]
    looks = phase_ref.shape[1]
    width = 2 * LANES
    source = iota((3 * LANES, 2 * width), 0) % LANES
    column = iota((3 * LANES, 2 * width), 1)
    block = column % width // CELLS
    chosen = jnp.where(source == SPAN * block + column // width, 1.0, 0.0).astype(jnp.bfloat16)
    rest = z_ref[...].reshape(count * CELLS, LANES)
    pieces = []
    for _ in range(3):
        pieces.append(rest.astype(jnp.bfloat16))
        rest = rest - pieces[-1].astype(jnp.float32)
    moved = jnp.dot(jnp.concatenate(pieces, axis=1), chosen, preferred_element_type=jnp.float32)
    moved = moved.reshape(count, CELLS, 2 * width)
    lines = jnp.where(iota(moved.shape, 1) == iota(moved.shape, 2) % CELLS, moved, 0.0).sum(axis=1)
    for q in range(count // looks):
        for which, out in enumerate((phase_ref, weight_ref)):
            out[0, :, width * q : width * (q + 1)] = lines[
                looks * q : looks * (q + 1), width * which : width * (which + 1)
            ]


def local(slc_stack, band_taps, pair_flags):
    n = lax.axis_size("date")
    looks = slc_stack.shape[2] // ML_AZ
    parts = n // looks
    lanes = slc_stack.shape[3] // (parts * LANES) * ML_AZ
    rows = 2 * (lanes + 2 * ML_AZ) + 8
    halos = n * 8 // LANES
    tile = (8, LANES)
    in_vmem = pl.BlockSpec(memory_space=pltpu.VMEM)
    anywhere = pl.BlockSpec(memory_space=pl.ANY)
    params = pltpu.CompilerParams(vmem_limit_bytes=60 * 1024 * 1024)
    chunks, matrix = pl.pallas_call(
        spread_kernel,
        out_shape=[
            pltpu.VMEM((n, rows, LANES), jnp.bfloat16),
            pltpu.VMEM((4 * LANES, 4 * LANES), jnp.bfloat16),
        ],
        in_specs=[anywhere] * 3,
        out_specs=[in_vmem] * 2,
        scratch_shapes=[
            pltpu.VMEM(slc_stack.shape[1:], jnp.bfloat16),
            pltpu.SMEM(pair_flags.shape, jnp.int32),
            pltpu.VMEM(band_taps.shape, jnp.bfloat16),
            pltpu.VMEM((4, 1, 2 * LANES), jnp.float32),
            pltpu.SemaphoreType.DMA((2, parts)),
            pltpu.SemaphoreType.DMA((2,)),
        ],
        compiler_params=params,
    )(slc_stack, pair_flags, band_taps)
    y = pltpu.with_memory_space_constraint(lax.all_to_all(chunks, "date", 0, 0, tiled=True), pltpu.VMEM)
    matrix = pltpu.with_memory_space_constraint(matrix, pltpu.VMEM)
    solved = pl.pallas_call(
        solve_kernel,
        out_shape=pltpu.VMEM((n, *tile), jnp.float32),
        in_specs=[in_vmem, in_vmem],
        out_specs=in_vmem,
        scratch_shapes=[
            pltpu.VMEM((n, 4 * LANES, LANES), jnp.float32),
            pltpu.VMEM((n if n <= 32 else 1, 4 * LANES, LANES), jnp.float32),
            pltpu.VMEM((n, 8, 4 * LANES), jnp.float32),
            pltpu.VMEM((halos, 4 * LANES, LANES), jnp.float32),
            pltpu.VMEM((n, 2, *tile), jnp.float32),
            pltpu.VMEM((n, *tile), jnp.float32),
            pltpu.VMEM((halos, *tile), jnp.float32),
            pltpu.VMEM((6, n, *tile), jnp.float32),
            pltpu.VMEM((halos, 2, 2, *tile), jnp.float32),
            pltpu.VMEM((2, n, *tile), jnp.float32),
            pltpu.VMEM((2, SPAN, n + SPAN, *tile), jnp.float32),
            pltpu.VMEM((2, n, *tile), jnp.float32),
            pltpu.VMEM((2, n + 2 * SPAN, *tile), jnp.float32),
        ],
        compiler_params=params,
    )(matrix, y)
    z = lax.all_to_all(solved, "date", 0, 0, tiled=True)
    shape = (1, looks, slc_stack.shape[3] // ML_RG)
    if lanes == LANES:
        return tuple(
            pl.pallas_call(
                gather_kernel,
                out_shape=[jax.ShapeDtypeStruct(shape, jnp.float32)] * 2,
                in_specs=[in_vmem],
                out_specs=[in_vmem] * 2,
                compiler_params=params,
            )(pltpu.with_memory_space_constraint(z, pltpu.VMEM))
        )
    z = z[:, :, :lanes].reshape(parts, looks, CELLS, lanes // SPAN, SPAN)[..., :2]
    z = z.transpose(4, 1, 0, 3, 2).reshape(2, *shape)
    return (z[0], z[1])


def solution(mesh):
    in_specs = (P("date", None, "group", None), P(), P("date", None))
    out_specs = (P("date", "group", None), P("date", "group", None))
    return jax.shard_map(local, mesh=mesh, in_specs=in_specs, out_specs=out_specs, check_vma=False)
```

```python
import jax
import jax.numpy as jnp
from jax import lax
from jax.experimental import pallas as pl
from jax.experimental.pallas import tpu as pltpu
from jax.sharding import PartitionSpec as P

TAPS = 32
ML_AZ = 4
ML_RG = 16
SPAN = 4
RADIUS = 8
ITERS = 4
LANES = 128
CELLS = LANES // ML_RG

eps_power = 1e-06
floor_weight = 0.1
ridge_weight = 0.05
split_coef = 2.0


def iota(shape, axis):
    return lax.broadcasted_iota(jnp.int32, shape, axis)


def back(x, steps):
    return pltpu.roll(x, LANES - steps, 1)


def group_sums(x0, x1, x2, x3):
    lane = iota((8, LANES), 1)
    even = lane % 2 == 0
    low = lane % 4 < 2
    u = jnp.where(even, x0 + back(x0, 1), x1 + pltpu.roll(x1, 1, 1))
    v = jnp.where(even, x2 + back(x2, 1), x3 + pltpu.roll(x3, 1, 1))
    return jnp.where(low, u + back(u, 2), v + pltpu.roll(v, 2, 1))


def pick4(x0, x1, x2, x3):
    lane = iota((8, LANES), 1) % 4
    return jnp.where(lane < 2, jnp.where(lane == 0, x0, x1), jnp.where(lane == 2, x2, x3))


def fill_filter(taps_ref, m_ref):
    width = 2 * LANES
    sub = iota((CELLS, width), 0)

    def placed(row):
        taps = jnp.broadcast_to(taps_ref[row], (CELLS, width))
        result = jnp.zeros((CELLS, width), jnp.float32)
        for c in range(CELLS):
            result = jnp.where(sub == c, pltpu.roll(taps, (ML_RG * c - TAPS // 2) % width, 1), result)
        return result

    def along(base, j):
        both = [base if jj == 0 else pltpu.roll(base, jj, 1) for jj in (j, j + 1)]
        return jnp.concatenate(both, axis=0)

    for band in range(2):
        real, imag = placed(2 * band), placed(2 * band + 1)
        for j in range(0, ML_RG, 2):
            tr, ti = along(real, j), along(imag, j)
            real_row = ((band * 2 + 0) * ML_RG + j) * CELLS
            imag_row = ((band * 2 + 1) * ML_RG + j) * CELLS
            m_ref[real_row : real_row + 16, :width] = tr.astype(jnp.bfloat16)
            m_ref[real_row : real_row + 16, width:] = (-ti).astype(jnp.bfloat16)
            m_ref[imag_row : imag_row + 16, :width] = ti.astype(jnp.bfloat16)
            m_ref[imag_row : imag_row + 16, width:] = tr.astype(jnp.bfloat16)


def row_of(band, part, j):
    start = ((band * 2 + part) * ML_RG + j) * CELLS
    return slice(start, start + CELLS)


def apply_filter(matrix, windows):
    bands = lax.dot_general(
        matrix, windows, (((1,), (1,)), ((), ())), preferred_element_type=jnp.float32
    )
    return bands.astype(jnp.bfloat16).astype(jnp.float32)


def power_of(b_ref, d, band):
    total = jnp.zeros((CELLS, LANES), jnp.float32)
    for j in range(ML_RG):
        r = b_ref[d, row_of(band, 0, j)]
        i = b_ref[d, row_of(band, 1, j)]
        total = total + (r * r + i * i)
    return group_sums(total, total, total, total)


def weigh(cross, own, partner, flags):
    (re0, im0), (re1, im1) = cross
    pow0 = own[0] * partner[0] + eps_power
    pow1 = own[1] * partner[1] + eps_power
    coherence = (re0 * re0 + im0 * im0) / pow0 + (re1 * re1 + im1 * im1) / pow1
    weight = flags * 0.5 * coherence
    raw = split_coef * (im0 * re1 - re0 * im1) / jnp.sqrt(pow0 * pow1)
    return weight, weight * raw


def cell_sums(x):
    sub = iota(x.shape, 1)
    upto = x
    for step in (1, 2, 4):
        upto = upto + jnp.where(sub >= step, pltpu.roll(upto, step, 1), 0.0)
    total = jnp.broadcast_to(upto[:, CELLS - 1 : CELLS], x.shape)
    return upto, total - upto + x, total


def solve_kernel(
    m_ref, y_ref, out_ref, b_ref, u_ref, wh_ref, hb_ref, pw_ref, fl_ref, fh_ref, c_ref, e_ref, q_ref, s_ref, bt_ref, x_ref
):
    n, rows, _ = y_ref.shape
    tiles = rows // 16
    lanes = 8 * (tiles - 1)
    halos = hb_ref.shape[0]
    kept = u_ref.shape[0] == n
    lane = iota((8, LANES), 1)
    sub = iota((8, LANES), 0)
    zero = jnp.zeros((8, LANES), jnp.float32)

    def groups(step, start):
        return lax.fori_loop(0, n // 16, step, start, unroll=n <= 16)

    def windows_of(d):
        windows, edges = [], []
        held = y_ref[d].astype(jnp.float32).reshape(rows // 8, 8, LANES)
        beyond = held[rows // 8 - 1]
        main = beyond[0:1]
        main = jnp.where(lane[:1] < LANES // 2, pltpu.roll(main, LANES // 2, 1), main)
        fl_ref[d] = jnp.broadcast_to(main, (8, LANES))
        side = beyond[4:5]
        middle = (lane[:1] >= LANES // 4) & (lane[:1] < 3 * LANES // 4)
        side = jnp.where(middle, side, pltpu.roll(side, LANES // 2, 1))
        fh_ref[d // 16] = jnp.where(lane // 8 == d % 16, jnp.broadcast_to(side, (8, LANES)), fh_ref[d // 16])
        for part in range(2):
            v = held[part * tiles : (part + 1) * tiles]
            subs = iota((tiles - 1, 8, LANES), 1)
            wide = iota((tiles - 1, 8, LANES), 2)
            main = pltpu.roll(jnp.where(subs < 4, v[1:], v[:-1]), 4, 1)
            edge = jnp.where(wide < LANES // 2, v[1:], v[:-1])
            windows.append(main.reshape(lanes, LANES))
            windows.append(edge.reshape(lanes, LANES))
            first, last = v[0], v[tiles - 1]
            far = beyond if part == 0 else pltpu.roll(beyond, LANES - TAPS // 2, 1)
            edges.append(pltpu.roll(jnp.where(sub < 4, first, last), 4, 0))
            later = jnp.where(sub < 4, far, first)
            sooner = jnp.where(sub < 4, last, far)
            edges.append(jnp.where(lane < LANES // 2, later, sooner))
        windows = jnp.concatenate(windows, axis=1)
        if lanes < LANES:
            windows = jnp.concatenate([windows, jnp.zeros((LANES - lanes, 4 * LANES), jnp.float32)], axis=0)
        wh_ref[d] = jnp.concatenate(edges, axis=1)
        return windows.astype(jnp.bfloat16)

    def filtered(pair, carry):
        dates = (2 * pair, 2 * pair + 1)
        bands = apply_filter(m_ref[...], jnp.concatenate([windows_of(d) for d in dates], axis=0))
        for t, d in enumerate(dates):
            own = bands[:, LANES * t : LANES * (t + 1)]
            b_ref[d] = own
            for band in range(2 if kept else 0):
                real = own[2 * band * LANES : (2 * band + 1) * LANES]
                imag = own[(2 * band + 1) * LANES : (2 * band + 2) * LANES]
                u_ref[d, 2 * band * LANES : (2 * band + 1) * LANES] = real + imag
                u_ref[d, (2 * band + 1) * LANES : (2 * band + 2) * LANES] = real - imag
            for band in range(2):
                pw_ref[d, band] = power_of(b_ref, d, band)
        return carry

    def mixed(d, band, j, which):
        if kept:
            return u_ref[d, row_of(band, which, j)]
        real, imag = b_ref[d, row_of(band, 0, j)], b_ref[d, row_of(band, 1, j)]
        return real - imag if which else real + imag

    def pairs(d, carry):
        later = [min(d + k, n - 1) if n <= 16 else jnp.minimum(d + k, n - 1) for k in range(1, SPAN + 1)]
        for band in range(2):
            shared = [zero] * SPAN
            plus = [zero] * SPAN
            minus = [zero] * SPAN
            for j in range(ML_RG):
                r = b_ref[d, row_of(band, 0, j)]
                i = b_ref[d, row_of(band, 1, j)]
                both = mixed(d, band, j, 0)
                for k in range(SPAN):
                    shared[k] = shared[k] + both * b_ref[later[k], row_of(band, 0, j)]
                    plus[k] = plus[k] + r * mixed(later[k], band, j, 0)
                    minus[k] = minus[k] + i * mixed(later[k], band, j, 1)
            c_ref[2 * band, d] = group_sums(*[a - b for a, b in zip(shared, minus)])
            c_ref[2 * band + 1, d] = group_sums(*[a - b for a, b in zip(shared, plus)])
            c_ref[4 + band, d] = pick4(*[pw_ref[e, band] for e in later])
        return carry

    if n <= 16:
        for d in range(0, n + SPAN, 2):
            if d < n:
                filtered(d // 2, 0)
            for due in range(max(0, d - SPAN), d - SPAN + 2):
                pairs(due, 0)
    else:
        lax.fori_loop(0, n // 2, filtered, 0)
        lax.fori_loop(0, n, pairs, 0)

    for h in range(halos):
        hb_ref[h] = apply_filter(m_ref[...], wh_ref[16 * h : 16 * h + 16].reshape(LANES, 4 * LANES).astype(jnp.bfloat16))

    def weights(h, carry):
        dates = pl.ds(16 * h, 16)
        cross = [(c_ref[2 * band, dates], c_ref[2 * band + 1, dates]) for band in range(2)]
        own = [pw_ref[dates, band] for band in range(2)]
        partner = [c_ref[4 + band, dates] for band in range(2)]
        q_ref[0, dates], q_ref[1, dates] = weigh(cross, own, partner, fl_ref[dates])
        return carry

    groups(weights, 0)

    hpow = [[power_of(hb_ref, h, band) for band in range(2)] for h in range(halos)]
    for h in range(halos):
        after = min(h + 1, halos - 1)

        def shifted(value, value_after, k):
            moved = back(value, 8 * k)
            if after == h:
                return moved
            return jnp.where(lane < LANES - 8 * k, moved, back(value_after, 8 * k))

        cross, partner = [], []
        for band in range(2):
            real = [zero] * SPAN
            imag = [zero] * SPAN
            for j in range(ML_RG):
                r = hb_ref[h, row_of(band, 0, j)]
                i = hb_ref[h, row_of(band, 1, j)]
                ra = hb_ref[after, row_of(band, 0, j)]
                ia = hb_ref[after, row_of(band, 1, j)]
                for k in range(SPAN):
                    pr = shifted(r, ra, k + 1)
                    pi = shifted(i, ia, k + 1)
                    real[k] = real[k] + (r * pr + i * pi)
                    imag[k] = imag[k] + (i * pr - r * pi)
            cross.append((group_sums(*real), group_sums(*imag)))
            partner.append(pick4(*[shifted(hpow[h][band], hpow[after][band], k) for k in range(1, SPAN + 1)]))
        weight, weighted = weigh(cross, hpow[h], partner, fh_ref[h])
        for which, value in enumerate((weight, weighted)):
            upto, onward, _ = cell_sums(value[None])
            e_ref[h, which, 0] = upto[0]
            e_ref[h, which, 1] = onward[0]

    for d in range(SPAN):
        x_ref[0, d] = zero
        x_ref[1, d] = zero
        x_ref[0, n + SPAN + d] = zero
        x_ref[1, n + SPAN + d] = zero
        for k in range(SPAN):
            s_ref[0, k, d] = zero
            s_ref[1, k, d] = zero

    def smooth(h, chain):
        dates = pl.ds(16 * h, 16)
        wide = iota((16, 8, LANES), 2)
        boxes = []
        for which in range(2):
            upto, onward, total = cell_sums(q_ref[which, dates])
            far_upto = [pltpu.roll(e_ref[h, which, 0], (lanes - 4 - 8 * t) % LANES, 1) for t in range(16)]
            far_onward = [pltpu.roll(e_ref[h, which, 1], (LANES - 4 - 8 * t) % LANES, 1) for t in range(16)]
            sooner = jnp.where(wide < 4, jnp.stack(far_onward), pltpu.roll(onward, 4, 2))
            later = jnp.where(wide >= lanes - 4, jnp.stack(far_upto), pltpu.roll(upto, LANES - 4, 2))
            boxes.append(total + sooner + later)
        phase = boxes[1] / (boxes[0] + floor_weight)
        weight = boxes[0] * (1.0 / (2 * RADIUS + 1))
        product = weight * phase
        own = pl.ds(16 * h + SPAN, 16)
        for k in range(SPAN):
            s_ref[0, k, own] = weight if k == 0 else pltpu.roll(weight, LANES - k, 2)
            s_ref[1, k, own] = product if k == 0 else pltpu.roll(product, LANES - k, 2)
        for t in range(16):
            x_ref[0, 16 * h + t + SPAN] = chain
            chain = chain + phase[t]
        total_weight = jnp.zeros((16, 8, LANES), jnp.float32)
        pull = ridge_weight * x_ref[0, own]
        for k in range(SPAN):
            low = pl.ds(16 * h + SPAN - 1 - k, 16)
            total_weight = total_weight + s_ref[0, k, own] + s_ref[0, k, low]
            pull = pull - s_ref[1, k, own] + s_ref[1, k, low]
        bt_ref[0, dates] = pull
        bt_ref[1, dates] = 1.0 / (total_weight + ridge_weight)
        out_ref[dates] = pltpu.roll(total_weight, 1, 2)
        return chain

    groups(smooth, zero)

    for sweep in range(ITERS):
        old, new = sweep % 2, (sweep + 1) % 2

        def relax(h, carry):
            total = bt_ref[0, pl.ds(16 * h, 16)]
            for k in range(SPAN):
                total = total + s_ref[0, k, pl.ds(16 * h + SPAN, 16)] * x_ref[old, pl.ds(16 * h + SPAN + 1 + k, 16)]
                below = pl.ds(16 * h + SPAN - 1 - k, 16)
                total = total + s_ref[0, k, below] * x_ref[old, below]
            value = total * bt_ref[1, pl.ds(16 * h, 16)]
            x_ref[new, pl.ds(16 * h + SPAN, 16)] = value
            if sweep == ITERS - 1:
                dates = pl.ds(16 * h, 16)
                out_ref[dates] = jnp.where(iota((16, 8, LANES), 2) % 4 == 1, out_ref[dates], value)
            return carry

        groups(relax, 0)


def spread_kernel(x_ref, far_flags_ref, far_taps_ref, out_ref, m_ref, held_ref, flags_ref, taps_ref, wide_ref, in_sems, side_sems):
    parts = in_sems.shape[1]
    looks = out_ref.shape[0] // parts
    width = x_ref.shape[3] // parts
    blocks = width // LANES
    pairs = blocks // 2
    reach = TAPS // 2
    sub = iota((8, LANES), 0)
    lane = iota((8, LANES), 1)
    zero = jnp.zeros((8, LANES), jnp.float32)

    def fetch(part, q):
        columns = pl.ds(q * width, width)
        return pltpu.make_async_copy(x_ref.at[0, part, :, columns], held_ref.at[part, :, columns], in_sems.at[part, q])

    get_flags = pltpu.make_async_copy(far_flags_ref, flags_ref, side_sems.at[0])
    get_taps = pltpu.make_async_copy(far_taps_ref, taps_ref, side_sems.at[1])
    get_taps.start()
    get_flags.start()
    for q in range(parts):
        for part in range(2):
            fetch(part, q).start()
    wide_ref[...] = jnp.zeros_like(wide_ref)
    get_taps.wait()
    for band in range(2):
        for part in range(2):
            wide_ref[2 * band + part, :, :TAPS] = taps_ref[band, part : part + 1, :].astype(jnp.float32)
    fill_filter(wide_ref, m_ref)
    get_flags.wait()
    flags = [flags_ref[0, k].astype(jnp.float32) for k in range(SPAN)]
    pattern = jnp.where(
        lane % 4 < 2, jnp.where(lane % 4 == 0, flags[0], flags[1]), jnp.where(lane % 4 == 2, flags[2], flags[3])
    )
    made = {}

    def half_of(part, block, half):
        if block < 0 or block >= parts * blocks:
            return zero
        start = block * LANES
        return held_ref[part, :, start : start + LANES].astype(jnp.float32)[8 * half : 8 * half + 8]

    def pair_of(part, index, half):
        if (part, index, half) not in made:
            first = half_of(part, 2 * index - 1, half)
            second = half_of(part, 2 * index, half)
            mixed = pltpu.roll(jnp.where(sub < 4, second, first), 4, 0)
            made[part, index, half] = (jnp.where(sub < 4, first, mixed), jnp.where(sub < 4, mixed, second))
        return made[part, index, half]

    def beyond(q, half, odd):
        after, before = [], []
        for part in range(2):
            value = half_of(part, blocks * (q + 1) + 1, half)
            after.append(pltpu.roll(value, 4, 0) if odd else value)
            value = half_of(part, blocks * q - 2, half)
            before.append(value if odd else pltpu.roll(value, 4, 0))
        side = lane // SPAN % 2
        inside = jnp.where(side == 0, float(q < parts - 1), float(q > 0))
        top = jnp.where(lane < reach, after[0], jnp.where(lane < 2 * reach, pltpu.roll(after[1], reach, 1), pattern))
        bottom = jnp.where(lane >= LANES - reach, before[0], pattern * inside)
        bottom = jnp.where(lane < reach, pltpu.roll(before[1], reach, 1), bottom)
        return jnp.where(sub < 4, top, bottom)

    for q in range(parts):
        for part in range(2):
            if q == 0:
                fetch(part, 0).wait()
            if q + 1 < parts:
                fetch(part, q + 1).wait()
        for half in range(looks // 2):
            for odd in range(2):
                chunk = q * looks + 2 * half + odd
                rows = [pair_of(part, q * pairs + i, half)[odd] for part in range(2) for i in range(pairs + 1)]
                for i in range(0, len(rows), 2):
                    both = jnp.concatenate(rows[i : i + 2], axis=0)
                    out_ref[chunk, 8 * i : 8 * i + 16, :] = both.astype(jnp.bfloat16)
                out_ref[chunk, 8 * len(rows) : 8 * len(rows) + 8, :] = beyond(q, half, odd).astype(jnp.bfloat16)


def gather_kernel(z_ref, phase_ref, weight_ref):
    count = z_ref.shape[0]
    looks = phase_ref.shape[1]
    width = 2 * LANES
    source = iota((3 * LANES, 2 * width), 0) % LANES
    column = iota((3 * LANES, 2 * width), 1)
    block = column % width // CELLS
    chosen = jnp.where(source == SPAN * block + column // width, 1.0, 0.0).astype(jnp.bfloat16)
    rest = z_ref[...].reshape(count * CELLS, LANES)
    pieces = []
    for _ in range(3):
        pieces.append(rest.astype(jnp.bfloat16))
        rest = rest - pieces[-1].astype(jnp.float32)
    moved = jnp.dot(jnp.concatenate(pieces, axis=1), chosen, preferred_element_type=jnp.float32)
    moved = moved.reshape(count, CELLS, 2 * width)
    lines = jnp.where(iota(moved.shape, 1) == iota(moved.shape, 2) % CELLS, moved, 0.0).sum(axis=1)
    for q in range(count // looks):
        for which, out in enumerate((phase_ref, weight_ref)):
            out[0, :, width * q : width * (q + 1)] = lines[
                looks * q : looks * (q + 1), width * which : width * (which + 1)
            ]


def local(slc_stack, band_taps, pair_flags):
    n = lax.axis_size("date")
    looks = slc_stack.shape[2] // ML_AZ
    parts = n // looks
    lanes = slc_stack.shape[3] // (parts * LANES) * ML_AZ
    rows = 2 * (lanes + 2 * ML_AZ) + 8
    halos = n * 8 // LANES
    tile = (8, LANES)
    in_vmem = pl.BlockSpec(memory_space=pltpu.VMEM)
    anywhere = pl.BlockSpec(memory_space=pl.ANY)
    params = pltpu.CompilerParams(vmem_limit_bytes=60 * 1024 * 1024)
    chunks, matrix = pl.pallas_call(
        spread_kernel,
        out_shape=[
            pltpu.VMEM((n, rows, LANES), jnp.bfloat16),
            pltpu.VMEM((4 * LANES, 4 * LANES), jnp.bfloat16),
        ],
        in_specs=[anywhere] * 3,
        out_specs=[in_vmem] * 2,
        scratch_shapes=[
            pltpu.VMEM(slc_stack.shape[1:], jnp.bfloat16),
            pltpu.SMEM(pair_flags.shape, jnp.int32),
            pltpu.VMEM(band_taps.shape, jnp.bfloat16),
            pltpu.VMEM((4, 1, 2 * LANES), jnp.float32),
            pltpu.SemaphoreType.DMA((2, parts)),
            pltpu.SemaphoreType.DMA((2,)),
        ],
        compiler_params=params,
    )(slc_stack, pair_flags, band_taps)
    y = pltpu.with_memory_space_constraint(lax.all_to_all(chunks, "date", 0, 0, tiled=True), pltpu.VMEM)
    matrix = pltpu.with_memory_space_constraint(matrix, pltpu.VMEM)
    solved = pl.pallas_call(
        solve_kernel,
        out_shape=pltpu.VMEM((n, *tile), jnp.float32),
        in_specs=[in_vmem, in_vmem],
        out_specs=in_vmem,
        scratch_shapes=[
            pltpu.VMEM((n, 4 * LANES, LANES), jnp.float32),
            pltpu.VMEM((n if n <= 32 else 1, 4 * LANES, LANES), jnp.float32),
            pltpu.VMEM((n, 8, 4 * LANES), jnp.float32),
            pltpu.VMEM((halos, 4 * LANES, LANES), jnp.float32),
            pltpu.VMEM((n, 2, *tile), jnp.float32),
            pltpu.VMEM((n, *tile), jnp.float32),
            pltpu.VMEM((halos, *tile), jnp.float32),
            pltpu.VMEM((6, n, *tile), jnp.float32),
            pltpu.VMEM((halos, 2, 2, *tile), jnp.float32),
            pltpu.VMEM((2, n, *tile), jnp.float32),
            pltpu.VMEM((2, SPAN, n + SPAN, *tile), jnp.float32),
            pltpu.VMEM((2, n, *tile), jnp.float32),
            pltpu.VMEM((2, n + 2 * SPAN, *tile), jnp.float32),
        ],
        compiler_params=params,
    )(matrix, y)
    z = lax.all_to_all(solved, "date", 0, 0, tiled=True)
    shape = (1, looks, slc_stack.shape[3] // ML_RG)
    if lanes == LANES:
        return tuple(
            pl.pallas_call(
                gather_kernel,
                out_shape=[jax.ShapeDtypeStruct(shape, jnp.float32)] * 2,
                in_specs=[in_vmem],
                out_specs=[in_vmem] * 2,
                compiler_params=params,
            )(pltpu.with_memory_space_constraint(z, pltpu.VMEM))
        )
    z = z[:, :, :lanes].reshape(parts, looks, CELLS, lanes // SPAN, SPAN)[..., :2]
    z = z.transpose(4, 1, 0, 3, 2).reshape(2, *shape)
    return (z[0], z[1])


def solution(mesh):
    in_specs = (P("date", None, "group", None), P(), P("date", None))
    out_specs = (P("date", "group", None), P("date", "group", None))
    return jax.shard_map(local, mesh=mesh, in_specs=in_specs, out_specs=out_specs, check_vma=False)
```

```python
import jax
import jax.numpy as jnp
from jax import lax
from jax.experimental import pallas as pl
from jax.experimental.pallas import tpu as pltpu
from jax.sharding import PartitionSpec as P

TAPS = 32
ML_AZ = 4
ML_RG = 16
SPAN = 4
RADIUS = 8
ITERS = 4
LANES = 128
CELLS = LANES // ML_RG

eps_power = 1e-06
floor_weight = 0.1
ridge_weight = 0.05
split_coef = 2.0


def iota(shape, axis):
    return lax.broadcasted_iota(jnp.int32, shape, axis)


def back(x, steps):
    return pltpu.roll(x, LANES - steps, 1)


def group_sums(x0, x1, x2, x3):
    lane = iota((8, LANES), 1)
    even = lane % 2 == 0
    low = lane % 4 < 2
    u = jnp.where(even, x0 + back(x0, 1), x1 + pltpu.roll(x1, 1, 1))
    v = jnp.where(even, x2 + back(x2, 1), x3 + pltpu.roll(x3, 1, 1))
    return jnp.where(low, u + back(u, 2), v + pltpu.roll(v, 2, 1))


def pick4(x0, x1, x2, x3):
    lane = iota((8, LANES), 1) % 4
    return jnp.where(lane < 2, jnp.where(lane == 0, x0, x1), jnp.where(lane == 2, x2, x3))


def fill_filter(taps_ref, m_ref):
    width = 2 * LANES
    sub = iota((CELLS, width), 0)

    def placed(row):
        taps = jnp.broadcast_to(taps_ref[row], (CELLS, width))
        result = jnp.zeros((CELLS, width), jnp.float32)
        for c in range(CELLS):
            result = jnp.where(sub == c, pltpu.roll(taps, (ML_RG * c - TAPS // 2) % width, 1), result)
        return result

    def along(base, j):
        both = [base if jj == 0 else pltpu.roll(base, jj, 1) for jj in (j, j + 1)]
        return jnp.concatenate(both, axis=0)

    for band in range(2):
        real, imag = placed(2 * band), placed(2 * band + 1)
        for j in range(0, ML_RG, 2):
            tr, ti = along(real, j), along(imag, j)
            real_row = ((band * 2 + 0) * ML_RG + j) * CELLS
            imag_row = ((band * 2 + 1) * ML_RG + j) * CELLS
            m_ref[real_row : real_row + 16, :width] = tr.astype(jnp.bfloat16)
            m_ref[real_row : real_row + 16, width:] = (-ti).astype(jnp.bfloat16)
            m_ref[imag_row : imag_row + 16, :width] = ti.astype(jnp.bfloat16)
            m_ref[imag_row : imag_row + 16, width:] = tr.astype(jnp.bfloat16)


def row_of(band, part, j):
    start = ((band * 2 + part) * ML_RG + j) * CELLS
    return slice(start, start + CELLS)


def apply_filter(matrix, windows):
    bands = lax.dot_general(
        matrix, windows, (((1,), (1,)), ((), ())), preferred_element_type=jnp.float32
    )
    return bands.astype(jnp.bfloat16).astype(jnp.float32)


def power_of(b_ref, d, band):
    total = jnp.zeros((CELLS, LANES), jnp.float32)
    for j in range(ML_RG):
        r = b_ref[d, row_of(band, 0, j)]
        i = b_ref[d, row_of(band, 1, j)]
        total = total + (r * r + i * i)
    return group_sums(total, total, total, total)


def weigh(cross, own, partner, flags):
    (re0, im0), (re1, im1) = cross
    pow0 = own[0] * partner[0] + eps_power
    pow1 = own[1] * partner[1] + eps_power
    coherence = (re0 * re0 + im0 * im0) / pow0 + (re1 * re1 + im1 * im1) / pow1
    weight = flags * 0.5 * coherence
    raw = split_coef * (im0 * re1 - re0 * im1) / jnp.sqrt(pow0 * pow1)
    return weight, weight * raw


def cell_sums(x):
    sub = iota(x.shape, 1)
    upto = x
    for step in (1, 2, 4):
        upto = upto + jnp.where(sub >= step, pltpu.roll(upto, step, 1), 0.0)
    total = jnp.broadcast_to(upto[:, CELLS - 1 : CELLS], x.shape)
    return upto, total - upto + x, total


def solve_kernel(
    m_ref, y_ref, out_ref, b_ref, u_ref, wh_ref, hb_ref, pw_ref, fl_ref, fh_ref, c_ref, e_ref, q_ref, s_ref, bt_ref, x_ref
):
    n, rows, _ = y_ref.shape
    tiles = rows // 16
    lanes = 8 * (tiles - 1)
    halos = hb_ref.shape[0]
    kept = u_ref.shape[0] == n
    lane = iota((8, LANES), 1)
    sub = iota((8, LANES), 0)
    zero = jnp.zeros((8, LANES), jnp.float32)

    def each(step, start):
        return lax.fori_loop(0, n, step, start, unroll=n <= 16)

    def groups(step, start):
        return lax.fori_loop(0, n // 16, step, start, unroll=n <= 16)

    def windows_of(d):
        windows, edges = [], []
        held = y_ref[d].astype(jnp.float32).reshape(rows // 8, 8, LANES)
        beyond = held[rows // 8 - 1]
        main = beyond[0:1]
        main = jnp.where(lane[:1] < LANES // 2, pltpu.roll(main, LANES // 2, 1), main)
        fl_ref[d] = jnp.broadcast_to(main, (8, LANES))
        side = beyond[4:5]
        middle = (lane[:1] >= LANES // 4) & (lane[:1] < 3 * LANES // 4)
        side = jnp.where(middle, side, pltpu.roll(side, LANES // 2, 1))
        fh_ref[d // 16] = jnp.where(lane // 8 == d % 16, jnp.broadcast_to(side, (8, LANES)), fh_ref[d // 16])
        for part in range(2):
            v = held[part * tiles : (part + 1) * tiles]
            subs = iota((tiles - 1, 8, LANES), 1)
            wide = iota((tiles - 1, 8, LANES), 2)
            main = pltpu.roll(jnp.where(subs < 4, v[1:], v[:-1]), 4, 1)
            edge = jnp.where(wide < LANES // 2, v[1:], v[:-1])
            windows.append(main.reshape(lanes, LANES))
            windows.append(edge.reshape(lanes, LANES))
            first, last = v[0], v[tiles - 1]
            far = beyond if part == 0 else pltpu.roll(beyond, LANES - TAPS // 2, 1)
            edges.append(pltpu.roll(jnp.where(sub < 4, first, last), 4, 0))
            later = jnp.where(sub < 4, far, first)
            sooner = jnp.where(sub < 4, last, far)
            edges.append(jnp.where(lane < LANES // 2, later, sooner))
        windows = jnp.concatenate(windows, axis=1)
        if lanes < LANES:
            windows = jnp.concatenate([windows, jnp.zeros((LANES - lanes, 4 * LANES), jnp.float32)], axis=0)
        wh_ref[d] = jnp.concatenate(edges, axis=1)
        return windows.astype(jnp.bfloat16)

    def filtered(pair, carry):
        dates = (2 * pair, 2 * pair + 1)
        bands = apply_filter(m_ref[...], jnp.concatenate([windows_of(d) for d in dates], axis=0))
        for t, d in enumerate(dates):
            own = bands[:, LANES * t : LANES * (t + 1)]
            b_ref[d] = own
            for band in range(2 if kept else 0):
                real = own[2 * band * LANES : (2 * band + 1) * LANES]
                imag = own[(2 * band + 1) * LANES : (2 * band + 2) * LANES]
                u_ref[d, 2 * band * LANES : (2 * band + 1) * LANES] = real + imag
                u_ref[d, (2 * band + 1) * LANES : (2 * band + 2) * LANES] = real - imag
                squares = (real * real + imag * imag).reshape(ML_RG, CELLS, LANES).sum(axis=0)
                pw_ref[d, band] = group_sums(squares, squares, squares, squares)
            for band in range(0 if kept else 2):
                pw_ref[d, band] = power_of(b_ref, d, band)
        return carry

    lax.fori_loop(0, n // 2, filtered, 0, unroll=n <= 16)

    for h in range(halos):
        hb_ref[h] = apply_filter(m_ref[...], wh_ref[16 * h : 16 * h + 16].reshape(LANES, 4 * LANES).astype(jnp.bfloat16))

    def mixed(d, band, j, which):
        if kept:
            return u_ref[d, row_of(band, which, j)]
        real, imag = b_ref[d, row_of(band, 0, j)], b_ref[d, row_of(band, 1, j)]
        return real - imag if which else real + imag

    def pairs(d, carry):
        later = [jnp.minimum(d + k, n - 1) for k in range(1, SPAN + 1)]
        for band in range(2):
            shared = [zero] * SPAN
            plus = [zero] * SPAN
            minus = [zero] * SPAN
            for j in range(ML_RG):
                r = b_ref[d, row_of(band, 0, j)]
                i = b_ref[d, row_of(band, 1, j)]
                both = mixed(d, band, j, 0)
                for k in range(SPAN):
                    shared[k] = shared[k] + both * b_ref[later[k], row_of(band, 0, j)]
                    plus[k] = plus[k] + r * mixed(later[k], band, j, 0)
                    minus[k] = minus[k] + i * mixed(later[k], band, j, 1)
            c_ref[2 * band, d] = group_sums(*[a - b for a, b in zip(shared, minus)])
            c_ref[2 * band + 1, d] = group_sums(*[a - b for a, b in zip(shared, plus)])
            c_ref[4 + band, d] = pick4(*[pw_ref[e, band] for e in later])
        return carry

    each(pairs, 0)

    def weights(h, carry):
        dates = pl.ds(16 * h, 16)
        cross = [(c_ref[2 * band, dates], c_ref[2 * band + 1, dates]) for band in range(2)]
        own = [pw_ref[dates, band] for band in range(2)]
        partner = [c_ref[4 + band, dates] for band in range(2)]
        q_ref[0, dates], q_ref[1, dates] = weigh(cross, own, partner, fl_ref[dates])
        return carry

    groups(weights, 0)

    hpow = [[power_of(hb_ref, h, band) for band in range(2)] for h in range(halos)]
    for h in range(halos):
        after = min(h + 1, halos - 1)

        def shifted(value, value_after, k):
            moved = back(value, 8 * k)
            if after == h:
                return moved
            return jnp.where(lane < LANES - 8 * k, moved, back(value_after, 8 * k))

        cross, partner = [], []
        for band in range(2):
            real = [zero] * SPAN
            imag = [zero] * SPAN
            for j in range(ML_RG):
                r = hb_ref[h, row_of(band, 0, j)]
                i = hb_ref[h, row_of(band, 1, j)]
                ra = hb_ref[after, row_of(band, 0, j)]
                ia = hb_ref[after, row_of(band, 1, j)]
                for k in range(SPAN):
                    pr = shifted(r, ra, k + 1)
                    pi = shifted(i, ia, k + 1)
                    real[k] = real[k] + (r * pr + i * pi)
                    imag[k] = imag[k] + (i * pr - r * pi)
            cross.append((group_sums(*real), group_sums(*imag)))
            partner.append(pick4(*[shifted(hpow[h][band], hpow[after][band], k) for k in range(1, SPAN + 1)]))
        weight, weighted = weigh(cross, hpow[h], partner, fh_ref[h])
        for which, value in enumerate((weight, weighted)):
            upto, onward, _ = cell_sums(value[None])
            e_ref[h, which, 0] = upto[0]
            e_ref[h, which, 1] = onward[0]

    for d in range(SPAN):
        x_ref[0, d] = zero
        x_ref[1, d] = zero
        x_ref[0, n + SPAN + d] = zero
        x_ref[1, n + SPAN + d] = zero
        for k in range(SPAN):
            s_ref[0, k, d] = zero
            s_ref[1, k, d] = zero

    def smooth(h, chain):
        dates = pl.ds(16 * h, 16)
        wide = iota((16, 8, LANES), 2)
        boxes = []
        for which in range(2):
            upto, onward, total = cell_sums(q_ref[which, dates])
            far_upto = [pltpu.roll(e_ref[h, which, 0], (lanes - 4 - 8 * t) % LANES, 1) for t in range(16)]
            far_onward = [pltpu.roll(e_ref[h, which, 1], (LANES - 4 - 8 * t) % LANES, 1) for t in range(16)]
            sooner = jnp.where(wide < 4, jnp.stack(far_onward), pltpu.roll(onward, 4, 2))
            later = jnp.where(wide >= lanes - 4, jnp.stack(far_upto), pltpu.roll(upto, LANES - 4, 2))
            boxes.append(total + sooner + later)
        phase = boxes[1] / (boxes[0] + floor_weight)
        weight = boxes[0] * (1.0 / (2 * RADIUS + 1))
        product = weight * phase
        own = pl.ds(16 * h + SPAN, 16)
        for k in range(SPAN):
            s_ref[0, k, own] = weight if k == 0 else pltpu.roll(weight, LANES - k, 2)
            s_ref[1, k, own] = product if k == 0 else pltpu.roll(product, LANES - k, 2)
        for t in range(16):
            x_ref[0, 16 * h + t + SPAN] = chain
            chain = chain + phase[t]
        total_weight = jnp.zeros((16, 8, LANES), jnp.float32)
        pull = ridge_weight * x_ref[0, own]
        for k in range(SPAN):
            low = pl.ds(16 * h + SPAN - 1 - k, 16)
            total_weight = total_weight + s_ref[0, k, own] + s_ref[0, k, low]
            pull = pull - s_ref[1, k, own] + s_ref[1, k, low]
        bt_ref[0, dates] = pull
        bt_ref[1, dates] = 1.0 / (total_weight + ridge_weight)
        out_ref[dates] = pltpu.roll(total_weight, 1, 2)
        return chain

    groups(smooth, zero)

    for sweep in range(ITERS):
        old, new = sweep % 2, (sweep + 1) % 2

        def relax(h, carry):
            total = bt_ref[0, pl.ds(16 * h, 16)]
            for k in range(SPAN):
                total = total + s_ref[0, k, pl.ds(16 * h + SPAN, 16)] * x_ref[old, pl.ds(16 * h + SPAN + 1 + k, 16)]
                below = pl.ds(16 * h + SPAN - 1 - k, 16)
                total = total + s_ref[0, k, below] * x_ref[old, below]
            value = total * bt_ref[1, pl.ds(16 * h, 16)]
            x_ref[new, pl.ds(16 * h + SPAN, 16)] = value
            if sweep == ITERS - 1:
                dates = pl.ds(16 * h, 16)
                out_ref[dates] = jnp.where(iota((16, 8, LANES), 2) % 4 == 1, out_ref[dates], value)
            return carry

        groups(relax, 0)


def spread_kernel(x_ref, far_flags_ref, far_taps_ref, out_ref, m_ref, held_ref, flags_ref, taps_ref, wide_ref, in_sems, side_sems):
    parts = in_sems.shape[1]
    looks = out_ref.shape[0] // parts
    width = x_ref.shape[3] // parts
    blocks = width // LANES
    pairs = blocks // 2
    reach = TAPS // 2
    sub = iota((8, LANES), 0)
    lane = iota((8, LANES), 1)
    zero = jnp.zeros((8, LANES), jnp.float32)

    def fetch(part, q):
        columns = pl.ds(q * width, width)
        return pltpu.make_async_copy(x_ref.at[0, part, :, columns], held_ref.at[part, :, columns], in_sems.at[part, q])

    get_flags = pltpu.make_async_copy(far_flags_ref, flags_ref, side_sems.at[0])
    get_taps = pltpu.make_async_copy(far_taps_ref, taps_ref, side_sems.at[1])
    get_taps.start()
    get_flags.start()
    for q in range(parts):
        for part in range(2):
            fetch(part, q).start()
    wide_ref[...] = jnp.zeros_like(wide_ref)
    get_taps.wait()
    for band in range(2):
        for part in range(2):
            wide_ref[2 * band + part, :, :TAPS] = taps_ref[band, part : part + 1, :].astype(jnp.float32)
    fill_filter(wide_ref, m_ref)
    get_flags.wait()
    flags = [flags_ref[0, k].astype(jnp.float32) for k in range(SPAN)]
    pattern = jnp.where(
        lane % 4 < 2, jnp.where(lane % 4 == 0, flags[0], flags[1]), jnp.where(lane % 4 == 2, flags[2], flags[3])
    )
    made = {}

    def half_of(part, block, half):
        if block < 0 or block >= parts * blocks:
            return zero
        start = block * LANES
        return held_ref[part, :, start : start + LANES].astype(jnp.float32)[8 * half : 8 * half + 8]

    def pair_of(part, index, half):
        if (part, index, half) not in made:
            first = half_of(part, 2 * index - 1, half)
            second = half_of(part, 2 * index, half)
            mixed = pltpu.roll(jnp.where(sub < 4, second, first), 4, 0)
            made[part, index, half] = (jnp.where(sub < 4, first, mixed), jnp.where(sub < 4, mixed, second))
        return made[part, index, half]

    def beyond(q, half, odd):
        after, before = [], []
        for part in range(2):
            value = half_of(part, blocks * (q + 1) + 1, half)
            after.append(pltpu.roll(value, 4, 0) if odd else value)
            value = half_of(part, blocks * q - 2, half)
            before.append(value if odd else pltpu.roll(value, 4, 0))
        side = lane // SPAN % 2
        inside = jnp.where(side == 0, float(q < parts - 1), float(q > 0))
        top = jnp.where(lane < reach, after[0], jnp.where(lane < 2 * reach, pltpu.roll(after[1], reach, 1), pattern))
        bottom = jnp.where(lane >= LANES - reach, before[0], pattern * inside)
        bottom = jnp.where(lane < reach, pltpu.roll(before[1], reach, 1), bottom)
        return jnp.where(sub < 4, top, bottom)

    for q in range(parts):
        for part in range(2):
            if q == 0:
                fetch(part, 0).wait()
            if q + 1 < parts:
                fetch(part, q + 1).wait()
        for half in range(looks // 2):
            for odd in range(2):
                chunk = q * looks + 2 * half + odd
                rows = [pair_of(part, q * pairs + i, half)[odd] for part in range(2) for i in range(pairs + 1)]
                for i in range(0, len(rows), 2):
                    both = jnp.concatenate(rows[i : i + 2], axis=0)
                    out_ref[chunk, 8 * i : 8 * i + 16, :] = both.astype(jnp.bfloat16)
                out_ref[chunk, 8 * len(rows) : 8 * len(rows) + 8, :] = beyond(q, half, odd).astype(jnp.bfloat16)


def gather_kernel(z_ref, phase_ref, weight_ref):
    count = z_ref.shape[0]
    looks = phase_ref.shape[1]
    width = 2 * LANES
    source = iota((3 * LANES, 2 * width), 0) % LANES
    column = iota((3 * LANES, 2 * width), 1)
    block = column % width // CELLS
    chosen = jnp.where(source == SPAN * block + column // width, 1.0, 0.0).astype(jnp.bfloat16)
    rest = z_ref[...].reshape(count * CELLS, LANES)
    pieces = []
    for _ in range(3):
        pieces.append(rest.astype(jnp.bfloat16))
        rest = rest - pieces[-1].astype(jnp.float32)
    moved = jnp.dot(jnp.concatenate(pieces, axis=1), chosen, preferred_element_type=jnp.float32)
    moved = moved.reshape(count, CELLS, 2 * width)
    lines = jnp.where(iota(moved.shape, 1) == iota(moved.shape, 2) % CELLS, moved, 0.0).sum(axis=1)
    for q in range(count // looks):
        for which, out in enumerate((phase_ref, weight_ref)):
            out[0, :, width * q : width * (q + 1)] = lines[
                looks * q : looks * (q + 1), width * which : width * (which + 1)
            ]


def local(slc_stack, band_taps, pair_flags):
    n = lax.axis_size("date")
    looks = slc_stack.shape[2] // ML_AZ
    parts = n // looks
    lanes = slc_stack.shape[3] // (parts * LANES) * ML_AZ
    rows = 2 * (lanes + 2 * ML_AZ) + 8
    halos = n * 8 // LANES
    tile = (8, LANES)
    in_vmem = pl.BlockSpec(memory_space=pltpu.VMEM)
    anywhere = pl.BlockSpec(memory_space=pl.ANY)
    params = pltpu.CompilerParams(vmem_limit_bytes=60 * 1024 * 1024)
    chunks, matrix = pl.pallas_call(
        spread_kernel,
        out_shape=[
            pltpu.VMEM((n, rows, LANES), jnp.bfloat16),
            pltpu.VMEM((4 * LANES, 4 * LANES), jnp.bfloat16),
        ],
        in_specs=[anywhere] * 3,
        out_specs=[in_vmem] * 2,
        scratch_shapes=[
            pltpu.VMEM(slc_stack.shape[1:], jnp.bfloat16),
            pltpu.SMEM(pair_flags.shape, jnp.int32),
            pltpu.VMEM(band_taps.shape, jnp.bfloat16),
            pltpu.VMEM((4, 1, 2 * LANES), jnp.float32),
            pltpu.SemaphoreType.DMA((2, parts)),
            pltpu.SemaphoreType.DMA((2,)),
        ],
        compiler_params=params,
    )(slc_stack, pair_flags, band_taps)
    y = pltpu.with_memory_space_constraint(lax.all_to_all(chunks, "date", 0, 0, tiled=True), pltpu.VMEM)
    matrix = pltpu.with_memory_space_constraint(matrix, pltpu.VMEM)
    solved = pl.pallas_call(
        solve_kernel,
        out_shape=pltpu.VMEM((n, *tile), jnp.float32),
        in_specs=[in_vmem, in_vmem],
        out_specs=in_vmem,
        scratch_shapes=[
            pltpu.VMEM((n, 4 * LANES, LANES), jnp.float32),
            pltpu.VMEM((n if n <= 32 else 1, 4 * LANES, LANES), jnp.float32),
            pltpu.VMEM((n, 8, 4 * LANES), jnp.float32),
            pltpu.VMEM((halos, 4 * LANES, LANES), jnp.float32),
            pltpu.VMEM((n, 2, *tile), jnp.float32),
            pltpu.VMEM((n, *tile), jnp.float32),
            pltpu.VMEM((halos, *tile), jnp.float32),
            pltpu.VMEM((6, n, *tile), jnp.float32),
            pltpu.VMEM((halos, 2, 2, *tile), jnp.float32),
            pltpu.VMEM((2, n, *tile), jnp.float32),
            pltpu.VMEM((2, SPAN, n + SPAN, *tile), jnp.float32),
            pltpu.VMEM((2, n, *tile), jnp.float32),
            pltpu.VMEM((2, n + 2 * SPAN, *tile), jnp.float32),
        ],
        compiler_params=params,
    )(matrix, y)
    z = lax.all_to_all(solved, "date", 0, 0, tiled=True)
    shape = (1, looks, slc_stack.shape[3] // ML_RG)
    if lanes == LANES:
        return tuple(
            pl.pallas_call(
                gather_kernel,
                out_shape=[jax.ShapeDtypeStruct(shape, jnp.float32)] * 2,
                in_specs=[in_vmem],
                out_specs=[in_vmem] * 2,
                compiler_params=params,
            )(pltpu.with_memory_space_constraint(z, pltpu.VMEM))
        )
    z = z[:, :, :lanes].reshape(parts, looks, CELLS, lanes // SPAN, SPAN)[..., :2]
    z = z.transpose(4, 1, 0, 3, 2).reshape(2, *shape)
    return (z[0], z[1])


def solution(mesh):
    in_specs = (P("date", None, "group", None), P(), P("date", None))
    out_specs = (P("date", "group", None), P("date", "group", None))
    return jax.shard_map(local, mesh=mesh, in_specs=in_specs, out_specs=out_specs, check_vma=False)
```

```python
import jax
import jax.numpy as jnp
from jax import lax
from jax.experimental import pallas as pl
from jax.experimental.pallas import tpu as pltpu
from jax.sharding import PartitionSpec as P

TAPS = 32
ML_AZ = 4
ML_RG = 16
SPAN = 4
RADIUS = 8
ITERS = 4
LANES = 128
CELLS = LANES // ML_RG

eps_power = 1e-06
floor_weight = 0.1
ridge_weight = 0.05
split_coef = 2.0


def iota(shape, axis):
    return lax.broadcasted_iota(jnp.int32, shape, axis)


def back(x, steps):
    return pltpu.roll(x, LANES - steps, 1)


def group_sums(x0, x1, x2, x3):
    lane = iota((8, LANES), 1)
    even = lane % 2 == 0
    low = lane % 4 < 2
    u = jnp.where(even, x0 + back(x0, 1), x1 + pltpu.roll(x1, 1, 1))
    v = jnp.where(even, x2 + back(x2, 1), x3 + pltpu.roll(x3, 1, 1))
    return jnp.where(low, u + back(u, 2), v + pltpu.roll(v, 2, 1))


def pick4(x0, x1, x2, x3):
    lane = iota((8, LANES), 1) % 4
    return jnp.where(lane < 2, jnp.where(lane == 0, x0, x1), jnp.where(lane == 2, x2, x3))


def fill_filter(taps_ref, m_ref):
    width = 2 * LANES
    sub = iota((CELLS, width), 0)

    def placed(row):
        taps = jnp.broadcast_to(taps_ref[row], (CELLS, width))
        result = jnp.zeros((CELLS, width), jnp.float32)
        for c in range(CELLS):
            result = jnp.where(sub == c, pltpu.roll(taps, (ML_RG * c - TAPS // 2) % width, 1), result)
        return result

    def along(base, j):
        both = [base if jj == 0 else pltpu.roll(base, jj, 1) for jj in (j, j + 1)]
        return jnp.concatenate(both, axis=0)

    for band in range(2):
        real, imag = placed(2 * band), placed(2 * band + 1)
        for j in range(0, ML_RG, 2):
            tr, ti = along(real, j), along(imag, j)
            real_row = ((band * 2 + 0) * ML_RG + j) * CELLS
            imag_row = ((band * 2 + 1) * ML_RG + j) * CELLS
            m_ref[real_row : real_row + 16, :width] = tr.astype(jnp.bfloat16)
            m_ref[real_row : real_row + 16, width:] = (-ti).astype(jnp.bfloat16)
            m_ref[imag_row : imag_row + 16, :width] = ti.astype(jnp.bfloat16)
            m_ref[imag_row : imag_row + 16, width:] = tr.astype(jnp.bfloat16)


def row_of(band, part, j):
    start = ((band * 2 + part) * ML_RG + j) * CELLS
    return slice(start, start + CELLS)


def apply_filter(matrix, windows):
    bands = lax.dot_general(
        matrix, windows, (((1,), (1,)), ((), ())), preferred_element_type=jnp.float32
    )
    return bands.astype(jnp.bfloat16).astype(jnp.float32)


def power_of(b_ref, d, band):
    total = jnp.zeros((CELLS, LANES), jnp.float32)
    for j in range(ML_RG):
        r = b_ref[d, row_of(band, 0, j)]
        i = b_ref[d, row_of(band, 1, j)]
        total = total + (r * r + i * i)
    return group_sums(total, total, total, total)


def weigh(cross, own, partner, flags):
    (re0, im0), (re1, im1) = cross
    pow0 = own[0] * partner[0] + eps_power
    pow1 = own[1] * partner[1] + eps_power
    coherence = (re0 * re0 + im0 * im0) / pow0 + (re1 * re1 + im1 * im1) / pow1
    weight = flags * 0.5 * coherence
    raw = split_coef * (im0 * re1 - re0 * im1) / jnp.sqrt(pow0 * pow1)
    return weight, weight * raw


def cell_sums(x):
    sub = iota(x.shape, 1)
    upto = x
    for step in (1, 2, 4):
        upto = upto + jnp.where(sub >= step, pltpu.roll(upto, step, 1), 0.0)
    total = jnp.broadcast_to(upto[:, CELLS - 1 : CELLS], x.shape)
    return upto, total - upto + x, total


def solve_kernel(
    m_ref, y_ref, out_ref, b_ref, u_ref, wh_ref, hb_ref, pw_ref, fl_ref, fh_ref, c_ref, e_ref, q_ref, s_ref, bt_ref, x_ref
):
    n, rows, _ = y_ref.shape
    tiles = rows // 16
    lanes = 8 * (tiles - 1)
    halos = hb_ref.shape[0]
    kept = u_ref.shape[0] == n
    lane = iota((8, LANES), 1)
    sub = iota((8, LANES), 0)
    zero = jnp.zeros((8, LANES), jnp.float32)

    def each(step, start):
        return lax.fori_loop(0, n, step, start, unroll=n <= 16)

    def groups(step, start):
        return lax.fori_loop(0, n // 16, step, start, unroll=n <= 16)

    def windows_of(d):
        windows, edges = [], []
        held = y_ref[d].astype(jnp.float32).reshape(rows // 8, 8, LANES)
        beyond = held[rows // 8 - 1]
        main = beyond[0:1]
        main = jnp.where(lane[:1] < LANES // 2, pltpu.roll(main, LANES // 2, 1), main)
        fl_ref[d] = jnp.broadcast_to(main, (8, LANES))
        side = beyond[4:5]
        middle = (lane[:1] >= LANES // 4) & (lane[:1] < 3 * LANES // 4)
        side = jnp.where(middle, side, pltpu.roll(side, LANES // 2, 1))
        fh_ref[d // 16] = jnp.where(lane // 8 == d % 16, jnp.broadcast_to(side, (8, LANES)), fh_ref[d // 16])
        for part in range(2):
            v = held[part * tiles : (part + 1) * tiles]
            subs = iota((tiles - 1, 8, LANES), 1)
            wide = iota((tiles - 1, 8, LANES), 2)
            main = pltpu.roll(jnp.where(subs < 4, v[1:], v[:-1]), 4, 1)
            edge = jnp.where(wide < LANES // 2, v[1:], v[:-1])
            windows.append(main.reshape(lanes, LANES))
            windows.append(edge.reshape(lanes, LANES))
            first, last = v[0], v[tiles - 1]
            far = beyond if part == 0 else pltpu.roll(beyond, LANES - TAPS // 2, 1)
            edges.append(pltpu.roll(jnp.where(sub < 4, first, last), 4, 0))
            later = jnp.where(sub < 4, far, first)
            sooner = jnp.where(sub < 4, last, far)
            edges.append(jnp.where(lane < LANES // 2, later, sooner))
        windows = jnp.concatenate(windows, axis=1)
        if lanes < LANES:
            windows = jnp.concatenate([windows, jnp.zeros((LANES - lanes, 4 * LANES), jnp.float32)], axis=0)
        wh_ref[d] = jnp.concatenate(edges, axis=1)
        return windows.astype(jnp.bfloat16)

    def filtered(pair, carry):
        dates = [4 * pair + t for t in range(4)]
        bands = apply_filter(m_ref[...], jnp.concatenate([windows_of(d) for d in dates], axis=0))
        for t, d in enumerate(dates):
            own = bands[:, LANES * t : LANES * (t + 1)]
            b_ref[d] = own
            for band in range(2 if kept else 0):
                real = own[2 * band * LANES : (2 * band + 1) * LANES]
                imag = own[(2 * band + 1) * LANES : (2 * band + 2) * LANES]
                u_ref[d, 2 * band * LANES : (2 * band + 1) * LANES] = real + imag
                u_ref[d, (2 * band + 1) * LANES : (2 * band + 2) * LANES] = real - imag
            for band in range(2):
                pw_ref[d, band] = power_of(b_ref, d, band)
        return carry

    lax.fori_loop(0, n // 4, filtered, 0, unroll=n <= 16)

    for h in range(halos):
        hb_ref[h] = apply_filter(m_ref[...], wh_ref[16 * h : 16 * h + 16].reshape(LANES, 4 * LANES).astype(jnp.bfloat16))

    def mixed(d, band, j, which):
        if kept:
            return u_ref[d, row_of(band, which, j)]
        real, imag = b_ref[d, row_of(band, 0, j)], b_ref[d, row_of(band, 1, j)]
        return real - imag if which else real + imag

    def pairs(d, carry):
        later = [jnp.minimum(d + k, n - 1) for k in range(1, SPAN + 1)]
        for band in range(2):
            shared = [zero] * SPAN
            plus = [zero] * SPAN
            minus = [zero] * SPAN
            for j in range(ML_RG):
                r = b_ref[d, row_of(band, 0, j)]
                i = b_ref[d, row_of(band, 1, j)]
                both = mixed(d, band, j, 0)
                for k in range(SPAN):
                    shared[k] = shared[k] + both * b_ref[later[k], row_of(band, 0, j)]
                    plus[k] = plus[k] + r * mixed(later[k], band, j, 0)
                    minus[k] = minus[k] + i * mixed(later[k], band, j, 1)
            c_ref[2 * band, d] = group_sums(*[a - b for a, b in zip(shared, minus)])
            c_ref[2 * band + 1, d] = group_sums(*[a - b for a, b in zip(shared, plus)])
            c_ref[4 + band, d] = pick4(*[pw_ref[e, band] for e in later])
        return carry

    each(pairs, 0)

    def weights(h, carry):
        dates = pl.ds(16 * h, 16)
        cross = [(c_ref[2 * band, dates], c_ref[2 * band + 1, dates]) for band in range(2)]
        own = [pw_ref[dates, band] for band in range(2)]
        partner = [c_ref[4 + band, dates] for band in range(2)]
        q_ref[0, dates], q_ref[1, dates] = weigh(cross, own, partner, fl_ref[dates])
        return carry

    groups(weights, 0)

    hpow = [[power_of(hb_ref, h, band) for band in range(2)] for h in range(halos)]
    for h in range(halos):
        after = min(h + 1, halos - 1)

        def shifted(value, value_after, k):
            moved = back(value, 8 * k)
            if after == h:
                return moved
            return jnp.where(lane < LANES - 8 * k, moved, back(value_after, 8 * k))

        cross, partner = [], []
        for band in range(2):
            real = [zero] * SPAN
            imag = [zero] * SPAN
            for j in range(ML_RG):
                r = hb_ref[h, row_of(band, 0, j)]
                i = hb_ref[h, row_of(band, 1, j)]
                ra = hb_ref[after, row_of(band, 0, j)]
                ia = hb_ref[after, row_of(band, 1, j)]
                for k in range(SPAN):
                    pr = shifted(r, ra, k + 1)
                    pi = shifted(i, ia, k + 1)
                    real[k] = real[k] + (r * pr + i * pi)
                    imag[k] = imag[k] + (i * pr - r * pi)
            cross.append((group_sums(*real), group_sums(*imag)))
            partner.append(pick4(*[shifted(hpow[h][band], hpow[after][band], k) for k in range(1, SPAN + 1)]))
        weight, weighted = weigh(cross, hpow[h], partner, fh_ref[h])
        for which, value in enumerate((weight, weighted)):
            upto, onward, _ = cell_sums(value[None])
            e_ref[h, which, 0] = upto[0]
            e_ref[h, which, 1] = onward[0]

    for d in range(SPAN):
        x_ref[0, d] = zero
        x_ref[1, d] = zero
        x_ref[0, n + SPAN + d] = zero
        x_ref[1, n + SPAN + d] = zero
        for k in range(SPAN):
            s_ref[0, k, d] = zero
            s_ref[1, k, d] = zero

    def smooth(h, chain):
        dates = pl.ds(16 * h, 16)
        wide = iota((16, 8, LANES), 2)
        boxes = []
        for which in range(2):
            upto, onward, total = cell_sums(q_ref[which, dates])
            far_upto = [pltpu.roll(e_ref[h, which, 0], (lanes - 4 - 8 * t) % LANES, 1) for t in range(16)]
            far_onward = [pltpu.roll(e_ref[h, which, 1], (LANES - 4 - 8 * t) % LANES, 1) for t in range(16)]
            sooner = jnp.where(wide < 4, jnp.stack(far_onward), pltpu.roll(onward, 4, 2))
            later = jnp.where(wide >= lanes - 4, jnp.stack(far_upto), pltpu.roll(upto, LANES - 4, 2))
            boxes.append(total + sooner + later)
        phase = boxes[1] / (boxes[0] + floor_weight)
        weight = boxes[0] * (1.0 / (2 * RADIUS + 1))
        product = weight * phase
        own = pl.ds(16 * h + SPAN, 16)
        for k in range(SPAN):
            s_ref[0, k, own] = weight if k == 0 else pltpu.roll(weight, LANES - k, 2)
            s_ref[1, k, own] = product if k == 0 else pltpu.roll(product, LANES - k, 2)
        for t in range(16):
            x_ref[0, 16 * h + t + SPAN] = chain
            chain = chain + phase[t]
        total_weight = jnp.zeros((16, 8, LANES), jnp.float32)
        pull = ridge_weight * x_ref[0, own]
        for k in range(SPAN):
            low = pl.ds(16 * h + SPAN - 1 - k, 16)
            total_weight = total_weight + s_ref[0, k, own] + s_ref[0, k, low]
            pull = pull - s_ref[1, k, own] + s_ref[1, k, low]
        bt_ref[0, dates] = pull
        bt_ref[1, dates] = 1.0 / (total_weight + ridge_weight)
        out_ref[dates] = pltpu.roll(total_weight, 1, 2)
        return chain

    groups(smooth, zero)

    for sweep in range(ITERS):
        old, new = sweep % 2, (sweep + 1) % 2

        def relax(h, carry):
            total = bt_ref[0, pl.ds(16 * h, 16)]
            for k in range(SPAN):
                total = total + s_ref[0, k, pl.ds(16 * h + SPAN, 16)] * x_ref[old, pl.ds(16 * h + SPAN + 1 + k, 16)]
                below = pl.ds(16 * h + SPAN - 1 - k, 16)
                total = total + s_ref[0, k, below] * x_ref[old, below]
            value = total * bt_ref[1, pl.ds(16 * h, 16)]
            x_ref[new, pl.ds(16 * h + SPAN, 16)] = value
            if sweep == ITERS - 1:
                dates = pl.ds(16 * h, 16)
                out_ref[dates] = jnp.where(iota((16, 8, LANES), 2) % 4 == 1, out_ref[dates], value)
            return carry

        groups(relax, 0)


def spread_kernel(x_ref, far_flags_ref, far_taps_ref, out_ref, m_ref, held_ref, flags_ref, taps_ref, wide_ref, in_sems, side_sems):
    parts = in_sems.shape[1]
    looks = out_ref.shape[0] // parts
    width = x_ref.shape[3] // parts
    blocks = width // LANES
    pairs = blocks // 2
    reach = TAPS // 2
    sub = iota((8, LANES), 0)
    lane = iota((8, LANES), 1)
    zero = jnp.zeros((8, LANES), jnp.float32)

    def fetch(part, q):
        columns = pl.ds(q * width, width)
        return pltpu.make_async_copy(x_ref.at[0, part, :, columns], held_ref.at[part, :, columns], in_sems.at[part, q])

    get_flags = pltpu.make_async_copy(far_flags_ref, flags_ref, side_sems.at[0])
    get_taps = pltpu.make_async_copy(far_taps_ref, taps_ref, side_sems.at[1])
    get_taps.start()
    get_flags.start()
    for q in range(parts):
        for part in range(2):
            fetch(part, q).start()
    wide_ref[...] = jnp.zeros_like(wide_ref)
    get_taps.wait()
    for band in range(2):
        for part in range(2):
            wide_ref[2 * band + part, :, :TAPS] = taps_ref[band, part : part + 1, :].astype(jnp.float32)
    fill_filter(wide_ref, m_ref)
    get_flags.wait()
    flags = [flags_ref[0, k].astype(jnp.float32) for k in range(SPAN)]
    pattern = jnp.where(
        lane % 4 < 2, jnp.where(lane % 4 == 0, flags[0], flags[1]), jnp.where(lane % 4 == 2, flags[2], flags[3])
    )
    made = {}

    def half_of(part, block, half):
        if block < 0 or block >= parts * blocks:
            return zero
        start = block * LANES
        return held_ref[part, :, start : start + LANES].astype(jnp.float32)[8 * half : 8 * half + 8]

    def pair_of(part, index, half):
        if (part, index, half) not in made:
            first = half_of(part, 2 * index - 1, half)
            second = half_of(part, 2 * index, half)
            mixed = pltpu.roll(jnp.where(sub < 4, second, first), 4, 0)
            made[part, index, half] = (jnp.where(sub < 4, first, mixed), jnp.where(sub < 4, mixed, second))
        return made[part, index, half]

    def beyond(q, half, odd):
        after, before = [], []
        for part in range(2):
            value = half_of(part, blocks * (q + 1) + 1, half)
            after.append(pltpu.roll(value, 4, 0) if odd else value)
            value = half_of(part, blocks * q - 2, half)
            before.append(value if odd else pltpu.roll(value, 4, 0))
        side = lane // SPAN % 2
        inside = jnp.where(side == 0, float(q < parts - 1), float(q > 0))
        top = jnp.where(lane < reach, after[0], jnp.where(lane < 2 * reach, pltpu.roll(after[1], reach, 1), pattern))
        bottom = jnp.where(lane >= LANES - reach, before[0], pattern * inside)
        bottom = jnp.where(lane < reach, pltpu.roll(before[1], reach, 1), bottom)
        return jnp.where(sub < 4, top, bottom)

    for q in range(parts):
        for part in range(2):
            if q == 0:
                fetch(part, 0).wait()
            if q + 1 < parts:
                fetch(part, q + 1).wait()
        for half in range(looks // 2):
            for odd in range(2):
                chunk = q * looks + 2 * half + odd
                rows = [pair_of(part, q * pairs + i, half)[odd] for part in range(2) for i in range(pairs + 1)]
                for i in range(0, len(rows), 2):
                    both = jnp.concatenate(rows[i : i + 2], axis=0)
                    out_ref[chunk, 8 * i : 8 * i + 16, :] = both.astype(jnp.bfloat16)
                out_ref[chunk, 8 * len(rows) : 8 * len(rows) + 8, :] = beyond(q, half, odd).astype(jnp.bfloat16)


def gather_kernel(z_ref, phase_ref, weight_ref):
    count = z_ref.shape[0]
    looks = phase_ref.shape[1]
    width = 2 * LANES
    source = iota((3 * LANES, 2 * width), 0) % LANES
    column = iota((3 * LANES, 2 * width), 1)
    block = column % width // CELLS
    chosen = jnp.where(source == SPAN * block + column // width, 1.0, 0.0).astype(jnp.bfloat16)
    rest = z_ref[...].reshape(count * CELLS, LANES)
    pieces = []
    for _ in range(3):
        pieces.append(rest.astype(jnp.bfloat16))
        rest = rest - pieces[-1].astype(jnp.float32)
    moved = jnp.dot(jnp.concatenate(pieces, axis=1), chosen, preferred_element_type=jnp.float32)
    moved = moved.reshape(count, CELLS, 2 * width)
    lines = jnp.where(iota(moved.shape, 1) == iota(moved.shape, 2) % CELLS, moved, 0.0).sum(axis=1)
    for q in range(count // looks):
        for which, out in enumerate((phase_ref, weight_ref)):
            out[0, :, width * q : width * (q + 1)] = lines[
                looks * q : looks * (q + 1), width * which : width * (which + 1)
            ]


def local(slc_stack, band_taps, pair_flags):
    n = lax.axis_size("date")
    looks = slc_stack.shape[2] // ML_AZ
    parts = n // looks
    lanes = slc_stack.shape[3] // (parts * LANES) * ML_AZ
    rows = 2 * (lanes + 2 * ML_AZ) + 8
    halos = n * 8 // LANES
    tile = (8, LANES)
    in_vmem = pl.BlockSpec(memory_space=pltpu.VMEM)
    anywhere = pl.BlockSpec(memory_space=pl.ANY)
    params = pltpu.CompilerParams(vmem_limit_bytes=60 * 1024 * 1024)
    chunks, matrix = pl.pallas_call(
        spread_kernel,
        out_shape=[
            pltpu.VMEM((n, rows, LANES), jnp.bfloat16),
            pltpu.VMEM((4 * LANES, 4 * LANES), jnp.bfloat16),
        ],
        in_specs=[anywhere] * 3,
        out_specs=[in_vmem] * 2,
        scratch_shapes=[
            pltpu.VMEM(slc_stack.shape[1:], jnp.bfloat16),
            pltpu.SMEM(pair_flags.shape, jnp.int32),
            pltpu.VMEM(band_taps.shape, jnp.bfloat16),
            pltpu.VMEM((4, 1, 2 * LANES), jnp.float32),
            pltpu.SemaphoreType.DMA((2, parts)),
            pltpu.SemaphoreType.DMA((2,)),
        ],
        compiler_params=params,
    )(slc_stack, pair_flags, band_taps)
    y = pltpu.with_memory_space_constraint(lax.all_to_all(chunks, "date", 0, 0, tiled=True), pltpu.VMEM)
    matrix = pltpu.with_memory_space_constraint(matrix, pltpu.VMEM)
    solved = pl.pallas_call(
        solve_kernel,
        out_shape=pltpu.VMEM((n, *tile), jnp.float32),
        in_specs=[in_vmem, in_vmem],
        out_specs=in_vmem,
        scratch_shapes=[
            pltpu.VMEM((n, 4 * LANES, LANES), jnp.float32),
            pltpu.VMEM((n if n <= 32 else 1, 4 * LANES, LANES), jnp.float32),
            pltpu.VMEM((n, 8, 4 * LANES), jnp.float32),
            pltpu.VMEM((halos, 4 * LANES, LANES), jnp.float32),
            pltpu.VMEM((n, 2, *tile), jnp.float32),
            pltpu.VMEM((n, *tile), jnp.float32),
            pltpu.VMEM((halos, *tile), jnp.float32),
            pltpu.VMEM((6, n, *tile), jnp.float32),
            pltpu.VMEM((halos, 2, 2, *tile), jnp.float32),
            pltpu.VMEM((2, n, *tile), jnp.float32),
            pltpu.VMEM((2, SPAN, n + SPAN, *tile), jnp.float32),
            pltpu.VMEM((2, n, *tile), jnp.float32),
            pltpu.VMEM((2, n + 2 * SPAN, *tile), jnp.float32),
        ],
        compiler_params=params,
    )(matrix, y)
    z = lax.all_to_all(solved, "date", 0, 0, tiled=True)
    shape = (1, looks, slc_stack.shape[3] // ML_RG)
    if lanes == LANES:
        return tuple(
            pl.pallas_call(
                gather_kernel,
                out_shape=[jax.ShapeDtypeStruct(shape, jnp.float32)] * 2,
                in_specs=[in_vmem],
                out_specs=[in_vmem] * 2,
                compiler_params=params,
            )(pltpu.with_memory_space_constraint(z, pltpu.VMEM))
        )
    z = z[:, :, :lanes].reshape(parts, looks, CELLS, lanes // SPAN, SPAN)[..., :2]
    z = z.transpose(4, 1, 0, 3, 2).reshape(2, *shape)
    return (z[0], z[1])


def solution(mesh):
    in_specs = (P("date", None, "group", None), P(), P("date", None))
    out_specs = (P("date", "group", None), P("date", "group", None))
    return jax.shard_map(local, mesh=mesh, in_specs=in_specs, out_specs=out_specs, check_vma=False)
```
